256 devices in a mesh: dp: 256 (over y, z, x, core).
Axes of the slice: x: 4, y: 4, z: 8, core: 2. Of those that a mesh axis runs over, the one named last changes fastest.
Arguments:
- tokens: bfloat16 [98304, 2560], P('dp'), may hold values from -24 to 24
- segment_ids: int32 [256, 384], P('dp'), may hold values from 0 to 3, never falling along the last dimension, each value on 1 to 192 neighbouring positions
- grad_out: bfloat16 [98304, 2560], P('dp'), may hold values from -24 to 24
- norm_gain: bfloat16 [2560], P('dp'), may hold values from 0.099609375 to 1.8984375
- w_qkv: bfloat16 [2560, 768], P('dp'), may hold values from -0.125 to 0.125
- w_out: bfloat16 [512, 2560], P(None, 'dp'), may hold values from -0.25 to 0.25
Outputs:
- output: bfloat16 [98304, 2560], P('dp')
- grad_tokens: bfloat16 [98304, 2560], P('dp')
- grad_qkv: float32 [2560, 768], P('dp')
- grad_wout: float32 [512, 2560], P(None, 'dp')
- grad_gain: float32 [2560], P('dp')
The draws below stay inside these ranges and needn't reach their ends.
Inputs may be any that keep to these rules, and one draw needn't show every extreme that they name: `segment_ids`: ids do not fall along a row; every id occurs in each row, no document spans more than 192 positions, and one spans exactly 192.
All inputs are finite; a program needn't handle non-finite values.
Results may differ from the reference program's by a relative error of at most 0.024.
Values may be sent and summed in bfloat16 or wider, within the bound.
A program may use at most 128 MiB of HBM per device.

```python
import math
from functools import partial
import jax
import jax.numpy as jnp
import numpy as np
from jax import lax

D = 2560
Q_HEADS = 4
HEAD_DIM = 128
QKV_WIDTH = 768
TOK_DEV = 384
DOCS = 4
DOC_MOST = 192
TOKENS = 98304
N_DP = 256


def raised(result, rng, source, target, shards_of, factor):
    def block_of(dim):
        return (jnp.arange(result.shape[dim]) // (result.shape[dim] // shards_of)).reshape((-1,) + (1,) * (result.ndim - 1 - dim))

    near = jax.random.permutation(rng, shards_of)[block_of(target)]
    other_side = (block_of(target) + shards_of // 2) % shards_of
    return jnp.where((block_of(source) == near) | (block_of(source) == other_side), factor * result, result)


def levels(stream_key, extent, shards, low, top_value):
    factor_of = 1.0
    for axis_at, shards_of in shards:
        steps = jax.random.uniform(jax.random.fold_in(jax.random.fold_in(stream_key, 6), axis_at), (shards_of,), jnp.float32, low / len(shards), top_value / len(shards))
        factor_of = factor_of * jnp.repeat(jnp.exp(steps), extent[axis_at] // shards_of).reshape((-1,) + (1,) * (len(extent) - 1 - axis_at))
    return factor_of


def split_up(amount, total, limit, slope):
    loads = [(1 << 20) // math.isqrt(rank ** slope) + 1 for rank in range(2, amount + 1)]
    rest, holding = total - limit - (amount - 1), [1] * (amount - 1)
    while rest > 0:
        free = [i for i in range(amount - 1) if holding[i] < limit]
        pool, left = sum([loads[i] for i in free]), rest
        for i in free:
            extra = min(limit - holding[i], max(1, left * loads[i] // pool), rest)
            holding[i] = holding[i] + extra
            rest = rest - extra
    return np.array([limit] + holding)


def ragged(key, number_of, total, most, skew):
    if number_of == 2:
        one = jax.random.randint(key, (), max(1, total - most), min(most, total - 1) + 1)
        return jnp.stack([one, total - one])
    lengths = jnp.asarray(split_up(number_of, total, most, skew), jnp.int32)
    pairs = (number_of - 1) // 2
    giver, taker = lengths[1:1 + 2 * pairs:2], lengths[2:2 + 2 * pairs:2]
    margin = jnp.minimum(giver - 1, most - taker)
    shifted = jax.random.randint(jax.random.fold_in(key, 1), (pairs,), 0, 1 << 20) % (margin + 1)
    lengths = lengths.at[1:1 + 2 * pairs:2].set(giver - shifted).at[2:2 + 2 * pairs:2].set(taker + shifted)
    return lengths[jax.random.permutation(jax.random.fold_in(key, 2), number_of)]


def noise(rng, shape, scale, limit, cuts=(), kind=jnp.bfloat16):
    gain = levels(rng, shape, cuts, -0.22, 0.18) if cuts else 1.0
    drawn = jax.random.normal(rng, shape, jnp.float32) * scale * gain
    return jnp.minimum(jnp.maximum(drawn, -limit), limit).astype(kind)


def noise_with(key, dims, scale, limit, pieces, heavy, kind=jnp.bfloat16):
    result = scale * jax.random.normal(key, dims, jnp.float32)
    if pieces:
        result = result * levels(key, dims, pieces, -0.22, 0.18)
    return jnp.clip(raised(result, jax.random.fold_in(key, 3), *heavy), -limit, limit).astype(kind)


def setup_inputs(seed: int = 0) -> dict:
    keys = jax.random.split(jax.random.key(seed), 7)
    return {
        "tokens": noise_with(keys[0], (TOKENS, D), 1.0, 24.0, ((0, 256),), (0, 1, 256, 6.0)),
        "segment_ids": jax.vmap(lambda own: jnp.searchsorted(jnp.cumsum(ragged(own, DOCS, TOK_DEV, DOC_MOST, 0)), jnp.arange(TOK_DEV), side="right"))(jax.random.split(keys[1], N_DP)).reshape((N_DP, TOK_DEV)).astype(jnp.int32),
        "grad_out": noise_with(keys[2], (TOKENS, D), 1.0, 24.0, ((0, 256),), (0, 1, 256, 6.0)),
        "norm_gain": jnp.clip(1.0 + 0.18 * jax.random.normal(keys[3], (D,), jnp.float32), 0.099609375, 1.8984375).astype(jnp.bfloat16),
        "w_qkv": noise(keys[4], (D, QKV_WIDTH), D ** -0.5, 0.125, ((0, 256),)),
        "w_out": noise(keys[5], (Q_HEADS * HEAD_DIM, D), (Q_HEADS * HEAD_DIM) ** -0.5, 0.25, ((1, 256),)),
    }


norm_eps = 1e-06
rope_base = 1000000.0

def rms_scale(values):
    return values * lax.rsqrt(lax.optimization_barrier(jnp.mean(values * values, axis=-1, keepdims=True)) + norm_eps)

def rotate(vectors, cosine, sine):
    half = vectors.shape[-1] // 2
    first = vectors[..., :half]
    second = vectors[..., half:]
    return jnp.concatenate([first * cosine - second * sine, second * cosine + first * sine], axis=-1)

def document_layout(segment):
    length = segment.shape[0]
    places = jnp.arange(length, dtype=jnp.int32)
    matching = segment[:, None] == segment[None, :]
    first_place = lax.optimization_barrier(jnp.min(jnp.where(matching, places[None, :], length), axis=1))
    positions = (places - first_place).astype(jnp.float32)
    allowed = matching & (places[None, :] <= places[:, None])
    return (positions, allowed)

def attention_core(projected, segment):
    length = projected.shape[0]
    width = Q_HEADS * HEAD_DIM
    queries = projected[:, :width].reshape(length, Q_HEADS, HEAD_DIM)
    key_head = projected[:, width:width + HEAD_DIM]
    value_head = projected[:, width + HEAD_DIM:]
    positions, allowed = document_layout(segment)
    half = HEAD_DIM // 2
    inverse = rope_base ** (-2.0 * jnp.arange(half, dtype=jnp.float32) / HEAD_DIM)
    angles = positions[:, None] * inverse[None, :]
    cosine = jnp.cos(angles)
    sine = jnp.sin(angles)
    queries = rotate(rms_scale(queries), cosine[:, None, :], sine[:, None, :]).astype(jnp.bfloat16)
    key_head = rotate(rms_scale(key_head), cosine, sine).astype(jnp.bfloat16)
    value_head = value_head.astype(jnp.bfloat16)
    scores = jnp.einsum('thd,sd->hts', queries.astype(jnp.float32), key_head.astype(jnp.float32)) * HEAD_DIM ** (-0.5)
    weights = jnp.where(allowed[None], jnp.exp(scores), 0.0)
    probs = (weights / lax.optimization_barrier(jnp.sum(weights, axis=-1, keepdims=True))).astype(jnp.bfloat16)
    mixed = jnp.einsum('hts,sd->thd', probs.astype(jnp.float32), value_head.astype(jnp.float32))
    return mixed.reshape(length, width).astype(jnp.bfloat16)

def section_attention(tokens, norm_gain, w_qkv, segment):
    scaled = rms_scale(tokens.astype(jnp.float32))
    normed = (scaled * norm_gain.astype(jnp.float32)).astype(jnp.bfloat16)
    projected = jnp.dot(normed, w_qkv, preferred_element_type=jnp.float32)
    return attention_core(projected, segment)

def section_output(tokens, mixed, w_out):
    update = jnp.dot(mixed, w_out, preferred_element_type=jnp.float32)
    return (tokens.astype(jnp.float32) + update).astype(jnp.bfloat16)

def widen(values):
    return lax.optimization_barrier(values).astype(jnp.float32)

def one_device(tokens, segment, grad_out, norm_gain, w_qkv, w_out):
    mixed, pull_attention = jax.vjp(partial(section_attention, segment=segment), tokens, norm_gain, w_qkv)
    output, pull_output = jax.vjp(section_output, tokens, mixed, w_out)
    grad_residual, grad_mixed, grad_weight_out = pull_output(grad_out)
    grad_normpath, grad_gain, grad_weight_qkv = pull_attention(grad_mixed)
    return (output, grad_residual + grad_normpath, widen(grad_weight_qkv), widen(grad_weight_out), widen(grad_gain))

def reference(tokens, segment_ids, grad_out, norm_gain, w_qkv, w_out):
    token_blocks = tokens.reshape(N_DP, TOK_DEV, D)
    grad_blocks = grad_out.reshape(N_DP, TOK_DEV, D)

    def advance(carry, items):
        token_block, segment_block, grad_block = items
        output, grad_block_tokens, sum_qkv, sum_out, sum_gain = one_device(token_block, segment_block, grad_block, norm_gain, w_qkv, w_out)
        return ((carry[0] + sum_qkv, carry[1] + sum_out, carry[2] + sum_gain), (output, grad_block_tokens))
    initial = (jnp.zeros((D, QKV_WIDTH), jnp.float32), jnp.zeros((Q_HEADS * HEAD_DIM, D), jnp.float32), jnp.zeros((D,), jnp.float32))
    totals, (outputs, grad_rows) = lax.scan(advance, initial, (token_blocks, segment_ids, grad_blocks))
    return (outputs.reshape(TOKENS, D), grad_rows.reshape(TOKENS, D), totals[0], totals[1], totals[2])
```

```python
import math

import jax
import jax.numpy as jnp
from jax import lax
from jax.experimental import pallas as pl
from jax.experimental.pallas import tpu as pltpu
from jax.sharding import PartitionSpec as P

NY, NZ, NX, NC = 4, 8, 4, 2
D, T, HD = 2560, 384, 128
ROWS = 10
GROUP = NX * NC
BLK = GROUP * ROWS
CH = NZ * BLK
WA_, WB_ = 384, 256
WX = WA_ + WB_
PAD = 16
EPS = 1e-06
LOG_BASE = math.log(1000000.0)
N_COPIES = 256
BF, F32 = jnp.bfloat16, jnp.float32
NT = (((1,), (1,)), ((), ()))
TN = (((0,), (0,)), ((), ()))


def mm(a, b, dims=(((1,), (0,)), ((), ()))):
    return lax.dot_general(a, b, dims, preferred_element_type=F32)


def rms(x):
    return lax.rsqrt(jnp.mean(x * x, axis=-1, keepdims=True) + EPS)


def kernel(
    tok_hbm, go_hbm, seg_ref, gain_ref, wq_ref, wo_ref,
    out_hbm, gt_hbm, s_ref,
    tok, go, sc, scT, goT, rr, blk, xg, tmp, wa, wb, proj, gm, mask, cs, sn,
    qb, kv, pb, mx, dpr, outv, gs,
    ta, sa, ra, ya1, ya2, za, tb, sb, rb, zb, zb4, yb, fin, xs, xr,
    lsem, ssem, rsem,
):
    idx = lax.axis_index("dp")
    me8 = lax.rem(idx, GROUP)
    base = idx - me8
    c = lax.rem(idx, 2)
    o = 1 - c
    x_c = me8
    yz = lax.div(idx, GROUP)
    z = lax.rem(yz, NZ)
    y = lax.div(yz, NZ)

    def ym(k):
        return lax.rem(y + (k + NY), NY)

    def zm(k):
        return lax.rem(z + (k + NZ), NZ)

    def dev(yy, zz):
        return (yy * NZ + zz) * GROUP + x_c

    right_y, left_y = dev(ym(1), z), dev(ym(-1), z)
    right_z, left_z = dev(y, zm(1)), dev(y, zm(-1))
    partner = idx + 1 - 2 * c

    def rows(zz):
        return pl.ds(pl.multiple_of(zz * BLK, 16), BLK)

    copies = []

    def send(src, dst, target):
        n = len(copies)
        copy = pltpu.make_async_remote_copy(
            src_ref=src, dst_ref=dst, send_sem=ssem.at[n], recv_sem=rsem.at[n],
            device_id=(target,), device_id_type=pl.DeviceIdType.MESH,
        )
        copy.start()
        copies.append(copy)
        return copy

    loads = []
    for i, (src, dst) in enumerate(((tok_hbm, tok), (go_hbm, go))):
        for j in range(NY):
            cp = pltpu.make_async_copy(
                src.at[:, pl.ds(j * CH, CH)], dst.at[j], lsem.at[i * NY + j])
            cp.start()
            loads.append(cp)

    barrier = pltpu.get_barrier_semaphore()
    group = [base + lax.rem(me8 + p, GROUP) for p in range(1, GROUP)]
    everyone = group + [right_y, left_y, right_z, left_z]
    for d in everyone:
        pl.semaphore_signal(barrier, inc=1, device_id=(d,), device_id_type=pl.DeviceIdType.MESH)

    diag = lax.broadcasted_iota(jnp.int32, (PAD, ROWS), 0) == lax.broadcasted_iota(
        jnp.int32, (PAD, ROWS), 1)
    gain_diag = jnp.where(diag, jnp.broadcast_to(gain_ref[...].astype(F32), (PAD, ROWS)), 0.0)
    gw = mm(gain_diag.astype(BF), wq_ref[...]).astype(BF)
    wt = mm(diag.astype(F32).astype(BF), wo_ref[...], NT).astype(BF)
    for h in range(NC):
        blk[h, :, :WA_] = gw[:, h * WA_:(h + 1) * WA_]
        blk[h, :, WA_:] = wt[:, h * WB_:(h + 1) * WB_]

    pl.semaphore_wait(barrier, len(everyone))

    xcop = []
    for p in range(1, GROUP):
        t = lax.rem(me8 + p, GROUP)
        xcop.append(send(blk.at[lax.rem(t, 2)], xg.at[me8], base + t))
    xg[me8] = blk[c]

    for j in range(NY):
        loads[j].wait()

    def scale_rows(i, _):
        r0 = pl.ds(pl.multiple_of(i * 16, 16), 16)
        parts = [tok[j, r0, :].astype(F32) for j in range(NY)]
        total = sum(jnp.sum(p * p, axis=-1, keepdims=True) for p in parts)
        r = lax.rsqrt(total * (1.0 / D) + EPS)
        rr[r0, :] = jnp.broadcast_to(r, (16, 128))
        for j in range(NY):
            sc[j, r0, :] = (parts[j] * r).astype(BF)
        return 0

    lax.fori_loop(0, T // 16, scale_rows, 0)

    for cp in xcop:
        cp.wait_recv()
    for i in range(GROUP):
        tmp[i * ROWS:(i + 1) * ROWS, :] = xg[i].astype(F32)[:ROWS, :]
    wa[c, y, rows(z), :] = tmp[:, :WA_].astype(BF)
    wb[c, y, rows(z), :] = tmp[:, WA_:].astype(BF)

    def ablk(yy, zz):
        return wa.at[c, yy, rows(zz), :]

    def bblk(yy, zz):
        return wb.at[c, yy, rows(zz), :]

    def bhalf(h, zz):
        return wb.at[c, pl.ds(2 * h, 2), rows(zz), :]

    offs = [0, -1, 1, -2, 2, -3, 3, -4]
    za_r, za_l, ya_r, ya_l, ya_f, zb_r, zb_l = {}, {}, {}, {}, {}, {}, {}

    def zA(s):
        za_r[s] = send(ablk(y, zm(1 - s)), ablk(y, zm(1 - s)), right_z)
        if s < 4:
            za_l[s] = send(ablk(y, zm(s - 1)), ablk(y, zm(s - 1)), left_z)

    def zA_wait(s):
        za_r[s].wait_recv()
        if s < 4:
            za_l[s].wait_recv()

    def yA(j):
        b = ablk(y, zm(offs[j]))
        ya_r[j] = send(b, b, right_y)
        ya_l[j] = send(b, b, left_y)

    def yA_forward(j):
        ya_r[j].wait_recv()
        ya_l[j].wait_recv()
        if j % 2 == 0:
            b = ablk(ym(-1), zm(offs[j]))
            ya_f[j] = send(b, b, right_y)
        else:
            b = ablk(ym(1), zm(offs[j]))
            ya_f[j] = send(b, b, left_y)

    def zB(s):
        for h in range(2):
            if s < 4 or h == 0:
                b = bhalf(h, zm(1 - s))
                zb_r[s, h] = send(b, b, right_z)
            if s < 4 or h == 1:
                b = bhalf(h, zm(s - 1))
                zb_l[s, h] = send(b, b, left_z)

    def zB_wait(s):
        for h in range(2):
            if s < 4 or h == 0:
                zb_r[s, h].wait_recv()
            if s < 4 or h == 1:
                zb_l[s, h].wait_recv()

    def transpose(src, dst, j):
        for k in range(CH // 128):
            piece = src[j, :, k * 128:(k + 1) * 128].astype(F32)
            dst[j, k * 128:(k + 1) * 128, :] = piece.T.astype(BF)

    zA(1)
    b = bblk(y, z)
    yb1_r = send(b, b, right_y)
    yb1_l = send(b, b, left_y)
    yA(0)

    seg = seg_ref[...].astype(F32)
    row_i = lax.broadcasted_iota(jnp.int32, (T, T), 0)
    col_i = lax.broadcasted_iota(jnp.int32, (T, T), 1)
    seg_s = jnp.broadcast_to(seg, (T, T))
    seg_t = jnp.sum(jnp.where(row_i == col_i, seg_s, 0.0), axis=1, keepdims=True)
    first = jnp.sum(jnp.where(seg_s < seg_t, 1.0, 0.0), axis=1, keepdims=True)
    mask[...] = jnp.where((seg_s == seg_t) & (col_i <= row_i), 1.0, 0.0)
    lane = lax.broadcasted_iota(jnp.int32, (T, HD), 1)
    place = lax.broadcasted_iota(jnp.int32, (T, HD), 0).astype(F32)
    inverse = jnp.exp(lax.rem(lane, HD // 2).astype(F32) * (-2.0 * LOG_BASE / HD))
    angles = (place - first) * inverse
    cs[...] = jnp.cos(angles)
    sn[...] = jnp.where(lane < HD // 2, -1.0, 1.0) * jnp.sin(angles)

    yb1_r.wait_recv()
    yb1_l.wait_recv()
    b = bblk(ym(-1), z)
    yb2 = send(b, b, right_y)
    zA_wait(1)
    zA(2)
    yA(1)
    yA(2)
    transpose(sc, scT, 0)
    yb2.wait_recv()
    zB(1)
    zA_wait(2)
    zA(3)
    yA(3)
    yA(4)
    yA_forward(0)
    transpose(sc, scT, 1)
    zA_wait(3)
    zA(4)
    yA(5)
    yA(6)
    yA_forward(1)
    yA_forward(2)
    transpose(sc, scT, 2)
    zB_wait(1)
    zB(2)
    zA_wait(4)
    yA(7)
    pa_own = send(wa.at[c, y], wa.at[c, y], partner)
    yA_forward(3)
    yA_forward(4)
    transpose(sc, scT, 3)
    zB_wait(2)
    zB(3)
    yA_forward(5)
    yA_forward(6)
    for j in range(NY):
        loads[NY + j].wait()
    transpose(go, goT, 0)
    transpose(go, goT, 1)
    yA_forward(7)
    pa_l = send(wa.at[c, ym(-1)], wa.at[c, ym(-1)], partner)
    pa_r = send(wa.at[c, ym(1)], wa.at[c, ym(1)], partner)
    zB_wait(3)
    zB(4)
    transpose(go, goT, 2)
    transpose(go, goT, 3)

    def project(yy, first_one=False):
        left = sc[yy]
        for h in range(NC):
            part = mm(left, wa[h, yy])
            proj[h] = part if first_one else proj[h] + part

    pa_own.wait_recv()
    project(y, True)
    pa_f = []
    for j in range(4):
        ya_f[j].wait_recv()
        b = ablk(ym(2), zm(offs[j]))
        pa_f.append(send(b, b, partner))
    pa_l.wait_recv()
    project(ym(-1))
    for j in range(4, 8):
        ya_f[j].wait_recv()
        b = ablk(ym(2), zm(offs[j]))
        pa_f.append(send(b, b, partner))
    pa_r.wait_recv()
    project(ym(1))
    zB_wait(4)
    pb_s = [send(wb.at[c, j], wb.at[c, j], partner) for j in range(NY)]
    for cp in pa_f:
        cp.wait_recv()
    project(ym(2))

    def head_cols(h):
        return h // 3, (h % 3) * HD

    def turn(v):
        return v * cs[...] + pltpu.roll(v, HD // 2, 1) * sn[...]

    def unturn(v):
        return v * cs[...] + pltpu.roll(v * sn[...], HD // 2, 1)

    for h in range(5):
        hf, col = head_cols(h)
        v = proj[hf, :, col:col + HD]
        qb[h] = turn(v * rms(v)).astype(BF)
    kv[...] = proj[1, :, 2 * HD:].astype(BF)
    scale = HD ** -0.5
    for h in range(4):
        for i in range(3):
            r0, n = slice(i * 128, (i + 1) * 128), (i + 1) * 128
            s = mm(qb[h, r0, :], qb[4, :n, :], NT) * scale
            w = jnp.exp(s) * mask[r0, :n]
            p = (w / jnp.sum(w, axis=-1, keepdims=True)).astype(BF)
            pb[h, r0, :n] = p
            mx[h // 2, r0, (h % 2) * HD:(h % 2 + 1) * HD] = mm(p, kv[:n, :]).astype(BF)

    rb_s = []
    for j in range(NY):
        sb[j] = mm(goT[j], mx[o]).astype(BF)
        rb_s.append(send(sb.at[j], rb.at[j], partner))
    for j in range(NY):
        tb[j] = mm(goT[j], mx[c]).astype(BF)
    for cp in pb_s:
        cp.wait_recv()
    for h in range(NC):
        gm[h] = sum(mm(go[j], wb[h, j]) for j in range(NY)).astype(BF)
    for j in range(NY):
        rb_s[j].wait_recv()
        tb[j] = (tb[j].astype(F32) + rb[j].astype(F32)).astype(BF)

    def tbz(zz, h0=0, n=NY):
        return tb.at[pl.ds(h0, n), rows(zz), :]

    def add_into(ref, *others):
        total = ref[...].astype(F32)
        for other in others:
            total = total + other[...].astype(F32)
        ref[...] = total.astype(BF)

    b4r = send(tbz(zm(4), 0, 2), zb4.at[0], right_z)
    b4l = send(tbz(zm(-4), 2, 2), zb4.at[1], left_z)
    bz = {}

    def zB_rs(s):
        if s == 3:
            b4r.wait_recv()
            add_into(tbz(zm(3), 0, 2), zb4.at[0])
            b4l.wait_recv()
            add_into(tbz(zm(-3), 2, 2), zb4.at[1])
        else:
            for side, k in ((0, s), (1, -s)):
                bz[side, s + 1].wait_recv()
                add_into(tbz(zm(k)), zb.at[side, s])
        bz[0, s] = send(tbz(zm(s)), zb.at[0, s - 1], right_z)
        bz[1, s] = send(tbz(zm(-s)), zb.at[1, s - 1], left_z)

    def head_back(h, dk, dv):
        dq = []
        for i in range(3):
            r0, n = slice(i * 128, (i + 1) * 128), (i + 1) * 128
            do = gm[h // 2, r0, (h % 2) * HD:(h % 2 + 1) * HD]
            dp = mm(do, kv[:n, :], NT)
            p = pb[h, r0, :n]
            pf = p.astype(F32)
            delta = jnp.sum(pf * dp, axis=-1, keepdims=True)
            ds = (pf * (dp - delta) * scale).astype(BF)
            dq.append(mm(ds, qb[4, :n, :]))
            tk = mm(ds, qb[h, r0, :], TN)
            tv = mm(p, do, TN)
            for m in range(i + 1):
                dk[m] = dk[m] + tk[m * 128:(m + 1) * 128]
                dv[m] = dv[m] + tv[m * 128:(m + 1) * 128]
        return jnp.concatenate(dq, axis=0)

    def project_back(h, d):
        hf, col = head_cols(h)
        v = proj[hf, :, col:col + HD]
        r = rms(v)
        xn = v * r
        dn = unturn(d)
        grad = r * (dn - xn * jnp.mean(dn * xn, axis=-1, keepdims=True))
        dpr[hf, :, col:col + HD] = grad.astype(BF)

    dk = [jnp.zeros((128, HD), F32)] * 3
    dv = [jnp.zeros((128, HD), F32)] * 3
    for h in range(4):
        project_back(h, head_back(h, dk, dv))
        if h < 3:
            zB_rs(3 - h)
    project_back(4, jnp.concatenate(dk, axis=0))
    dpr[1, :, 2 * HD:] = jnp.concatenate(dv, axis=0).astype(BF)

    ra_s = {}
    for k in (2, 1, 3, 0):
        yy = ym(k)
        sa[yy] = mm(scT[yy], dpr[o]).astype(BF)
        ra_s[k] = send(sa.at[yy], ra.at[yy], partner)
        ta[yy] = mm(scT[yy], dpr[c]).astype(BF)

    bz[0, 1].wait_recv()
    bz[1, 1].wait_recv()
    add_into(tbz(z), zb.at[0, 0], zb.at[1, 0])
    yb_r2 = send(tb.at[ym(2), rows(z), :], yb.at[0], right_y)
    yb_l = send(tb.at[ym(-1), rows(z), :], yb.at[1], left_y)

    roffs = [4, 3, -3, 2, -2, 1, -1, 0]

    def tblk(yy, j):
        return ta.at[yy, rows(zm(roffs[j])), :]

    s1, s2r, s2l, sz = {}, {}, {}, {}
    ra_s[2].wait_recv()
    for j in range(8):
        add_into(tblk(ym(2), j), ra.at[ym(2), rows(zm(roffs[j])), :])
        s1[j] = send(tblk(ym(2), j), ya1.at[j], right_y if j % 2 == 0 else left_y)
    ra_s[1].wait_recv()
    add_into(ta.at[ym(1)], ra.at[ym(1)])
    ra_s[3].wait_recv()
    add_into(ta.at[ym(3)], ra.at[ym(3)])

    yb_r2.wait_recv()
    add_into(tb.at[ym(1), rows(z), :], yb.at[0])
    yb_r1 = send(tb.at[ym(1), rows(z), :], yb.at[2], right_y)

    def step2(j):
        s1[j].wait_recv()
        add_into(tblk(ym(1) if j % 2 == 0 else ym(3), j), ya1.at[j])
        s2r[j] = send(tblk(ym(1), j), ya2.at[0, j], right_y)
        s2l[j] = send(tblk(ym(3), j), ya2.at[1, j], left_y)

    def step3(j):
        s2r[j].wait_recv()
        s2l[j].wait_recv()
        add_into(tblk(y, j), ya2.at[0, j], ya2.at[1, j])

    def step_z(j):
        if j == 0:
            sz[0] = send(tblk(y, 0), za.at[0], right_z)
        elif j == 7:
            return
        elif j % 2 == 1:
            n = (j + 1) // 2
            sz[n - 1].wait_recv()
            add_into(tblk(y, j), za.at[n - 1])
            sz[n] = send(tblk(y, j), za.at[n], right_z)
        else:
            n = 3 + j // 2
            if n > 4:
                sz[n - 1].wait_recv()
                add_into(tblk(y, j), za.at[n - 1])
            sz[n] = send(tblk(y, j), za.at[n], left_z)

    def out_chunk(j):
        update = sum(mm(mx[h], wb[h, j], NT) for h in range(NC))
        outv[j] = (tok[j].astype(F32) + update).astype(BF)

    def gs_chunk(j):
        gs[j] = sum(mm(dpr[h], wa[h, j], NT) for h in range(NC))

    for j in range(4):
        step2(j)
        out_chunk(j)
    stores = []
    for j in range(NY):
        cp = pltpu.make_async_copy(
            outv.at[j], out_hbm.at[:, pl.ds(j * CH, CH)], lsem.at[2 * NY + j])
        cp.start()
        stores.append(cp)
    ra_s[0].wait_recv()
    add_into(ta.at[y], ra.at[y])
    step2(4)
    step2(5)
    gs_chunk(0)
    step3(0)
    step_z(0)
    step2(6)
    step2(7)
    gs_chunk(1)
    step3(1)
    step3(2)
    step_z(1)
    step_z(2)
    gs_chunk(2)
    step3(3)
    step3(4)
    step_z(3)
    step_z(4)
    gs_chunk(3)
    step3(5)
    step3(6)
    step_z(5)
    step_z(6)

    def token_rows(i, _):
        r0 = pl.ds(pl.multiple_of(i * 16, 16), 16)
        r = rr[r0, :][:, :1]
        xn = [tok[j, r0, :].astype(F32) * r for j in range(NY)]
        g = [gs[j, r0, :] for j in range(NY)]
        dot = sum(jnp.sum(a * b, axis=-1, keepdims=True) for a, b in zip(xn, g)) * (1.0 / D)
        for j in range(NY):
            path = (r * (g[j] - xn[j] * dot)).astype(BF).astype(F32)
            go[j, r0, :] = (go[j, r0, :].astype(F32) + path).astype(BF)
        return 0

    lax.fori_loop(0, T // 16, token_rows, 0)
    for j in range(NY):
        cp = pltpu.make_async_copy(
            go.at[j], gt_hbm.at[:, pl.ds(j * CH, CH)], lsem.at[3 * NY + j])
        cp.start()
        stores.append(cp)

    step3(7)
    sz[3].wait_recv()
    sz[6].wait_recv()
    fin[:BLK, :WA_] = (
        tblk(y, 7)[...].astype(F32) + za[3].astype(F32) + za[6].astype(F32))
    yb_r1.wait_recv()
    yb_l.wait_recv()
    fin[:BLK, WA_:] = (
        tb[y, rows(z), :].astype(F32) + yb[1].astype(F32) + yb[2].astype(F32))
    fin[BLK:, :] = jnp.zeros((PAD, WX), F32)

    for i in range(GROUP):
        xs[i] = fin[i * ROWS:i * ROWS + PAD, :].astype(BF)
    last = []
    for p in range(1, GROUP):
        t = lax.rem(me8 + p, GROUP)
        last.append(send(xs.at[t], xr.at[me8], base + t))
    xr[me8] = xs[me8]
    for cp in last:
        cp.wait_recv()
    for h in range(NC):
        s_ref[h] = sum(xr[2 * i + h].astype(F32) for i in range(NX))

    for cp in copies:
        cp.wait_send()
    for cp in stores:
        cp.wait()


def block_step(tokens, segment_ids, grad_out, norm_gain, w_qkv, w_out):
    any_, vm = pl.BlockSpec(memory_space=pl.ANY), pl.BlockSpec(memory_space=pltpu.VMEM)
    v = pltpu.VMEM
    out, grad_tokens, sums = pl.pallas_call(
        kernel,
        out_shape=(
            jax.ShapeDtypeStruct((T, D), BF),
            jax.ShapeDtypeStruct((T, D), BF),
            jax.ShapeDtypeStruct((NC, PAD, WX), F32),
        ),
        in_specs=[any_, any_, vm, vm, vm, vm],
        out_specs=(any_, any_, vm),
        scratch_shapes=[
            v((NY, T, CH), BF), v((NY, T, CH), BF), v((NY, T, CH), BF),
            v((NY, CH, T), BF), v((NY, CH, T), BF), v((T, 128), F32),
            v((NC, PAD, WX), BF), v((GROUP, PAD, WX), BF), v((BLK, WX), F32),
            v((NC, NY, CH, WA_), BF), v((NC, NY, CH, WB_), BF),
            v((NC, T, WA_), F32), v((NC, T, WB_), BF), v((T, T), F32),
            v((T, HD), F32), v((T, HD), F32),
            v((5, T, HD), BF), v((T, HD), BF), v((4, T, T), BF),
            v((NC, T, WB_), BF), v((NC, T, WA_), BF), v((NY, T, CH), BF), v((NY, T, CH), F32),
            v((NY, CH, WA_), BF), v((NY, CH, WA_), BF), v((NY, CH, WA_), BF),
            v((NZ, BLK, WA_), BF), v((2, NZ, BLK, WA_), BF), v((7, BLK, WA_), BF),
            v((NY, CH, WB_), BF), v((NY, CH, WB_), BF), v((NY, CH, WB_), BF),
            v((2, 3, NY, BLK, WB_), BF), v((2, 2, BLK, WB_), BF), v((3, BLK, WB_), BF),
            v((BLK + PAD, WX), F32), v((GROUP, PAD, WX), BF), v((GROUP, PAD, WX), BF),
            pltpu.SemaphoreType.DMA((4 * NY,)),
            pltpu.SemaphoreType.DMA((N_COPIES,)), pltpu.SemaphoreType.DMA((N_COPIES,)),
        ],
        compiler_params=pltpu.CompilerParams(
            collective_id=0, has_side_effects=True, vmem_limit_bytes=60 * 2 ** 20),
        name="block_step",
    )(tokens, grad_out, segment_ids, norm_gain.reshape(1, ROWS), w_qkv, w_out)
    scaled_sum = jnp.concatenate([sums[0, :ROWS, :WA_], sums[1, :ROWS, :WA_]], axis=1)
    out_sum = jnp.concatenate([sums[0, :ROWS, WA_:], sums[1, :ROWS, WA_:]], axis=1)
    grad_qkv = scaled_sum * norm_gain.astype(F32)[:, None]
    grad_gain = jnp.sum(scaled_sum * w_qkv.astype(F32), axis=1)
    return out, grad_tokens, grad_qkv, out_sum.T, grad_gain


def solution(mesh):
    return jax.shard_map(
        block_step,
        mesh=mesh,
        in_specs=(P("dp", None), P("dp", None), P("dp", None), P("dp"), P("dp", None),
                  P(None, "dp")),
        out_specs=(P("dp", None), P("dp", None), P("dp", None), P(None, "dp"), P("dp")),
        check_vma=False,
    )
```

```python
import math

import jax
import jax.numpy as jnp
from jax import lax
from jax.experimental import pallas as pl
from jax.experimental.pallas import tpu as pltpu
from jax.sharding import PartitionSpec as P

NY, NZ, NX, NC = 4, 8, 4, 2
D, T, HD = 2560, 384, 128
ROWS = 10
GROUP = NX * NC
BLK = GROUP * ROWS
CH = NZ * BLK
WA_, WB_ = 384, 256
WX = WA_ + WB_
PAD = 16
EPS = 1e-06
LOG_BASE = math.log(1000000.0)
N_COPIES = 256
BF, F32 = jnp.bfloat16, jnp.float32
NT = (((1,), (1,)), ((), ()))
TN = (((0,), (0,)), ((), ()))


def mm(a, b, dims=(((1,), (0,)), ((), ()))):
    return lax.dot_general(a, b, dims, preferred_element_type=F32)


def rms(x):
    return lax.rsqrt(jnp.mean(x * x, axis=-1, keepdims=True) + EPS)


def kernel(
    tok_hbm, go_hbm, seg_ref, gain_ref, wq_ref, wo_ref,
    out_ref, gt_ref, s_ref,
    tok, go, sc, scT, goT, rr, blk, xg, tmp, wa, wb, proj, gm, mask, cs, sn,
    qb, kv, pb, mx, dpr, gs,
    ta, sa, ra, ya1, ya2, za, tb, sb, rb, xb, zb, fin, finb, xs, xr, xsb, xrb,
    lsem, ssem, rsem, fsem,
):
    idx = lax.axis_index("dp")
    me8 = lax.rem(idx, GROUP)
    base = idx - me8
    c = lax.rem(idx, 2)
    o = 1 - c
    xi = lax.div(me8, 2)
    yz = lax.div(idx, GROUP)
    z = lax.rem(yz, NZ)
    y = lax.div(yz, NZ)

    def ym(k):
        return lax.rem(y + (k + NY), NY)

    def zm(k):
        return lax.rem(z + (k + NZ), NZ)

    def dev(yy, zz):
        return (yy * NZ + zz) * GROUP + me8

    def xdev(k):
        return base + lax.rem(me8 + 2 * k, GROUP)

    right_y, left_y = dev(ym(1), z), dev(ym(-1), z)
    right_z, left_z = dev(y, zm(1)), dev(y, zm(-1))
    partner = idx + 1 - 2 * c

    def rows(zz):
        return pl.ds(pl.multiple_of(zz * BLK, 16), BLK)

    copies = []

    def send(src, dst, target):
        n = len(copies)
        copy = pltpu.make_async_remote_copy(
            src_ref=src, dst_ref=dst, send_sem=ssem.at[n], recv_sem=rsem.at[n],
            device_id=(target,), device_id_type=pl.DeviceIdType.MESH,
        )
        copy.start()
        copies.append(copy)
        return copy

    barrier = pltpu.get_barrier_semaphore()

    def greet(d):
        pl.semaphore_signal(barrier, inc=1, device_id=(d,), device_id_type=pl.DeviceIdType.MESH)

    greetings = [base + lax.rem(me8 + p, GROUP) for p in range(1, GROUP)]
    greetings += [dev(ym(k), z) for k in range(1, NY)]
    greetings += [dev(y, zm(k)) for k in range(1, NZ)]
    for k in range(NY):
        for core in (c, o):
            if k > 0 or core is o:
                greetings.append((ym(k) * NZ + z) * GROUP + 2 * y + core)
    for d in greetings:
        greet(d)

    @pl.when(y != xi)
    def _():
        greet((y * NZ + z) * GROUP + 2 * y + c)

    loads = []
    for i, (src, dst) in enumerate(((tok_hbm, tok), (go_hbm, go))):
        for j in range(NY):
            cp = pltpu.make_async_copy(
                src.at[:, pl.ds(j * CH, CH)], dst.at[j], lsem.at[i * NY + j])
            cp.start()
            loads.append(cp)

    diag = lax.broadcasted_iota(jnp.int32, (PAD, ROWS), 0) == lax.broadcasted_iota(
        jnp.int32, (PAD, ROWS), 1)
    gain_diag = jnp.where(diag, jnp.broadcast_to(gain_ref[...].astype(F32), (PAD, ROWS)), 0.0)
    gw = mm(gain_diag.astype(BF), wq_ref[...]).astype(BF)
    wt = mm(diag.astype(F32).astype(BF), wo_ref[...]).astype(BF)
    for h in range(NC):
        blk[h, :, :WA_] = gw[:, h * WA_:(h + 1) * WA_]
        blk[h, :, WA_:] = wt[:, h * WB_:(h + 1) * WB_]

    pl.semaphore_wait(barrier, jnp.where(y == xi, len(greetings), len(greetings) + 1))

    xcop = []
    for p in range(1, GROUP):
        t = lax.rem(me8 + p, GROUP)
        xcop.append(send(blk.at[lax.rem(t, 2)], xg.at[me8], base + t))
    xg[me8] = blk[c]

    for j in range(NY):
        loads[j].wait()

    def scale_rows(i, _):
        r0 = pl.ds(pl.multiple_of(i * 16, 16), 16)
        parts = [tok[j, r0, :].astype(F32) for j in range(NY)]
        total = sum(jnp.sum(p * p, axis=-1, keepdims=True) for p in parts)
        r = lax.rsqrt(total * (1.0 / D) + EPS)
        rr[r0, :] = jnp.broadcast_to(r, (16, 128))
        for j in range(NY):
            sc[j, r0, :] = (parts[j] * r).astype(BF)
        return 0

    lax.fori_loop(0, T // 16, scale_rows, 0, unroll=2)

    for cp in xcop:
        cp.wait_recv()
    for i in range(GROUP):
        tmp[i * ROWS:(i + 1) * ROWS, :] = xg[i].astype(F32)[:ROWS, :]
    wa[c, y, rows(z), :] = tmp[:, :WA_].astype(BF)
    wb[c, y, rows(z), :] = tmp[:, WA_:].astype(BF)

    def ablk(yy, zz):
        return wa.at[c, yy, rows(zz), :]

    def bblk(yy, zz):
        return wb.at[c, yy, rows(zz), :]

    offs = [0, -1, 1, -2, 2, -3, 3, -4]
    za_r, za_l, ya_r, ya_l, ya_f, zb_c, xb_c = {}, {}, {}, {}, {}, {}, []

    def zA(s):
        za_r[s] = send(ablk(y, zm(1 - s)), ablk(y, zm(1 - s)), right_z)
        if s < 4:
            za_l[s] = send(ablk(y, zm(s - 1)), ablk(y, zm(s - 1)), left_z)

    def zA_wait(s):
        za_r[s].wait_recv()
        if s < 4:
            za_l[s].wait_recv()

    def yA(j):
        b = ablk(y, zm(offs[j]))
        ya_r[j] = send(b, b, right_y)
        ya_l[j] = send(b, b, left_y)

    def yA_forward(j):
        ya_r[j].wait_recv()
        ya_l[j].wait_recv()
        if j % 2 == 0:
            b = ablk(ym(-1), zm(offs[j]))
            ya_f[j] = send(b, b, right_y)
        else:
            b = ablk(ym(1), zm(offs[j]))
            ya_f[j] = send(b, b, left_y)

    def zB(k):
        b = bblk(xi, z)
        zb_c[k] = send(b, b, dev(y, zm(k)))

    def xB(k):
        zb_c[k].wait_recv()
        b = bblk(xi, zm(-k))
        for m in (1, 3, 2):
            xb_c.append(send(b, b, xdev(m)))

    def transpose(src, dst, j):
        for k in range(CH // 128):
            piece = src[j, :, k * 128:(k + 1) * 128].astype(F32)
            dst[j, k * 128:(k + 1) * 128, :] = piece.T.astype(BF)

    zA(1)
    b = bblk(y, z)
    yb_c = [send(b, b, dev(ym(k), z)) for k in (1, 3, 2)]
    yA(0)

    seg = seg_ref[...].astype(F32)
    row_i = lax.broadcasted_iota(jnp.int32, (T, T), 0)
    col_i = lax.broadcasted_iota(jnp.int32, (T, T), 1)
    seg_s = jnp.broadcast_to(seg, (T, T))
    seg_t = jnp.sum(jnp.where(row_i == col_i, seg_s, 0.0), axis=1, keepdims=True)
    first = jnp.sum(jnp.where(seg_s < seg_t, 1.0, 0.0), axis=1, keepdims=True)
    mask[...] = jnp.where((seg_s == seg_t) & (col_i <= row_i), 1.0, 0.0)
    lane = lax.broadcasted_iota(jnp.int32, (T, HD), 1)
    place = lax.broadcasted_iota(jnp.int32, (T, HD), 0).astype(F32)
    inverse = jnp.exp(lax.rem(lane, HD // 2).astype(F32) * (-2.0 * LOG_BASE / HD))
    angles = (place - first) * inverse
    cs[...] = jnp.cos(angles)
    sn[...] = jnp.where(lane < HD // 2, -1.0, 1.0) * jnp.sin(angles)

    for cp in yb_c:
        cp.wait_recv()
    zA_wait(1)
    zA(2)
    yA(1)
    yA(2)
    for k in (1, 7, 2, 6, 3, 5, 4):
        zB(k)
    transpose(sc, scT, 0)
    yA_forward(0)
    zA_wait(2)
    zA(3)
    yA(3)
    yA(4)
    transpose(sc, scT, 1)
    yA_forward(1)
    yA_forward(2)
    zA_wait(3)
    zA(4)
    yA(5)
    yA(6)
    xB(1)
    xB(7)
    transpose(sc, scT, 2)
    yA_forward(3)
    yA_forward(4)
    zA_wait(4)
    yA(7)
    pa_own = send(wa.at[c, y], wa.at[c, y], partner)
    xB(2)
    xB(6)
    transpose(sc, scT, 3)
    yA_forward(5)
    yA_forward(6)
    for j in range(NY):
        loads[NY + j].wait()
    xB(3)
    xB(5)
    xB(4)
    yA_forward(7)
    pa_l = send(wa.at[c, ym(-1)], wa.at[c, ym(-1)], partner)
    pa_r = send(wa.at[c, ym(1)], wa.at[c, ym(1)], partner)
    for j in range(NY):
        transpose(go, goT, j)

    def project(yy, first_one=False):
        left = sc[yy]
        for h in range(NC):
            part = mm(left, wa[h, yy])
            proj[h] = part if first_one else proj[h] + part

    pa_own.wait_recv()
    project(y, True)
    pa_f = []
    for j in range(4):
        ya_f[j].wait_recv()
        b = ablk(ym(2), zm(offs[j]))
        pa_f.append(send(b, b, partner))
    pa_l.wait_recv()
    project(ym(-1))
    for j in range(4, 8):
        ya_f[j].wait_recv()
        b = ablk(ym(2), zm(offs[j]))
        pa_f.append(send(b, b, partner))
    pa_r.wait_recv()
    project(ym(1))
    for cp in pa_f:
        cp.wait_recv()
    project(ym(2))

    def head_cols(h):
        return h // 3, (h % 3) * HD

    def turn(v):
        return v * cs[...] + pltpu.roll(v, HD // 2, 1) * sn[...]

    def unturn(v):
        return v * cs[...] + pltpu.roll(v * sn[...], HD // 2, 1)

    for h in range(5):
        hf, col = head_cols(h)
        v = proj[hf, :, col:col + HD]
        qb[h] = turn(v * rms(v)).astype(BF)
    kv[...] = proj[1, :, 2 * HD:].astype(BF)
    scale = HD ** -0.5
    for h in range(4):
        for i in range(3):
            r0, n = slice(i * 128, (i + 1) * 128), (i + 1) * 128
            s = mm(qb[h, r0, :], qb[4, :n, :], NT) * scale
            w = jnp.exp(s) * mask[r0, :n]
            p = (w / jnp.sum(w, axis=-1, keepdims=True)).astype(BF)
            pb[h, r0, :n] = p
            mx[h // 2, r0, (h % 2) * HD:(h % 2 + 1) * HD] = mm(p, kv[:n, :]).astype(BF)
        if h == 1:
            for cp in xb_c:
                cp.wait_recv()
            pb_s = [send(wb.at[c, j], wb.at[c, j], partner) for j in range(NY)]

    rb_s = []
    for j in range(NY):
        sb[j] = mm(goT[j], mx[o]).astype(BF)
        rb_s.append(send(sb.at[j], rb.at[j], partner))
    for j in range(NY):
        tb[j] = mm(goT[j], mx[c]).astype(BF)
    for cp in pb_s:
        cp.wait_recv()
    for h in range(NC):
        gm[h] = sum(mm(go[j], wb[h, j]) for j in range(NY)).astype(BF)
    for j in range(NY):
        rb_s[j].wait_recv()
        tb[j] = (tb[j].astype(F32) + rb[j].astype(F32)).astype(BF)

    xb_s = []
    for m in (1, 3, 2):
        t = lax.rem(xi + m, NX)
        xb_s.append(send(tb.at[t], xb.at[m - 1], xdev(m)))

    def add_into(ref, *others):
        total = ref[...].astype(F32)
        for other in others:
            total = total + other[...].astype(F32)
        ref[...] = total.astype(BF)

    def head_back(h, dk, dv):
        dq = []
        for i in range(3):
            r0, n = slice(i * 128, (i + 1) * 128), (i + 1) * 128
            do = gm[h // 2, r0, (h % 2) * HD:(h % 2 + 1) * HD]
            dp = mm(do, kv[:n, :], NT)
            p = pb[h, r0, :n]
            pf = p.astype(F32)
            delta = jnp.sum(pf * dp, axis=-1, keepdims=True)
            ds = (pf * (dp - delta) * scale).astype(BF)
            dq.append(mm(ds, qb[4, :n, :]))
            tk = mm(ds, qb[h, r0, :], TN)
            tv = mm(p, do, TN)
            for m in range(i + 1):
                dk[m] = dk[m] + tk[m * 128:(m + 1) * 128]
                dv[m] = dv[m] + tv[m * 128:(m + 1) * 128]
        return jnp.concatenate(dq, axis=0)

    def project_back(h, d):
        hf, col = head_cols(h)
        v = proj[hf, :, col:col + HD]
        r = rms(v)
        xn = v * r
        dn = unturn(d)
        grad = r * (dn - xn * jnp.mean(dn * xn, axis=-1, keepdims=True))
        dpr[hf, :, col:col + HD] = grad.astype(BF)

    dk = [jnp.zeros((128, HD), F32)] * 3
    dv = [jnp.zeros((128, HD), F32)] * 3
    for h in range(4):
        project_back(h, head_back(h, dk, dv))
    project_back(4, jnp.concatenate(dk, axis=0))
    dpr[1, :, 2 * HD:] = jnp.concatenate(dv, axis=0).astype(BF)

    ra_s = {}
    for k in (2, 1, 3, 0):
        yy = ym(k)
        sa[yy] = mm(scT[yy], dpr[o]).astype(BF)
        ra_s[k] = send(sa.at[yy], ra.at[yy], partner)
        ta[yy] = mm(scT[yy], dpr[c]).astype(BF)

    roffs = [4, 3, -3, 2, -2, 1, -1, 0]

    def tblk(yy, j):
        return ta.at[yy, rows(zm(roffs[j])), :]

    s1, s2r, s2l, sz = {}, {}, {}, {}
    ra_s[2].wait_recv()
    for j in range(8):
        add_into(tblk(ym(2), j), ra.at[ym(2), rows(zm(roffs[j])), :])
        s1[j] = send(tblk(ym(2), j), ya1.at[j], right_y if j % 2 == 0 else left_y)
    ra_s[1].wait_recv()
    add_into(ta.at[ym(1)], ra.at[ym(1)])
    ra_s[3].wait_recv()
    add_into(ta.at[ym(3)], ra.at[ym(3)])

    def step2(j):
        s1[j].wait_recv()
        add_into(tblk(ym(1) if j % 2 == 0 else ym(3), j), ya1.at[j])
        s2r[j] = send(tblk(ym(1), j), ya2.at[0, j], right_y)
        s2l[j] = send(tblk(ym(3), j), ya2.at[1, j], left_y)

    def step3(j):
        s2r[j].wait_recv()
        s2l[j].wait_recv()
        add_into(tblk(y, j), ya2.at[0, j], ya2.at[1, j])

    def step_z(j):
        if j == 0:
            sz[0] = send(tblk(y, 0), za.at[0], right_z)
        elif j == 7:
            return
        elif j % 2 == 1:
            n = (j + 1) // 2
            sz[n - 1].wait_recv()
            add_into(tblk(y, j), za.at[n - 1])
            sz[n] = send(tblk(y, j), za.at[n], right_z)
        else:
            n = 3 + j // 2
            if n > 4:
                sz[n - 1].wait_recv()
                add_into(tblk(y, j), za.at[n - 1])
            sz[n] = send(tblk(y, j), za.at[n], left_z)

    def out_chunk(j):
        update = sum(mm(mx[h], wb[h, j], NT) for h in range(NC))
        out_ref[:, j * CH:(j + 1) * CH] = (tok[j].astype(F32) + update).astype(BF)

    def gs_chunk(j):
        gs[j] = sum(mm(dpr[h], wa[h, j], NT) for h in range(NC))

    zb_s = []

    def sum_x():
        for cp in xb_s:
            cp.wait_recv()
        add_into(tb.at[xi], xb.at[0], xb.at[1], xb.at[2])
        for k in (4, 3, 5, 2, 6, 1, 7):
            zb_s.append(send(tb.at[xi, rows(zm(k)), :], zb.at[k - 1], dev(y, zm(k))))

    def piece_copy(p):
        t = lax.rem(me8 + p, GROUP)
        return pltpu.make_async_remote_copy(
            src_ref=xsb.at[t], dst_ref=xrb.at[2 * y + c],
            send_sem=fsem.at[p], recv_sem=fsem.at[GROUP + 2 * y + c],
            device_id=((xi * NZ + z) * GROUP + t,), device_id_type=pl.DeviceIdType.MESH,
        )

    def self_copy():
        return pltpu.make_async_copy(
            xsb.at[me8], xrb.at[2 * y + c], fsem.at[GROUP + 2 * y + c])

    def sum_z():
        for cp in zb_s:
            cp.wait_recv()
        finb[:BLK, :] = tb[xi, rows(z), :].astype(F32) + sum(
            zb[k].astype(F32) for k in range(NZ - 1))
        finb[BLK:, :] = jnp.zeros((PAD, WB_), F32)
        for i in range(GROUP):
            xsb[i] = finb[i * ROWS:i * ROWS + PAD, :].astype(BF)
        for p in range(1, GROUP):
            piece_copy(p).start()

        @pl.when(y != xi)
        def _():
            piece_copy(0).start()

        @pl.when(y == xi)
        def _():
            self_copy().start()

    step2(0)
    out_chunk(0)
    step2(1)
    out_chunk(1)
    step2(2)
    out_chunk(2)
    sum_x()
    step2(3)
    out_chunk(3)
    ra_s[0].wait_recv()
    add_into(ta.at[y], ra.at[y])
    step2(4)
    step2(5)
    gs_chunk(0)
    step3(0)
    step_z(0)
    step2(6)
    step2(7)
    gs_chunk(1)
    step3(1)
    step3(2)
    step_z(1)
    step_z(2)
    gs_chunk(2)
    step3(3)
    step3(4)
    step_z(3)
    step_z(4)
    gs_chunk(3)
    step3(5)
    step3(6)
    step_z(5)
    step_z(6)

    def token_rows(i, _):
        r0 = pl.ds(pl.multiple_of(i * 16, 16), 16)
        r = rr[r0, :][:, :1]
        xn = [tok[j, r0, :].astype(F32) * r for j in range(NY)]
        g = [gs[j, r0, :] for j in range(NY)]
        dot = sum(jnp.sum(a * b, axis=-1, keepdims=True) for a, b in zip(xn, g)) * (1.0 / D)
        for j in range(NY):
            path = (r * (g[j] - xn[j] * dot)).astype(BF).astype(F32)
            gt_ref[r0, j * CH:(j + 1) * CH] = (go[j, r0, :].astype(F32) + path).astype(BF)
        return 0

    lax.fori_loop(0, T // 16, token_rows, 0, unroll=2)
    sum_z()
    step3(7)
    sz[3].wait_recv()
    sz[6].wait_recv()
    fin[:BLK, :] = (
        tblk(y, 7)[...].astype(F32) + za[3].astype(F32) + za[6].astype(F32))
    fin[BLK:, :] = jnp.zeros((PAD, WA_), F32)

    for i in range(GROUP):
        xs[i] = fin[i * ROWS:i * ROWS + PAD, :].astype(BF)
    last = []
    for p in range(1, GROUP):
        t = lax.rem(me8 + p, GROUP)
        last.append(send(xs.at[t], xr.at[me8], base + t))
    xr[me8] = xs[me8]
    for i in range(GROUP):
        pltpu.make_async_copy(xsb.at[i], xrb.at[i], fsem.at[GROUP + i]).wait()
    for h in range(NC):
        s_ref[h, :, WA_:] = sum(xrb[2 * i + h].astype(F32) for i in range(NY))
    for cp in copies[:-len(last)]:
        cp.wait_send()
    for p in range(1, GROUP):
        piece_copy(p).wait_send()

    @pl.when(y != xi)
    def _():
        piece_copy(0).wait_send()

    for cp in last:
        cp.wait_recv()
    for h in range(NC):
        s_ref[h, :, :WA_] = sum(xr[2 * i + h].astype(F32) for i in range(NX))
    for cp in last:
        cp.wait_send()


def finish_kernel(out_in, gt_in, s_ref, gain_ref, wq_ref, out_hbm, gt_hbm, gq_ref, gw_ref, gg_ref, sem):
    moves = []
    for i, (src, dst) in enumerate(((out_in, out_hbm), (gt_in, gt_hbm))):
        for j in range(4):
            part = pl.ds(j * (T // 4), T // 4)
            cp = pltpu.make_async_copy(src.at[part, :], dst.at[part, :], sem.at[4 * i + j])
            cp.start()
            moves.append(cp)
    eye = lax.broadcasted_iota(jnp.int32, (ROWS, ROWS), 0) == lax.broadcasted_iota(
        jnp.int32, (ROWS, ROWS), 1)
    gain = jnp.sum(
        jnp.where(eye, jnp.broadcast_to(gain_ref[...].astype(F32), (ROWS, ROWS)), 0.0),
        axis=1, keepdims=True)
    along = jnp.zeros((ROWS, 1), F32)
    for h in range(NC):
        part = s_ref[h][:ROWS, :WA_]
        cols = slice(h * WA_, (h + 1) * WA_)
        gq_ref[:, cols] = part * gain
        along += jnp.sum(part * wq_ref[:, cols].astype(F32), axis=1, keepdims=True)
        gw_ref[:, h * WB_:(h + 1) * WB_] = s_ref[h][:ROWS, WA_:]
    gg_ref[...] = jnp.sum(
        jnp.where(eye, jnp.broadcast_to(along, (ROWS, ROWS)), 0.0), axis=0, keepdims=True)
    for cp in moves:
        cp.wait()


def block_step(tokens, segment_ids, grad_out, norm_gain, w_qkv, w_out):
    any_, vm = pl.BlockSpec(memory_space=pl.ANY), pl.BlockSpec(memory_space=pltpu.VMEM)
    v = pltpu.VMEM
    gain = norm_gain.reshape(1, ROWS)
    out, grad_tokens, sums = pl.pallas_call(
        kernel,
        out_shape=(
            pltpu.VMEM((T, D), BF),
            pltpu.VMEM((T, D), BF),
            pltpu.VMEM((NC, PAD, WX), F32),
        ),
        in_specs=[any_, any_, vm, vm, vm, vm],
        out_specs=(vm, vm, vm),
        scratch_shapes=[
            v((NY, T, CH), BF), v((NY, T, CH), BF), v((NY, T, CH), BF),
            v((NY, CH, T), BF), v((NY, CH, T), BF), v((T, 128), F32),
            v((NC, PAD, WX), BF), v((GROUP, PAD, WX), BF), v((BLK, WX), F32),
            v((NC, NY, CH, WA_), BF), v((NC, NY, CH, WB_), BF),
            v((NC, T, WA_), F32), v((NC, T, WB_), BF), v((T, T), F32),
            v((T, HD), F32), v((T, HD), F32),
            v((5, T, HD), BF), v((T, HD), BF), v((4, T, T), BF),
            v((NC, T, WB_), BF), v((NC, T, WA_), BF), v((NY, T, CH), F32),
            v((NY, CH, WA_), BF), v((NY, CH, WA_), BF), v((NY, CH, WA_), BF),
            v((NZ, BLK, WA_), BF), v((2, NZ, BLK, WA_), BF), v((7, BLK, WA_), BF),
            v((NY, CH, WB_), BF), v((NY, CH, WB_), BF), v((NY, CH, WB_), BF),
            v((3, CH, WB_), BF), v((NZ - 1, BLK, WB_), BF),
            v((BLK + PAD, WA_), F32), v((BLK + PAD, WB_), F32),
            v((GROUP, PAD, WA_), BF), v((GROUP, PAD, WA_), BF),
            v((GROUP, PAD, WB_), BF), v((GROUP, PAD, WB_), BF),
            pltpu.SemaphoreType.DMA((2 * NY,)),
            pltpu.SemaphoreType.DMA((N_COPIES,)), pltpu.SemaphoreType.DMA((N_COPIES,)),
            pltpu.SemaphoreType.DMA((2 * GROUP,)),
        ],
        compiler_params=pltpu.CompilerParams(
            collective_id=0, has_side_effects=True, vmem_limit_bytes=50 * 2 ** 20),
        name="block_step",
    )(tokens, grad_out, segment_ids, gain, w_qkv, w_out.T)
    out, grad_tokens, grad_qkv, grad_wout, grad_gain = pl.pallas_call(
        finish_kernel,
        out_shape=(
            jax.ShapeDtypeStruct((T, D), BF),
            jax.ShapeDtypeStruct((T, D), BF),
            jax.ShapeDtypeStruct((ROWS, NC * WA_), F32),
            jax.ShapeDtypeStruct((ROWS, NC * WB_), F32),
            jax.ShapeDtypeStruct((1, ROWS), F32),
        ),
        in_specs=[vm, vm, vm, vm, vm],
        out_specs=(any_, any_, vm, vm, vm),
        scratch_shapes=[pltpu.SemaphoreType.DMA((8,))],
        name="finish",
    )(out, grad_tokens, sums, gain, w_qkv)
    return out, grad_tokens, grad_qkv, grad_wout.T, grad_gain.reshape(ROWS)


def solution(mesh):
    return jax.shard_map(
        block_step,
        mesh=mesh,
        in_specs=(P("dp", None), P("dp", None), P("dp", None), P("dp"), P("dp", None),
                  P(None, "dp")),
        out_specs=(P("dp", None), P("dp", None), P("dp", None), P(None, "dp"), P("dp")),
        check_vma=False,
    )
```

```python
import math

import jax
import jax.numpy as jnp
from jax import lax
from jax.experimental import pallas as pl
from jax.experimental.pallas import tpu as pltpu
from jax.sharding import PartitionSpec as P

NY, NZ, NX, NC = 4, 8, 4, 2
D, T, HD = 2560, 384, 128
ROWS = 10
GROUP = NX * NC
BLK = GROUP * ROWS
CH = NZ * BLK
WA_, WB_ = 384, 256
WX = WA_ + WB_
PAD = 16
EPS = 1e-06
LOG_BASE = math.log(1000000.0)
N_COPIES = 256
BF, F32 = jnp.bfloat16, jnp.float32
NT = (((1,), (1,)), ((), ()))
TN = (((0,), (0,)), ((), ()))


def mm(a, b, dims=(((1,), (0,)), ((), ()))):
    return lax.dot_general(a, b, dims, preferred_element_type=F32)


def rms(x):
    return lax.rsqrt(jnp.mean(x * x, axis=-1, keepdims=True) + EPS)


def kernel(
    tok_hbm, go_hbm, seg_hbm, gain_hbm, wq_hbm, wo_hbm,
    out_ref, gt_ref, s_ref,
    seg_ref, gain_ref, wq_ref, wo_ref,
    tok, go, sc, scT, goT, rr, blk, xg, tmp, wa, wb, proj, gm, mask, cs, sn,
    qb, kb, kv, pb, mx, dpr, gs,
    ta, sa, ra, ya1, ya2, za, tb, sb, rb, xb, zb, fin, finb, xs, xr, xsb, xrb,
    lsem, ssem, rsem, fsem,
):
    idx = lax.axis_index("dp")
    me8 = lax.rem(idx, GROUP)
    base = idx - me8
    c = lax.rem(idx, 2)
    o = 1 - c
    xi = lax.div(me8, 2)
    yz = lax.div(idx, GROUP)
    z = lax.rem(yz, NZ)
    y = lax.div(yz, NZ)

    def ym(k):
        return lax.rem(y + (k + NY), NY)

    def zm(k):
        return lax.rem(z + (k + NZ), NZ)

    def dev(yy, zz):
        return (yy * NZ + zz) * GROUP + me8

    def xdev(k):
        return base + lax.rem(me8 + 2 * k, GROUP)

    right_y, left_y = dev(ym(1), z), dev(ym(-1), z)
    right_z, left_z = dev(y, zm(1)), dev(y, zm(-1))
    partner = idx + 1 - 2 * c

    def rows(zz):
        return pl.ds(pl.multiple_of(zz * BLK, 16), BLK)

    copies = []

    def send(src, dst, target):
        n = len(copies)
        copy = pltpu.make_async_remote_copy(
            src_ref=src, dst_ref=dst, send_sem=ssem.at[n], recv_sem=rsem.at[n],
            device_id=(target,), device_id_type=pl.DeviceIdType.MESH,
        )
        copy.start()
        copies.append(copy)
        return copy

    small = []
    for i, (src, dst) in enumerate(
            ((gain_hbm, gain_ref), (wq_hbm, wq_ref), (wo_hbm, wo_ref), (seg_hbm, seg_ref))):
        cp = pltpu.make_async_copy(src, dst, lsem.at[2 * NY + i])
        cp.start()
        small.append(cp)

    barrier = pltpu.get_barrier_semaphore()

    def greet(d):
        pl.semaphore_signal(barrier, inc=1, device_id=(d,), device_id_type=pl.DeviceIdType.MESH)

    greetings = [base + lax.rem(me8 + p, GROUP) for p in range(1, GROUP)]
    greetings += [dev(ym(k), z) for k in range(1, NY)]
    greetings += [dev(y, zm(k)) for k in range(1, NZ)]
    for k in range(NY):
        for core in (c, o):
            if k > 0 or core is o:
                greetings.append((ym(k) * NZ + z) * GROUP + 2 * y + core)
    for d in greetings:
        greet(d)

    @pl.when(y != xi)
    def _():
        greet((y * NZ + z) * GROUP + 2 * y + c)

    loads = []
    for i, (src, dst) in enumerate(((tok_hbm, tok), (go_hbm, go))):
        for j in range(NY):
            cp = pltpu.make_async_copy(
                src.at[:, pl.ds(j * CH, CH)], dst.at[j], lsem.at[i * NY + j])
            cp.start()
            loads.append(cp)

    for cp in small:
        cp.wait()
    diag = lax.broadcasted_iota(jnp.int32, (PAD, ROWS), 0) == lax.broadcasted_iota(
        jnp.int32, (PAD, ROWS), 1)
    gain_diag = jnp.where(diag, jnp.broadcast_to(gain_ref[...].astype(F32), (PAD, ROWS)), 0.0)
    gw = mm(gain_diag.astype(BF), wq_ref[...]).astype(BF)
    wt = mm(diag.astype(F32).astype(BF), wo_ref[...]).astype(BF)
    for h in range(NC):
        blk[h, :, :WA_] = gw[:, h * WA_:(h + 1) * WA_]
        blk[h, :, WA_:] = wt[:, h * WB_:(h + 1) * WB_]

    pl.semaphore_wait(barrier, jnp.where(y == xi, len(greetings), len(greetings) + 1))

    xcop = []
    for p in range(1, GROUP):
        t = lax.rem(me8 + p, GROUP)
        xcop.append(send(blk.at[lax.rem(t, 2)], xg.at[me8], base + t))
    xg[me8] = blk[c]

    for j in range(NY):
        loads[j].wait()

    def scale_rows(i, _):
        r0 = pl.ds(pl.multiple_of(i * 16, 16), 16)
        parts = [tok[j, r0, :].astype(F32) for j in range(NY)]
        total = sum(jnp.sum(p * p, axis=-1, keepdims=True) for p in parts)
        r = lax.rsqrt(total * (1.0 / D) + EPS)
        rr[r0, :] = jnp.broadcast_to(r, (16, 128))
        for j in range(NY):
            sc[j, r0, :] = (parts[j] * r).astype(BF)
        return 0

    lax.fori_loop(0, T // 16, scale_rows, 0, unroll=2)

    for cp in xcop:
        cp.wait_recv()
    for i in range(GROUP):
        tmp[i * ROWS:(i + 1) * ROWS, :] = xg[i].astype(F32)[:ROWS, :]
    wa[c, y, rows(z), :] = tmp[:, :WA_].astype(BF)
    wb[c, y, rows(z), :] = tmp[:, WA_:].astype(BF)

    def ablk(yy, zz):
        return wa.at[c, yy, rows(zz), :]

    def bblk(yy, zz):
        return wb.at[c, yy, rows(zz), :]

    offs = [0, -1, 1, -2, 2, -3, 3, -4]
    za_r, za_l, ya_r, ya_l, ya_f, zb_c, xb_c = {}, {}, {}, {}, {}, {}, []

    def zA(s):
        za_r[s] = send(ablk(y, zm(1 - s)), ablk(y, zm(1 - s)), right_z)
        if s < 4:
            za_l[s] = send(ablk(y, zm(s - 1)), ablk(y, zm(s - 1)), left_z)

    def zA_wait(s):
        za_r[s].wait_recv()
        if s < 4:
            za_l[s].wait_recv()

    def yA(j):
        b = ablk(y, zm(offs[j]))
        ya_r[j] = send(b, b, right_y)
        ya_l[j] = send(b, b, left_y)

    def yA_forward(j):
        ya_r[j].wait_recv()
        ya_l[j].wait_recv()
        if j % 2 == 0:
            b = ablk(ym(-1), zm(offs[j]))
            ya_f[j] = send(b, b, right_y)
        else:
            b = ablk(ym(1), zm(offs[j]))
            ya_f[j] = send(b, b, left_y)

    def zB(k):
        b = bblk(xi, z)
        zb_c[k] = send(b, b, dev(y, zm(k)))

    def xB(k):
        zb_c[k].wait_recv()
        b = bblk(xi, zm(-k))
        for m in (1, 3, 2):
            xb_c.append(send(b, b, xdev(m)))

    def transpose(src, dst, j):
        for k in range(CH // 128):
            piece = src[j, :, k * 128:(k + 1) * 128].astype(F32)
            dst[j, k * 128:(k + 1) * 128, :] = piece.T.astype(BF)

    zA(1)
    b = bblk(y, z)
    yb_c = [send(b, b, dev(ym(k), z)) for k in (1, 3, 2)]
    yA(0)

    seg = seg_ref[...].astype(F32)
    row_i = lax.broadcasted_iota(jnp.int32, (T, T), 0)
    col_i = lax.broadcasted_iota(jnp.int32, (T, T), 1)
    seg_s = jnp.broadcast_to(seg, (T, T))
    seg_t = jnp.sum(jnp.where(row_i == col_i, seg_s, 0.0), axis=1, keepdims=True)
    first = jnp.sum(jnp.where(seg_s < seg_t, 1.0, 0.0), axis=1, keepdims=True)
    mask[...] = jnp.where((seg_s == seg_t) & (col_i <= row_i), 1.0, 0.0)
    lane = lax.broadcasted_iota(jnp.int32, (T, HD), 1)
    place = lax.broadcasted_iota(jnp.int32, (T, HD), 0).astype(F32)
    inverse = jnp.exp(lax.rem(lane, HD // 2).astype(F32) * (-2.0 * LOG_BASE / HD))
    angles = (place - first) * inverse
    cs[...] = jnp.cos(angles)
    sn[...] = jnp.where(lane < HD // 2, -1.0, 1.0) * jnp.sin(angles)

    zA_wait(1)
    zA(2)
    yA(1)
    yA(2)
    for cp in yb_c:
        cp.wait_recv()
    zB(1)
    zB(7)
    yA_forward(0)
    transpose(sc, scT, 0)
    zA_wait(2)
    zA(3)
    yA(3)
    yA(4)
    zB(2)
    zB(6)
    yA_forward(1)
    yA_forward(2)
    transpose(sc, scT, 1)
    zA_wait(3)
    zA(4)
    yA(5)
    yA(6)
    zB(3)
    zB(5)
    xB(1)
    xB(7)
    yA_forward(3)
    yA_forward(4)
    transpose(sc, scT, 2)
    zA_wait(4)
    yA(7)
    pa_own = send(wa.at[c, y], wa.at[c, y], partner)
    zB(4)
    xB(2)
    xB(6)
    yA_forward(5)
    yA_forward(6)
    transpose(sc, scT, 3)
    for j in range(NY):
        loads[NY + j].wait()
    transpose(go, goT, 0)
    transpose(go, goT, 1)
    yA_forward(7)
    pa_l = send(wa.at[c, ym(-1)], wa.at[c, ym(-1)], partner)
    pa_r = send(wa.at[c, ym(1)], wa.at[c, ym(1)], partner)
    xB(3)
    xB(5)
    transpose(go, goT, 2)
    transpose(go, goT, 3)

    def project(yy, first_one=False):
        left = sc[yy]
        for h in range(NC):
            part = mm(left, wa[h, yy])
            proj[h] = part if first_one else proj[h] + part

    pa_own.wait_recv()
    project(y, True)
    pa_f = []

    def last_chunk(j):
        ya_f[j].wait_recv()
        b = ablk(ym(2), zm(offs[j]))
        pa_f.append(send(b, b, partner))

    for j in range(4):
        last_chunk(j)
    pa_l.wait_recv()
    project(ym(-1))
    xB(4)
    last_chunk(4)
    last_chunk(5)
    pa_r.wait_recv()
    project(ym(1))
    last_chunk(6)
    last_chunk(7)
    for cp in pa_f:
        cp.wait_recv()
    project(ym(2))

    def head_cols(h):
        return h // 3, (h % 3) * HD

    def turn(v):
        return v * cs[...] + pltpu.roll(v, HD // 2, 1) * sn[...]

    def four(block):
        return jnp.concatenate([block] * 4, axis=0)

    for h in range(5):
        hf, col = head_cols(h)
        v = proj[hf, :, col:col + HD]
        t = turn(v * rms(v)).astype(BF)
        if h == 4:
            kb[...] = t
        else:
            for i in range(3):
                qb[i, h * 128:(h + 1) * 128, :] = t[i * 128:(i + 1) * 128]
    kv[...] = proj[1, :, 2 * HD:].astype(BF)
    scale = HD ** -0.5
    for i in range(3):
        r0, n = slice(i * 128, (i + 1) * 128), (i + 1) * 128
        w = jnp.exp(mm(qb[i], kb[:n, :], NT) * scale) * four(mask[r0, :n])
        p = (w * (1.0 / jnp.sum(w, axis=-1, keepdims=True))).astype(BF)
        pb[i, :, :n] = p
        mixed = mm(p, kv[:n, :]).astype(BF)
        for h in range(4):
            mx[h // 2, r0, (h % 2) * HD:(h % 2 + 1) * HD] = mixed[h * 128:(h + 1) * 128]
        if i == 1:
            for cp in xb_c:
                cp.wait_recv()
            pb_s = [send(wb.at[c, j], wb.at[c, j], partner) for j in range(NY)]

    rb_s = []
    for j in range(NY):
        sb[j] = mm(goT[j], mx[o]).astype(BF)
        rb_s.append(send(sb.at[j], rb.at[j], partner))
    for cp in pb_s:
        cp.wait_recv()
    for h in range(NC):
        part = sum(mm(go[j], wb[h, j]) for j in range(NY)).astype(BF)
        for i in range(3):
            for k in range(2):
                gm[i, (2 * h + k) * 128:(2 * h + k + 1) * 128, :] = (
                    part[i * 128:(i + 1) * 128, k * HD:(k + 1) * HD])

    def add_into(ref, *others):
        total = ref[...].astype(F32)
        for other in others:
            total = total + other[...].astype(F32)
        ref[...] = total.astype(BF)

    xb_s = []

    def start_x():
        for j in range(NY):
            tb[j] = mm(goT[j], mx[c]).astype(BF)
        for j in range(NY):
            rb_s[j].wait_recv()
            add_into(tb.at[j], rb.at[j])
        for m in (1, 3, 2):
            t = lax.rem(xi + m, NX)
            xb_s.append(send(tb.at[t], xb.at[m - 1], xdev(m)))

    def norm_back(v, d, cos, sin):
        r = rms(v)
        xn = v * r
        dn = d * cos + pltpu.roll(d * sin, HD // 2, 1)
        return (r * (dn - xn * jnp.mean(dn * xn, axis=-1, keepdims=True))).astype(BF)

    dk = [jnp.zeros((128, HD), F32)] * 3
    dv = [jnp.zeros((128, HD), F32)] * 3
    for i in range(3):
        r0, n = slice(i * 128, (i + 1) * 128), (i + 1) * 128
        do = gm[i]
        p = pb[i, :, :n]
        pf = p.astype(F32)
        dp = mm(do, kv[:n, :], NT)
        delta = jnp.sum(pf * dp, axis=-1, keepdims=True)
        ds = (pf * (dp - delta) * scale).astype(BF)
        tk = mm(ds, qb[i], TN)
        tv = mm(p, do, TN)
        for m in range(i + 1):
            dk[m] = dk[m] + tk[m * 128:(m + 1) * 128]
            dv[m] = dv[m] + tv[m * 128:(m + 1) * 128]
        v = jnp.concatenate(
            [proj[h // 3, r0, (h % 3) * HD:(h % 3 + 1) * HD] for h in range(4)], axis=0)
        grad = norm_back(v, mm(ds, kb[:n, :]), four(cs[r0, :]), four(sn[r0, :]))
        for h in range(4):
            dpr[h // 3, r0, (h % 3) * HD:(h % 3 + 1) * HD] = grad[h * 128:(h + 1) * 128]
        if i == 0:
            start_x()
    dpr[1, :, HD:2 * HD] = norm_back(
        proj[1, :, HD:2 * HD], jnp.concatenate(dk, axis=0), cs[...], sn[...])
    dpr[1, :, 2 * HD:] = jnp.concatenate(dv, axis=0).astype(BF)

    ra_s = {}
    for k in (2, 1, 3, 0):
        yy = ym(k)
        sa[yy] = mm(scT[yy], dpr[o]).astype(BF)
        ra_s[k] = send(sa.at[yy], ra.at[yy], partner)
        ta[yy] = mm(scT[yy], dpr[c]).astype(BF)

    roffs = [4, 3, -3, 2, -2, 1, -1, 0]

    def tblk(yy, j):
        return ta.at[yy, rows(zm(roffs[j])), :]

    s1, s2r, s2l, sz = {}, {}, {}, {}
    ra_s[2].wait_recv()
    for j in range(8):
        add_into(tblk(ym(2), j), ra.at[ym(2), rows(zm(roffs[j])), :])
        s1[j] = send(tblk(ym(2), j), ya1.at[j], right_y if j % 2 == 0 else left_y)
    ra_s[1].wait_recv()
    add_into(ta.at[ym(1)], ra.at[ym(1)])
    ra_s[3].wait_recv()
    add_into(ta.at[ym(3)], ra.at[ym(3)])

    def step2(j):
        s1[j].wait_recv()
        add_into(tblk(ym(1) if j % 2 == 0 else ym(3), j), ya1.at[j])
        s2r[j] = send(tblk(ym(1), j), ya2.at[0, j], right_y)
        s2l[j] = send(tblk(ym(3), j), ya2.at[1, j], left_y)

    def step3(j):
        s2r[j].wait_recv()
        s2l[j].wait_recv()
        add_into(tblk(y, j), ya2.at[0, j], ya2.at[1, j])

    def step_z(j):
        if j == 0:
            sz[0] = send(tblk(y, 0), za.at[0], right_z)
        elif j == 7:
            return
        elif j % 2 == 1:
            n = (j + 1) // 2
            sz[n - 1].wait_recv()
            add_into(tblk(y, j), za.at[n - 1])
            sz[n] = send(tblk(y, j), za.at[n], right_z)
        else:
            n = 3 + j // 2
            if n > 4:
                sz[n - 1].wait_recv()
                add_into(tblk(y, j), za.at[n - 1])
            sz[n] = send(tblk(y, j), za.at[n], left_z)

    def out_chunk(j):
        update = sum(mm(mx[h], wb[h, j], NT) for h in range(NC))
        out_ref[:, j * CH:(j + 1) * CH] = (tok[j].astype(F32) + update).astype(BF)

    def gs_chunk(j):
        gs[j] = sum(mm(dpr[h], wa[h, j], NT) for h in range(NC))

    zb_s = []

    def sum_x():
        for cp in xb_s:
            cp.wait_recv()
        add_into(tb.at[xi], xb.at[0], xb.at[1], xb.at[2])
        for k in (4, 3, 5, 2, 6, 1, 7):
            zb_s.append(send(tb.at[xi, rows(zm(k)), :], zb.at[k - 1], dev(y, zm(k))))

    def piece_copy(p):
        t = lax.rem(me8 + p, GROUP)
        return pltpu.make_async_remote_copy(
            src_ref=xsb.at[t], dst_ref=xrb.at[2 * y + c],
            send_sem=fsem.at[p], recv_sem=fsem.at[GROUP + 2 * y + c],
            device_id=((xi * NZ + z) * GROUP + t,), device_id_type=pl.DeviceIdType.MESH,
        )

    def self_copy():
        return pltpu.make_async_copy(
            xsb.at[me8], xrb.at[2 * y + c], fsem.at[GROUP + 2 * y + c])

    def sum_z():
        for cp in zb_s:
            cp.wait_recv()
        finb[:BLK, :] = tb[xi, rows(z), :].astype(F32) + sum(
            zb[k].astype(F32) for k in range(NZ - 1))
        finb[BLK:, :] = jnp.zeros((PAD, WB_), F32)
        for i in range(GROUP):
            xsb[i] = finb[i * ROWS:i * ROWS + PAD, :].astype(BF)
        for p in range(1, GROUP):
            piece_copy(p).start()

        @pl.when(y != xi)
        def _():
            piece_copy(0).start()

        @pl.when(y == xi)
        def _():
            self_copy().start()

    out_chunk(0)
    out_chunk(1)
    step2(0)
    step2(1)
    out_chunk(2)
    step2(2)
    step2(3)
    out_chunk(3)
    step2(4)
    step2(5)
    ra_s[0].wait_recv()
    add_into(ta.at[y], ra.at[y])
    gs_chunk(0)
    step2(6)
    step2(7)
    gs_chunk(1)
    step3(0)
    step_z(0)
    gs_chunk(2)
    sum_x()
    step3(1)
    step3(2)
    step_z(1)
    step_z(2)
    gs_chunk(3)
    step3(3)
    step3(4)
    step_z(3)
    step_z(4)

    def token_rows(i, _):
        r0 = pl.ds(pl.multiple_of(i * 16, 16), 16)
        r = rr[r0, :][:, :1]
        xn = [tok[j, r0, :].astype(F32) * r for j in range(NY)]
        g = [gs[j, r0, :] for j in range(NY)]
        dot = sum(jnp.sum(a * b, axis=-1, keepdims=True) for a, b in zip(xn, g)) * (1.0 / D)
        for j in range(NY):
            path = (r * (g[j] - xn[j] * dot)).astype(BF).astype(F32)
            gt_ref[r0, j * CH:(j + 1) * CH] = (go[j, r0, :].astype(F32) + path).astype(BF)
        return 0

    lax.fori_loop(0, 8, token_rows, 0, unroll=2)
    step3(5)
    step3(6)
    step_z(5)
    step_z(6)
    sum_z()
    step3(7)
    sz[3].wait_recv()
    sz[6].wait_recv()
    fin[:BLK, :] = (
        tblk(y, 7)[...].astype(F32) + za[3].astype(F32) + za[6].astype(F32))
    fin[BLK:, :] = jnp.zeros((PAD, WA_), F32)

    for i in range(GROUP):
        xs[i] = fin[i * ROWS:i * ROWS + PAD, :].astype(BF)
    last = []
    for p in range(1, GROUP):
        t = lax.rem(me8 + p, GROUP)
        last.append(send(xs.at[t], xr.at[me8], base + t))
    xr[me8] = xs[me8]
    lax.fori_loop(8, T // 16, token_rows, 0, unroll=2)
    for i in range(GROUP):
        pltpu.make_async_copy(xsb.at[i], xrb.at[i], fsem.at[GROUP + i]).wait()
    for h in range(NC):
        s_ref[h, :, WA_:] = sum(xrb[2 * i + h].astype(F32) for i in range(NY))
    for cp in copies[:-len(last)]:
        cp.wait_send()
    for p in range(1, GROUP):
        piece_copy(p).wait_send()

    @pl.when(y != xi)
    def _():
        piece_copy(0).wait_send()

    for cp in last:
        cp.wait_recv()
    for h in range(NC):
        s_ref[h, :, :WA_] = sum(xr[2 * i + h].astype(F32) for i in range(NX))
    for cp in last:
        cp.wait_send()


def finish_kernel(out_in, gt_in, s_ref, gain_ref, wq_ref, out_hbm, gt_hbm, gq_ref, gw_ref, gg_ref, sem):
    moves = []
    for i, (src, dst) in enumerate(((out_in, out_hbm), (gt_in, gt_hbm))):
        for j in range(4):
            part = pl.ds(j * (T // 4), T // 4)
            cp = pltpu.make_async_copy(src.at[part, :], dst.at[part, :], sem.at[4 * i + j])
            cp.start()
            moves.append(cp)
    eye = lax.broadcasted_iota(jnp.int32, (ROWS, ROWS), 0) == lax.broadcasted_iota(
        jnp.int32, (ROWS, ROWS), 1)
    gain = jnp.sum(
        jnp.where(eye, jnp.broadcast_to(gain_ref[...].astype(F32), (ROWS, ROWS)), 0.0),
        axis=1, keepdims=True)
    along = jnp.zeros((ROWS, 1), F32)
    for h in range(NC):
        part = s_ref[h][:ROWS, :WA_]
        cols = slice(h * WA_, (h + 1) * WA_)
        gq_ref[:, cols] = part * gain
        along += jnp.sum(part * wq_ref[:, cols].astype(F32), axis=1, keepdims=True)
        gw_ref[:, h * WB_:(h + 1) * WB_] = s_ref[h][:ROWS, WA_:]
    gg_ref[...] = jnp.sum(
        jnp.where(eye, jnp.broadcast_to(along, (ROWS, ROWS)), 0.0), axis=0, keepdims=True)
    for cp in moves:
        cp.wait()


def block_step(tokens, segment_ids, grad_out, norm_gain, w_qkv, w_out):
    any_, vm = pl.BlockSpec(memory_space=pl.ANY), pl.BlockSpec(memory_space=pltpu.VMEM)
    hbm = pl.BlockSpec(memory_space=pltpu.HBM)
    v = pltpu.VMEM
    gain = norm_gain.reshape(1, ROWS)
    out, grad_tokens, sums = pl.pallas_call(
        kernel,
        out_shape=(
            pltpu.VMEM((T, D), BF),
            pltpu.VMEM((T, D), BF),
            pltpu.VMEM((NC, PAD, WX), F32),
        ),
        in_specs=[hbm] * 6,
        out_specs=(vm, vm, vm),
        scratch_shapes=[
            v((1, T), jnp.int32), v((1, ROWS), BF), v((ROWS, NC * WA_), BF), v((ROWS, NC * WB_), BF),
            v((NY, T, CH), BF), v((NY, T, CH), BF), v((NY, T, CH), BF),
            v((NY, CH, T), BF), v((NY, CH, T), BF), v((T, 128), F32),
            v((NC, PAD, WX), BF), v((GROUP, PAD, WX), BF), v((BLK, WX), F32),
            v((NC, NY, CH, WA_), BF), v((NC, NY, CH, WB_), BF),
            v((NC, T, WA_), F32), v((3, 512, HD), BF), v((T, T), F32),
            v((T, HD), F32), v((T, HD), F32),
            v((3, 512, HD), BF), v((T, HD), BF), v((T, HD), BF), v((3, 512, T), BF),
            v((NC, T, WB_), BF), v((NC, T, WA_), BF), v((NY, T, CH), F32),
            v((NY, CH, WA_), BF), v((NY, CH, WA_), BF), v((NY, CH, WA_), BF),
            v((NZ, BLK, WA_), BF), v((2, NZ, BLK, WA_), BF), v((7, BLK, WA_), BF),
            v((NY, CH, WB_), BF), v((NY, CH, WB_), BF), v((NY, CH, WB_), BF),
            v((3, CH, WB_), BF), v((NZ - 1, BLK, WB_), BF),
            v((BLK + PAD, WA_), F32), v((BLK + PAD, WB_), F32),
            v((GROUP, PAD, WA_), BF), v((GROUP, PAD, WA_), BF),
            v((GROUP, PAD, WB_), BF), v((GROUP, PAD, WB_), BF),
            pltpu.SemaphoreType.DMA((2 * NY + 4,)),
            pltpu.SemaphoreType.DMA((N_COPIES,)), pltpu.SemaphoreType.DMA((N_COPIES,)),
            pltpu.SemaphoreType.DMA((2 * GROUP,)),
        ],
        compiler_params=pltpu.CompilerParams(
            collective_id=0, has_side_effects=True, vmem_limit_bytes=55 * 2 ** 20),
        name="block_step",
    )(tokens, grad_out, segment_ids, gain, w_qkv, w_out.T)
    out, grad_tokens, grad_qkv, grad_wout, grad_gain = pl.pallas_call(
        finish_kernel,
        out_shape=(
            jax.ShapeDtypeStruct((T, D), BF),
            jax.ShapeDtypeStruct((T, D), BF),
            jax.ShapeDtypeStruct((ROWS, NC * WA_), F32),
            jax.ShapeDtypeStruct((ROWS, NC * WB_), F32),
            jax.ShapeDtypeStruct((1, ROWS), F32),
        ),
        in_specs=[vm, vm, vm, vm, vm],
        out_specs=(any_, any_, vm, vm, vm),
        scratch_shapes=[pltpu.SemaphoreType.DMA((8,))],
        compiler_params=pltpu.CompilerParams(vmem_limit_bytes=8 * 2 ** 20),
        name="finish",
    )(out, grad_tokens, sums, gain, w_qkv)
    return out, grad_tokens, grad_qkv, grad_wout.T, grad_gain.reshape(ROWS)


def solution(mesh):
    return jax.shard_map(
        block_step,
        mesh=mesh,
        in_specs=(P("dp", None), P("dp", None), P("dp", None), P("dp"), P("dp", None),
                  P(None, "dp")),
        out_specs=(P("dp", None), P("dp", None), P("dp", None), P(None, "dp"), P("dp")),
        check_vma=False,
    )
```

```python
import math

import jax
import jax.numpy as jnp
from jax import lax
from jax.experimental import pallas as pl
from jax.experimental.pallas import tpu as pltpu
from jax.sharding import PartitionSpec as P

NY, NZ, NX, NC = 4, 8, 4, 2
D, T, HD = 2560, 384, 128
ROWS = 10
GROUP = NX * NC
BLK = GROUP * ROWS
CH = NZ * BLK
WA_, WB_ = 384, 256
WX = WA_ + WB_
W1, W2 = 256, 128
PAD = 16
EPS = 1e-06
LOG_BASE = math.log(1000000.0)
N_COPIES = 256
BF, F32 = jnp.bfloat16, jnp.float32
NT = (((1,), (1,)), ((), ()))
TN = (((0,), (0,)), ((), ()))


def mm(a, b, dims=(((1,), (0,)), ((), ()))):
    return lax.dot_general(a, b, dims, preferred_element_type=F32)


def rms(x):
    return lax.rsqrt(jnp.mean(x * x, axis=-1, keepdims=True) + EPS)


def kernel(
    tok_hbm, go_hbm, seg_hbm, gain_hbm, wq_hbm, wo_hbm,
    out_ref, gt_ref, s_ref,
    seg_ref, gain_ref, wq_ref, wo_ref,
    tok, go, sc, scT, goT, rr, blk, xg, tmp, wa, wb, proj, gm, mask, cs, sn,
    qb, kb, kv, pb, mx, dpr, gs,
    ta, sa, ra, ya1, ya2, za, zc, yc, tb, sb, rb, xb, zb, fin, finb, xs, xr, xsb, xrb,
    lsem, ssem, rsem, fsem,
):
    idx = lax.axis_index("dp")
    me8 = lax.rem(idx, GROUP)
    base = idx - me8
    c = lax.rem(idx, 2)
    o = 1 - c
    xi = lax.div(me8, 2)
    yz = lax.div(idx, GROUP)
    z = lax.rem(yz, NZ)
    y = lax.div(yz, NZ)

    def ym(k):
        return lax.rem(y + (k + NY), NY)

    def zm(k):
        return lax.rem(z + (k + NZ), NZ)

    def dev(yy, zz):
        return (yy * NZ + zz) * GROUP + me8

    def xdev(k):
        return base + lax.rem(me8 + 2 * k, GROUP)

    right_y, left_y = dev(ym(1), z), dev(ym(-1), z)
    right_z, left_z = dev(y, zm(1)), dev(y, zm(-1))
    partner = idx + 1 - 2 * c

    def rows(zz):
        return pl.ds(pl.multiple_of(zz * BLK, 16), BLK)

    copies = []

    def send(src, dst, target):
        n = len(copies)
        copy = pltpu.make_async_remote_copy(
            src_ref=src, dst_ref=dst, send_sem=ssem.at[n], recv_sem=rsem.at[n],
            device_id=(target,), device_id_type=pl.DeviceIdType.MESH,
        )
        copy.start()
        copies.append(copy)
        return copy

    small = []
    for i, (src, dst) in enumerate(
            ((gain_hbm, gain_ref), (wq_hbm, wq_ref), (wo_hbm, wo_ref), (seg_hbm, seg_ref))):
        cp = pltpu.make_async_copy(src, dst, lsem.at[2 * NY + i])
        cp.start()
        small.append(cp)

    barrier = pltpu.get_barrier_semaphore()

    def greet(d):
        pl.semaphore_signal(barrier, inc=1, device_id=(d,), device_id_type=pl.DeviceIdType.MESH)

    greetings = [base + lax.rem(me8 + p, GROUP) for p in range(1, GROUP)]
    greetings += [dev(ym(k), z) for k in range(1, NY)]
    greetings += [dev(y, zm(k)) for k in range(1, NZ)]
    for k in range(NY):
        for core in (c, o):
            if k > 0 or core is o:
                greetings.append((ym(k) * NZ + z) * GROUP + 2 * y + core)
    for d in greetings:
        greet(d)

    @pl.when(y != xi)
    def _():
        greet((y * NZ + z) * GROUP + 2 * y + c)

    loads = []
    for i, (src, dst) in enumerate(((tok_hbm, tok), (go_hbm, go))):
        for j in range(NY):
            cp = pltpu.make_async_copy(
                src.at[:, pl.ds(j * CH, CH)], dst.at[j], lsem.at[i * NY + j])
            cp.start()
            loads.append(cp)

    for cp in small:
        cp.wait()
    diag = lax.broadcasted_iota(jnp.int32, (PAD, ROWS), 0) == lax.broadcasted_iota(
        jnp.int32, (PAD, ROWS), 1)
    gain_diag = jnp.where(diag, jnp.broadcast_to(gain_ref[...].astype(F32), (PAD, ROWS)), 0.0)
    gw = mm(gain_diag.astype(BF), wq_ref[...]).astype(BF)
    wt = mm(diag.astype(F32).astype(BF), wo_ref[...]).astype(BF)
    for h in range(NC):
        blk[h, :, :WA_] = gw[:, h * WA_:(h + 1) * WA_]
        blk[h, :, WA_:] = wt[:, h * WB_:(h + 1) * WB_]

    pl.semaphore_wait(barrier, jnp.where(y == xi, len(greetings), len(greetings) + 1))

    xcop = []
    for p in range(1, GROUP):
        t = lax.rem(me8 + p, GROUP)
        xcop.append(send(blk.at[lax.rem(t, 2)], xg.at[me8], base + t))
    xg[me8] = blk[c]

    for j in range(NY):
        loads[j].wait()

    def scale_rows(i, _):
        r0 = pl.ds(pl.multiple_of(i * 16, 16), 16)
        parts = [tok[j, r0, :].astype(F32) for j in range(NY)]
        total = sum(jnp.sum(p * p, axis=-1, keepdims=True) for p in parts)
        r = lax.rsqrt(total * (1.0 / D) + EPS)
        rr[r0, :] = jnp.broadcast_to(r, (16, 128))
        for j in range(NY):
            sc[j, r0, :] = (parts[j] * r).astype(BF)
        return 0

    lax.fori_loop(0, T // 16, scale_rows, 0, unroll=2)

    for cp in xcop:
        cp.wait_recv()
    for i in range(GROUP):
        tmp[i * ROWS:(i + 1) * ROWS, :] = xg[i].astype(F32)[:ROWS, :]
    wa[c, y, rows(z), :] = tmp[:, :WA_].astype(BF)
    wb[c, y, rows(z), :] = tmp[:, WA_:].astype(BF)

    def ablk(yy, zz):
        return wa.at[c, yy, rows(zz), :]

    def bblk(yy, zz):
        return wb.at[c, yy, rows(zz), :]

    offs = [0, -1, 1, -2, 2, -3, 3, -4]
    za_r, za_l, ya_r, ya_l, ya_f, zb_c, xb_c = {}, {}, {}, {}, {}, {}, []

    def zA(s):
        za_r[s] = send(ablk(y, zm(1 - s)), ablk(y, zm(1 - s)), right_z)
        if s < 4:
            za_l[s] = send(ablk(y, zm(s - 1)), ablk(y, zm(s - 1)), left_z)

    def zA_wait(s):
        za_r[s].wait_recv()
        if s < 4:
            za_l[s].wait_recv()

    def yA(j):
        b = ablk(y, zm(offs[j]))
        ya_r[j] = send(b, b, right_y)
        ya_l[j] = send(b, b, left_y)

    def yA_forward(j):
        ya_r[j].wait_recv()
        ya_l[j].wait_recv()
        if j % 2 == 0:
            b = ablk(ym(-1), zm(offs[j]))
            ya_f[j] = send(b, b, right_y)
        else:
            b = ablk(ym(1), zm(offs[j]))
            ya_f[j] = send(b, b, left_y)

    def zB(k):
        b = bblk(xi, z)
        zb_c[k] = send(b, b, dev(y, zm(k)))

    def xB(k):
        zb_c[k].wait_recv()
        b = bblk(xi, zm(-k))
        for m in (1, 3, 2):
            xb_c.append((m, send(b, b, xdev(m))))

    def transpose(src, dst, j):
        for k in range(CH // 128):
            piece = src[j, :, k * 128:(k + 1) * 128].astype(F32)
            dst[j, k * 128:(k + 1) * 128, :] = piece.T.astype(BF)

    zA(1)
    b = bblk(y, z)
    yb_c = [send(b, b, dev(ym(k), z)) for k in (1, 3, 2)]
    yA(0)

    seg = seg_ref[...].astype(F32)
    row_i = lax.broadcasted_iota(jnp.int32, (T, T), 0)
    col_i = lax.broadcasted_iota(jnp.int32, (T, T), 1)
    seg_s = jnp.broadcast_to(seg, (T, T))
    seg_t = jnp.sum(jnp.where(row_i == col_i, seg_s, 0.0), axis=1, keepdims=True)
    first = jnp.sum(jnp.where(seg_s < seg_t, 1.0, 0.0), axis=1, keepdims=True)
    mask[...] = jnp.where((seg_s == seg_t) & (col_i <= row_i), 1.0, 0.0)
    lane = lax.broadcasted_iota(jnp.int32, (T, HD), 1)
    place = lax.broadcasted_iota(jnp.int32, (T, HD), 0).astype(F32)
    inverse = jnp.exp(lax.rem(lane, HD // 2).astype(F32) * (-2.0 * LOG_BASE / HD))
    angles = (place - first) * inverse
    cs[...] = jnp.cos(angles)
    sn[...] = jnp.where(lane < HD // 2, -1.0, 1.0) * jnp.sin(angles)

    zA_wait(1)
    zA(2)
    yA(1)
    yA(2)
    for cp in yb_c:
        cp.wait_recv()
    zB(1)
    zB(7)
    yA_forward(0)
    transpose(sc, scT, 0)
    zA_wait(2)
    zA(3)
    yA(3)
    yA(4)
    zB(2)
    zB(6)
    yA_forward(1)
    yA_forward(2)
    transpose(sc, scT, 1)
    zA_wait(3)
    zA(4)
    yA(5)
    yA(6)
    zB(3)
    zB(5)
    zB(4)
    xB(1)
    xB(7)
    yA_forward(3)
    yA_forward(4)
    transpose(sc, scT, 2)
    zA_wait(4)
    yA(7)
    pa_own = send(wa.at[c, y], wa.at[c, y], partner)
    xB(2)
    xB(6)
    transpose(sc, scT, 3)
    yA_forward(5)
    xB(3)
    xB(5)
    yA_forward(6)
    for j in range(NY):
        loads[NY + j].wait()
    transpose(go, goT, 0)
    transpose(go, goT, 1)
    xB(4)
    yA_forward(7)
    pa_l = send(wa.at[c, ym(-1)], wa.at[c, ym(-1)], partner)
    pa_r = send(wa.at[c, ym(1)], wa.at[c, ym(1)], partner)
    pb_s = [send(wb.at[c, xi], wb.at[c, xi], partner)]
    transpose(go, goT, 2)
    transpose(go, goT, 3)

    def project(yy, first_one=False):
        left = sc[yy]
        for h in range(NC):
            part = mm(left, wa[h, yy])
            proj[h] = part if first_one else proj[h] + part

    pa_own.wait_recv()
    project(y, True)
    pa_f = []

    def last_chunk(j):
        ya_f[j].wait_recv()
        b = ablk(ym(2), zm(offs[j]))
        pa_f.append(send(b, b, partner))

    for j in range(4):
        last_chunk(j)
    pa_l.wait_recv()
    project(ym(-1))
    last_chunk(4)
    last_chunk(5)
    pa_r.wait_recv()
    project(ym(1))
    last_chunk(6)
    last_chunk(7)
    for cp in pa_f:
        cp.wait_recv()
    project(ym(2))

    def head_cols(h):
        return h // 3, (h % 3) * HD

    def turn(v):
        return v * cs[...] + pltpu.roll(v, HD // 2, 1) * sn[...]

    def four(block):
        return jnp.concatenate([block] * 4, axis=0)

    for h in range(5):
        hf, col = head_cols(h)
        v = proj[hf, :, col:col + HD]
        t = turn(v * rms(v)).astype(BF)
        if h == 4:
            kb[...] = t
        else:
            for i in range(3):
                qb[i, h * 128:(h + 1) * 128, :] = t[i * 128:(i + 1) * 128]
    kv[...] = proj[1, :, 2 * HD:].astype(BF)
    scale = HD ** -0.5
    for i in range(3):
        r0, n = slice(i * 128, (i + 1) * 128), (i + 1) * 128
        w = jnp.exp(mm(qb[i], kb[:n, :], NT) * scale) * four(mask[r0, :n])
        p = (w * (1.0 / jnp.sum(w, axis=-1, keepdims=True))).astype(BF)
        pb[i, :, :n] = p
        mixed = mm(p, kv[:n, :]).astype(BF)
        for h in range(4):
            mx[h // 2, r0, (h % 2) * HD:(h % 2 + 1) * HD] = mixed[h * 128:(h + 1) * 128]
        if i == 1:
            for m in (1, 3, 2):
                for mm_, cp in xb_c:
                    if mm_ == m:
                        cp.wait_recv()
                b = wb.at[c, lax.rem(xi + NX - m, NX)]
                pb_s.append(send(b, b, partner))

    rb_s = []
    for j in range(NY):
        sb[j] = mm(goT[j], mx[o]).astype(BF)
        rb_s.append(send(sb.at[j], rb.at[j], partner))
    for cp in pb_s:
        cp.wait_recv()
    for h in range(NC):
        part = sum(mm(go[j], wb[h, j]) for j in range(NY)).astype(BF)
        for i in range(3):
            for k in range(2):
                gm[i, (2 * h + k) * 128:(2 * h + k + 1) * 128, :] = (
                    part[i * 128:(i + 1) * 128, k * HD:(k + 1) * HD])

    def add_into(ref, *others):
        total = ref[...].astype(F32)
        for other in others:
            total = total + other[...].astype(F32)
        ref[...] = total.astype(BF)

    xb_s = []

    def start_x():
        for j in range(NY):
            tb[j] = mm(goT[j], mx[c]).astype(BF)
        for j in range(NY):
            rb_s[j].wait_recv()
            add_into(tb.at[j], rb.at[j])
        for m in (1, 3, 2):
            t = lax.rem(xi + m, NX)
            xb_s.append(send(tb.at[t], xb.at[m - 1], xdev(m)))

    def norm_back(v, d, cos, sin):
        r = rms(v)
        xn = v * r
        dn = d * cos + pltpu.roll(d * sin, HD // 2, 1)
        return (r * (dn - xn * jnp.mean(dn * xn, axis=-1, keepdims=True))).astype(BF)

    dk = [jnp.zeros((128, HD), F32)] * 3
    dv = [jnp.zeros((128, HD), F32)] * 3
    for i in range(3):
        r0, n = slice(i * 128, (i + 1) * 128), (i + 1) * 128
        do = gm[i]
        p = pb[i, :, :n]
        pf = p.astype(F32)
        dp = mm(do, kv[:n, :], NT)
        delta = jnp.sum(pf * dp, axis=-1, keepdims=True)
        ds = (pf * (dp - delta) * scale).astype(BF)
        tk = mm(ds, qb[i], TN)
        tv = mm(p, do, TN)
        for m in range(i + 1):
            dk[m] = dk[m] + tk[m * 128:(m + 1) * 128]
            dv[m] = dv[m] + tv[m * 128:(m + 1) * 128]
        v = jnp.concatenate(
            [proj[h // 3, r0, (h % 3) * HD:(h % 3 + 1) * HD] for h in range(4)], axis=0)
        grad = norm_back(v, mm(ds, kb[:n, :]), four(cs[r0, :]), four(sn[r0, :]))
        for h in range(4):
            dpr[h // 3, r0, (h % 3) * HD:(h % 3 + 1) * HD] = grad[h * 128:(h + 1) * 128]
        if i == 0:
            start_x()
    dpr[1, :, HD:2 * HD] = norm_back(
        proj[1, :, HD:2 * HD], jnp.concatenate(dk, axis=0), cs[...], sn[...])
    dpr[1, :, 2 * HD:] = jnp.concatenate(dv, axis=0).astype(BF)

    ra_s = {}

    def partial(k):
        yy = ym(k)
        sa[yy] = mm(scT[yy], dpr[o]).astype(BF)
        ra_s[k] = send(sa.at[yy], ra.at[yy], partner)
        ta[yy] = mm(scT[yy], dpr[c]).astype(BF)

    roffs = [4, 3, -3, 2, -2, 1, -1, 0]

    def tblk(yy, j):
        return ta.at[yy, rows(zm(roffs[j])), pl.ds(0, W1)]

    def thalf(h, k):
        return ta.at[pl.ds(2 * h, 2), rows(zm(k)), pl.ds(W1, W2)]

    s1, s2r, s2l, sz, zc_s = {}, {}, {}, {}, {}
    partial(2)
    partial(1)
    ra_s[2].wait_recv()
    for j in range(8):
        b = rows(zm(roffs[j]))
        add_into(ta.at[ym(2), b, :], ra.at[ym(2), b, :])
        s1[j] = send(tblk(ym(2), j), ya1.at[j], right_y if j % 2 == 0 else left_y)
    partial(3)
    partial(0)
    for k in (1, 3, 0):
        ra_s[k].wait_recv()
        add_into(ta.at[ym(k)], ra.at[ym(k)])

    def zc_send(side, h, s):
        zc_s[side, h, s] = send(
            thalf(h, -s if side else s), zc.at[side, h, s - 1], left_z if side else right_z)

    def zc_add(side, h, s):
        zc_s[side, h, s + 1].wait_recv()
        add_into(thalf(h, -s if side else s), zc.at[side, h, s])

    def zc_round(n):
        for side, h, s in ((0, 0, 4 - n), (1, 1, 4 - n), (0, 1, 3 - n), (1, 0, 3 - n)):
            if s > 0:
                zc_add(side, h, s)
                zc_send(side, h, s)

    def zc_end():
        for h in range(2):
            for side in range(2):
                zc_s[side, h, 1].wait_recv()
            add_into(thalf(h, 0), zc.at[0, h, 0], zc.at[1, h, 0])
        return [
            send(ta.at[ym(k), rows(z), pl.ds(W1, W2)], yc.at[k - 1], dev(ym(k), z))
            for k in (2, 1, 3)]

    zc_send(0, 0, 4)
    zc_send(1, 1, 4)
    zc_send(0, 1, 3)
    zc_send(1, 0, 3)

    def step2(j):
        s1[j].wait_recv()
        add_into(tblk(ym(1) if j % 2 == 0 else ym(3), j), ya1.at[j])
        s2r[j] = send(tblk(ym(1), j), ya2.at[0, j], right_y)
        s2l[j] = send(tblk(ym(3), j), ya2.at[1, j], left_y)

    def step3(j):
        s2r[j].wait_recv()
        s2l[j].wait_recv()
        add_into(tblk(y, j), ya2.at[0, j], ya2.at[1, j])

    def step_z(j):
        if j == 0:
            sz[0] = send(tblk(y, 0), za.at[0], right_z)
        elif j == 7:
            return
        elif j % 2 == 1:
            n = (j + 1) // 2
            sz[n - 1].wait_recv()
            add_into(tblk(y, j), za.at[n - 1])
            sz[n] = send(tblk(y, j), za.at[n], right_z)
        else:
            n = 3 + j // 2
            if n > 4:
                sz[n - 1].wait_recv()
                add_into(tblk(y, j), za.at[n - 1])
            sz[n] = send(tblk(y, j), za.at[n], left_z)

    def out_chunk(j):
        update = sum(mm(mx[h], wb[h, j], NT) for h in range(NC))
        out_ref[:, j * CH:(j + 1) * CH] = (tok[j].astype(F32) + update).astype(BF)

    def gs_chunk(j):
        gs[j] = sum(mm(dpr[h], wa[h, j], NT) for h in range(NC))

    zb_s = []

    def sum_x():
        for cp in xb_s:
            cp.wait_recv()
        add_into(tb.at[xi], xb.at[0], xb.at[1], xb.at[2])
        for k in (4, 3, 5, 2, 6, 1, 7):
            zb_s.append(send(tb.at[xi, rows(zm(k)), :], zb.at[k - 1], dev(y, zm(k))))

    def piece_copy(p):
        t = lax.rem(me8 + p, GROUP)
        return pltpu.make_async_remote_copy(
            src_ref=xsb.at[t], dst_ref=xrb.at[2 * y + c],
            send_sem=fsem.at[p], recv_sem=fsem.at[GROUP + 2 * y + c],
            device_id=((xi * NZ + z) * GROUP + t,), device_id_type=pl.DeviceIdType.MESH,
        )

    def self_copy():
        return pltpu.make_async_copy(
            xsb.at[me8], xrb.at[2 * y + c], fsem.at[GROUP + 2 * y + c])

    def sum_z():
        for cp in zb_s:
            cp.wait_recv()
        finb[:BLK, :] = tb[xi, rows(z), :].astype(F32) + sum(
            zb[k].astype(F32) for k in range(NZ - 1))
        finb[BLK:, :] = jnp.zeros((PAD, WB_), F32)
        for i in range(GROUP):
            xsb[i] = finb[i * ROWS:i * ROWS + PAD, :].astype(BF)
        for p in range(1, GROUP):
            piece_copy(p).start()

        @pl.when(y != xi)
        def _():
            piece_copy(0).start()

        @pl.when(y == xi)
        def _():
            self_copy().start()

    out_chunk(0)
    out_chunk(1)
    step2(0)
    step2(1)
    zc_round(1)
    out_chunk(2)
    step2(2)
    step2(3)
    out_chunk(3)
    zc_round(2)
    step2(4)
    step2(5)
    gs_chunk(0)
    step2(6)
    step2(7)
    zc_round(3)
    gs_chunk(1)
    step3(0)
    step_z(0)
    gs_chunk(2)
    yc_s = zc_end()
    step3(1)
    step3(2)
    step_z(1)
    step_z(2)
    sum_x()
    gs_chunk(3)
    step3(3)
    step3(4)
    step_z(3)
    step_z(4)

    def token_rows(i, _):
        r0 = pl.ds(pl.multiple_of(i * 16, 16), 16)
        r = rr[r0, :][:, :1]
        xn = [tok[j, r0, :].astype(F32) * r for j in range(NY)]
        g = [gs[j, r0, :] for j in range(NY)]
        dot = sum(jnp.sum(a * b, axis=-1, keepdims=True) for a, b in zip(xn, g)) * (1.0 / D)
        for j in range(NY):
            path = (r * (g[j] - xn[j] * dot)).astype(BF).astype(F32)
            gt_ref[r0, j * CH:(j + 1) * CH] = (go[j, r0, :].astype(F32) + path).astype(BF)
        return 0

    lax.fori_loop(0, 8, token_rows, 0, unroll=2)
    step3(5)
    step3(6)
    step_z(5)
    step_z(6)
    lax.fori_loop(8, 16, token_rows, 0, unroll=2)
    step3(7)
    for cp in yc_s:
        cp.wait_recv()
    fin[:BLK, W1:] = ta[y, rows(z), W1:].astype(F32) + sum(
        yc[k].astype(F32) for k in range(NY - 1))
    sz[3].wait_recv()
    sz[6].wait_recv()
    fin[:BLK, :W1] = (
        tblk(y, 7)[...].astype(F32) + za[3].astype(F32) + za[6].astype(F32))
    fin[BLK:, :] = jnp.zeros((PAD, WA_), F32)

    for i in range(GROUP):
        xs[i] = fin[i * ROWS:i * ROWS + PAD, :].astype(BF)
    last = []
    for p in range(1, GROUP):
        t = lax.rem(me8 + p, GROUP)
        last.append(send(xs.at[t], xr.at[me8], base + t))
    xr[me8] = xs[me8]
    sum_z()
    lax.fori_loop(16, T // 16, token_rows, 0, unroll=2)
    for i in range(GROUP):
        pltpu.make_async_copy(xsb.at[i], xrb.at[i], fsem.at[GROUP + i]).wait()
    for h in range(NC):
        s_ref[h, :, WA_:] = sum(xrb[2 * i + h].astype(F32) for i in range(NY))
    for cp in copies[:-len(last)]:
        cp.wait_send()
    for p in range(1, GROUP):
        piece_copy(p).wait_send()

    @pl.when(y != xi)
    def _():
        piece_copy(0).wait_send()

    for cp in last:
        cp.wait_recv()
    for h in range(NC):
        s_ref[h, :, :WA_] = sum(xr[2 * i + h].astype(F32) for i in range(NX))
    for cp in last:
        cp.wait_send()


def finish_kernel(out_in, gt_in, s_ref, gain_ref, wq_ref, out_hbm, gt_hbm, gq_ref, gw_ref, gg_ref, sem):
    moves = []
    for i, (src, dst) in enumerate(((out_in, out_hbm), (gt_in, gt_hbm))):
        for j in range(4):
            part = pl.ds(j * (T // 4), T // 4)
            cp = pltpu.make_async_copy(src.at[part, :], dst.at[part, :], sem.at[4 * i + j])
            cp.start()
            moves.append(cp)
    eye = lax.broadcasted_iota(jnp.int32, (ROWS, ROWS), 0) == lax.broadcasted_iota(
        jnp.int32, (ROWS, ROWS), 1)
    gain = jnp.sum(
        jnp.where(eye, jnp.broadcast_to(gain_ref[...].astype(F32), (ROWS, ROWS)), 0.0),
        axis=1, keepdims=True)
    along = jnp.zeros((ROWS, 1), F32)
    for h in range(NC):
        part = s_ref[h][:ROWS, :WA_]
        cols = slice(h * WA_, (h + 1) * WA_)
        gq_ref[:, cols] = part * gain
        along += jnp.sum(part * wq_ref[:, cols].astype(F32), axis=1, keepdims=True)
        gw_ref[:, h * WB_:(h + 1) * WB_] = s_ref[h][:ROWS, WA_:]
    gg_ref[...] = jnp.sum(
        jnp.where(eye, jnp.broadcast_to(along, (ROWS, ROWS)), 0.0), axis=0, keepdims=True)
    for cp in moves:
        cp.wait()


def block_step(tokens, segment_ids, grad_out, norm_gain, w_qkv, w_out):
    any_, vm = pl.BlockSpec(memory_space=pl.ANY), pl.BlockSpec(memory_space=pltpu.VMEM)
    hbm = pl.BlockSpec(memory_space=pltpu.HBM)
    v = pltpu.VMEM
    gain = norm_gain.reshape(1, ROWS)
    out, grad_tokens, sums = pl.pallas_call(
        kernel,
        out_shape=(
            pltpu.VMEM((T, D), BF),
            pltpu.VMEM((T, D), BF),
            pltpu.VMEM((NC, PAD, WX), F32),
        ),
        in_specs=[hbm] * 6,
        out_specs=(vm, vm, vm),
        scratch_shapes=[
            v((1, T), jnp.int32), v((1, ROWS), BF), v((ROWS, NC * WA_), BF), v((ROWS, NC * WB_), BF),
            v((NY, T, CH), BF), v((NY, T, CH), BF), v((NY, T, CH), BF),
            v((NY, CH, T), BF), v((NY, CH, T), BF), v((T, 128), F32),
            v((NC, PAD, WX), BF), v((GROUP, PAD, WX), BF), v((BLK, WX), F32),
            v((NC, NY, CH, WA_), BF), v((NC, NY, CH, WB_), BF),
            v((NC, T, WA_), F32), v((3, 512, HD), BF), v((T, T), F32),
            v((T, HD), F32), v((T, HD), F32),
            v((3, 512, HD), BF), v((T, HD), BF), v((T, HD), BF), v((3, 512, T), BF),
            v((NC, T, WB_), BF), v((NC, T, WA_), BF), v((NY, T, CH), F32),
            v((NY, CH, WA_), BF), v((NY, CH, WA_), BF), v((NY, CH, WA_), BF),
            v((NZ, BLK, W1), BF), v((2, NZ, BLK, W1), BF), v((7, BLK, W1), BF),
            v((2, 2, 4, 2, BLK, W2), BF), v((NY - 1, BLK, W2), BF),
            v((NY, CH, WB_), BF), v((NY, CH, WB_), BF), v((NY, CH, WB_), BF),
            v((3, CH, WB_), BF), v((NZ - 1, BLK, WB_), BF),
            v((BLK + PAD, WA_), F32), v((BLK + PAD, WB_), F32),
            v((GROUP, PAD, WA_), BF), v((GROUP, PAD, WA_), BF),
            v((GROUP, PAD, WB_), BF), v((GROUP, PAD, WB_), BF),
            pltpu.SemaphoreType.DMA((2 * NY + 4,)),
            pltpu.SemaphoreType.DMA((N_COPIES,)), pltpu.SemaphoreType.DMA((N_COPIES,)),
            pltpu.SemaphoreType.DMA((2 * GROUP,)),
        ],
        compiler_params=pltpu.CompilerParams(
            collective_id=0, has_side_effects=True, vmem_limit_bytes=55 * 2 ** 20),
        name="block_step",
    )(tokens, grad_out, segment_ids, gain, w_qkv, w_out.T)
    out, grad_tokens, grad_qkv, grad_wout, grad_gain = pl.pallas_call(
        finish_kernel,
        out_shape=(
            jax.ShapeDtypeStruct((T, D), BF),
            jax.ShapeDtypeStruct((T, D), BF),
            jax.ShapeDtypeStruct((ROWS, NC * WA_), F32),
            jax.ShapeDtypeStruct((ROWS, NC * WB_), F32),
            jax.ShapeDtypeStruct((1, ROWS), F32),
        ),
        in_specs=[vm, vm, vm, vm, vm],
        out_specs=(any_, any_, vm, vm, vm),
        scratch_shapes=[pltpu.SemaphoreType.DMA((8,))],
        compiler_params=pltpu.CompilerParams(vmem_limit_bytes=8 * 2 ** 20),
        name="finish",
    )(out, grad_tokens, sums, gain, w_qkv)
    return out, grad_tokens, grad_qkv, grad_wout.T, grad_gain.reshape(ROWS)


def solution(mesh):
    return jax.shard_map(
        block_step,
        mesh=mesh,
        in_specs=(P("dp", None), P("dp", None), P("dp", None), P("dp"), P("dp", None),
                  P(None, "dp")),
        out_specs=(P("dp", None), P("dp", None), P("dp", None), P(None, "dp"), P("dp")),
        check_vma=False,
    )
```

```python
import math

import jax
import jax.numpy as jnp
from jax import lax
from jax.experimental import pallas as pl
from jax.experimental.pallas import tpu as pltpu
from jax.sharding import PartitionSpec as P

NY, NZ, NX, NC = 4, 8, 4, 2
D, T, HD = 2560, 384, 128
ROWS = 10
GROUP = NX * NC
BLK = GROUP * ROWS
CH = NZ * BLK
WA_, WB_ = 384, 256
WX = WA_ + WB_
W1, W2 = 256, 128
PAD = 16
EPS = 1e-06
LOG_BASE = math.log(1000000.0)
N_COPIES = 256
BF, F32 = jnp.bfloat16, jnp.float32
NT = (((1,), (1,)), ((), ()))
TN = (((0,), (0,)), ((), ()))


def mm(a, b, dims=(((1,), (0,)), ((), ()))):
    return lax.dot_general(a, b, dims, preferred_element_type=F32)


def rms(x):
    return lax.rsqrt(jnp.mean(x * x, axis=-1, keepdims=True) + EPS)


def kernel(
    tok_hbm, go_hbm, seg_hbm, gain_hbm, wq_hbm, wo_hbm,
    out_ref, gt_ref, s_ref,
    seg_ref, gain_ref, wq_ref, wo_ref,
    tok, go, sc, scT, goT, rr, blk, xg, tmp, wa, wb, proj, gm, mask, cs, sn,
    qb, kb, kv, pb, mx, dpr, dots,
    ta, sa, ra, ya1, ya2, za, zc, yc, tb, sb, rb, xb, zb, fin, finb, xs, xr, xsb, xrb,
    lsem, ssem, rsem, fsem,
):
    idx = lax.axis_index("dp")
    me8 = lax.rem(idx, GROUP)
    base = idx - me8
    c = lax.rem(idx, 2)
    o = 1 - c
    xi = lax.div(me8, 2)
    yz = lax.div(idx, GROUP)
    z = lax.rem(yz, NZ)
    y = lax.div(yz, NZ)

    def ym(k):
        return lax.rem(y + (k + NY), NY)

    def zm(k):
        return lax.rem(z + (k + NZ), NZ)

    def dev(yy, zz):
        return (yy * NZ + zz) * GROUP + me8

    def xdev(k):
        return base + lax.rem(me8 + 2 * k, GROUP)

    right_y, left_y = dev(ym(1), z), dev(ym(-1), z)
    right_z, left_z = dev(y, zm(1)), dev(y, zm(-1))
    partner = idx + 1 - 2 * c

    def rows(zz):
        return pl.ds(pl.multiple_of(zz * BLK, 16), BLK)

    copies = []

    def send(src, dst, target):
        n = len(copies)
        copy = pltpu.make_async_remote_copy(
            src_ref=src, dst_ref=dst, send_sem=ssem.at[n], recv_sem=rsem.at[n],
            device_id=(target,), device_id_type=pl.DeviceIdType.MESH,
        )
        copy.start()
        copies.append(copy)
        return copy

    small = []
    for i, (src, dst) in enumerate(
            ((gain_hbm, gain_ref), (wq_hbm, wq_ref), (wo_hbm, wo_ref), (seg_hbm, seg_ref))):
        cp = pltpu.make_async_copy(src, dst, lsem.at[2 * NY + i])
        cp.start()
        small.append(cp)

    barrier = pltpu.get_barrier_semaphore()

    def greet(d):
        pl.semaphore_signal(barrier, inc=1, device_id=(d,), device_id_type=pl.DeviceIdType.MESH)

    greetings = [base + lax.rem(me8 + p, GROUP) for p in range(1, GROUP)]
    greetings += [dev(ym(k), z) for k in range(1, NY)]
    greetings += [dev(y, zm(k)) for k in range(1, NZ)]
    for k in range(NY):
        for core in (c, o):
            if k > 0 or core is o:
                greetings.append((ym(k) * NZ + z) * GROUP + 2 * y + core)
    for d in greetings:
        greet(d)

    @pl.when(y != xi)
    def _():
        greet((y * NZ + z) * GROUP + 2 * y + c)

    loads = []
    for i, (src, dst) in enumerate(((tok_hbm, tok), (go_hbm, go))):
        for j in range(NY):
            cp = pltpu.make_async_copy(
                src.at[:, pl.ds(j * CH, CH)], dst.at[j], lsem.at[i * NY + j])
            cp.start()
            loads.append(cp)

    for cp in small:
        cp.wait()
    diag = lax.broadcasted_iota(jnp.int32, (PAD, ROWS), 0) == lax.broadcasted_iota(
        jnp.int32, (PAD, ROWS), 1)
    gain_diag = jnp.where(diag, jnp.broadcast_to(gain_ref[...].astype(F32), (PAD, ROWS)), 0.0)
    gw = mm(gain_diag.astype(BF), wq_ref[...]).astype(BF)
    wt = mm(diag.astype(F32).astype(BF), wo_ref[...]).astype(BF)
    for h in range(NC):
        blk[h, :, :WA_] = gw[:, h * WA_:(h + 1) * WA_]
        blk[h, :, WA_:] = wt[:, h * WB_:(h + 1) * WB_]

    pl.semaphore_wait(barrier, jnp.where(y == xi, len(greetings), len(greetings) + 1))

    xcop = []
    for p in range(1, GROUP):
        t = lax.rem(me8 + p, GROUP)
        xcop.append(send(blk.at[lax.rem(t, 2)], xg.at[me8], base + t))
    xg[me8] = blk[c]

    for j in range(NY):
        loads[j].wait()

    def scale_rows(i, _):
        r0 = pl.ds(pl.multiple_of(i * 16, 16), 16)
        parts = [tok[j, r0, :].astype(F32) for j in range(NY)]
        total = sum(jnp.sum(p * p, axis=-1, keepdims=True) for p in parts)
        r = lax.rsqrt(total * (1.0 / D) + EPS)
        rr[r0, :] = jnp.broadcast_to(r, (16, 128))
        for j in range(NY):
            sc[j, r0, :] = (parts[j] * r).astype(BF)
        return 0

    lax.fori_loop(0, T // 16, scale_rows, 0, unroll=2)

    for cp in xcop:
        cp.wait_recv()
    for i in range(GROUP):
        tmp[i * ROWS:(i + 1) * ROWS, :] = xg[i].astype(F32)[:ROWS, :]
    wa[c, y, rows(z), :] = tmp[:, :WA_].astype(BF)
    wb[c, y, rows(z), :] = tmp[:, WA_:].astype(BF)

    def ablk(yy, zz):
        return wa.at[c, yy, rows(zz), :]

    def bblk(yy, zz):
        return wb.at[c, yy, rows(zz), :]

    offs = [0, -1, 1, -2, 2, -3, 3, -4]
    za_r, za_l, ya_r, ya_l, ya_f, zb_c, xb_c = {}, {}, {}, {}, {}, {}, []

    def zA(s):
        za_r[s] = send(ablk(y, zm(1 - s)), ablk(y, zm(1 - s)), right_z)
        if s < 4:
            za_l[s] = send(ablk(y, zm(s - 1)), ablk(y, zm(s - 1)), left_z)

    def zA_wait(s):
        za_r[s].wait_recv()
        if s < 4:
            za_l[s].wait_recv()

    def yA(j):
        b = ablk(y, zm(offs[j]))
        ya_r[j] = send(b, b, right_y)
        ya_l[j] = send(b, b, left_y)

    def yA_forward(j):
        ya_r[j].wait_recv()
        ya_l[j].wait_recv()
        if j % 2 == 0:
            b = ablk(ym(-1), zm(offs[j]))
            ya_f[j] = send(b, b, right_y)
        else:
            b = ablk(ym(1), zm(offs[j]))
            ya_f[j] = send(b, b, left_y)

    def zB(k):
        b = bblk(xi, z)
        zb_c[k] = send(b, b, dev(y, zm(k)))

    def xB(k):
        zb_c[k].wait_recv()
        b = bblk(xi, zm(-k))
        for m in (1, 3, 2):
            xb_c.append((m, send(b, b, xdev(m))))

    def transpose(src, dst, j):
        for k in range(CH // 128):
            piece = src[j, :, k * 128:(k + 1) * 128].astype(F32)
            dst[j, k * 128:(k + 1) * 128, :] = piece.T.astype(BF)

    zA(1)
    b = bblk(y, z)
    yb_c = [send(b, b, dev(ym(k), z)) for k in (1, 3, 2)]
    yA(0)

    seg = seg_ref[...].astype(F32)
    row_i = lax.broadcasted_iota(jnp.int32, (T, T), 0)
    col_i = lax.broadcasted_iota(jnp.int32, (T, T), 1)
    seg_s = jnp.broadcast_to(seg, (T, T))
    seg_t = jnp.sum(jnp.where(row_i == col_i, seg_s, 0.0), axis=1, keepdims=True)
    first = jnp.sum(jnp.where(seg_s < seg_t, 1.0, 0.0), axis=1, keepdims=True)
    mask[...] = jnp.where((seg_s == seg_t) & (col_i <= row_i), 1.0, 0.0)
    lane = lax.broadcasted_iota(jnp.int32, (T, HD), 1)
    place = lax.broadcasted_iota(jnp.int32, (T, HD), 0).astype(F32)
    inverse = jnp.exp(lax.rem(lane, HD // 2).astype(F32) * (-2.0 * LOG_BASE / HD))
    angles = (place - first) * inverse
    cs[...] = jnp.cos(angles)
    sn[...] = jnp.where(lane < HD // 2, -1.0, 1.0) * jnp.sin(angles)

    zA_wait(1)
    zA(2)
    yA(1)
    yA(2)
    for cp in yb_c:
        cp.wait_recv()
    zB(1)
    zB(7)
    yA_forward(0)
    transpose(sc, scT, 0)
    zA_wait(2)
    zA(3)
    yA(3)
    yA(4)
    zB(2)
    zB(6)
    yA_forward(1)
    yA_forward(2)
    transpose(sc, scT, 1)
    zA_wait(3)
    zA(4)
    yA(5)
    yA(6)
    zB(3)
    zB(5)
    zB(4)
    xB(1)
    xB(7)
    yA_forward(3)
    yA_forward(4)
    transpose(sc, scT, 2)
    zA_wait(4)
    yA(7)
    pa_own = send(wa.at[c, y], wa.at[c, y], partner)
    xB(2)
    xB(6)
    transpose(sc, scT, 3)
    yA_forward(5)
    xB(3)
    xB(5)
    yA_forward(6)
    for j in range(NY):
        loads[NY + j].wait()
    transpose(go, goT, 0)
    transpose(go, goT, 1)
    xB(4)
    yA_forward(7)
    pa_l = send(wa.at[c, ym(-1)], wa.at[c, ym(-1)], partner)
    pa_r = send(wa.at[c, ym(1)], wa.at[c, ym(1)], partner)
    pb_s = [send(wb.at[c, xi], wb.at[c, xi], partner)]
    transpose(go, goT, 2)
    transpose(go, goT, 3)

    def project(yy, first_one=False):
        left = sc[yy]
        for h in range(NC):
            part = mm(left, wa[h, yy])
            proj[h] = part if first_one else proj[h] + part

    pa_own.wait_recv()
    project(y, True)
    pa_f = []

    def last_chunk(j):
        ya_f[j].wait_recv()
        b = ablk(ym(2), zm(offs[j]))
        pa_f.append(send(b, b, partner))

    for j in range(4):
        last_chunk(j)
    pa_l.wait_recv()
    project(ym(-1))
    last_chunk(4)
    last_chunk(5)
    pa_r.wait_recv()
    project(ym(1))
    last_chunk(6)
    last_chunk(7)
    for cp in pa_f:
        cp.wait_recv()
    project(ym(2))

    def head_cols(h):
        return h // 3, (h % 3) * HD

    def turn(v):
        return v * cs[...] + pltpu.roll(v, HD // 2, 1) * sn[...]

    def four(block):
        return jnp.concatenate([block] * 4, axis=0)

    for h in range(5):
        hf, col = head_cols(h)
        v = proj[hf, :, col:col + HD]
        t = turn(v * rms(v)).astype(BF)
        if h == 4:
            kb[...] = t
        else:
            for i in range(3):
                qb[i, h * 128:(h + 1) * 128, :] = t[i * 128:(i + 1) * 128]
    kv[...] = proj[1, :, 2 * HD:].astype(BF)
    scale = HD ** -0.5
    for i in range(3):
        r0, n = slice(i * 128, (i + 1) * 128), (i + 1) * 128
        w = jnp.exp(mm(qb[i], kb[:n, :], NT) * scale) * four(mask[r0, :n])
        p = (w * (1.0 / jnp.sum(w, axis=-1, keepdims=True))).astype(BF)
        pb[i, :, :n] = p
        mixed = mm(p, kv[:n, :]).astype(BF)
        for h in range(4):
            mx[h // 2, r0, (h % 2) * HD:(h % 2 + 1) * HD] = mixed[h * 128:(h + 1) * 128]
        if i == 1:
            for m in (1, 3, 2):
                for mm_, cp in xb_c:
                    if mm_ == m:
                        cp.wait_recv()
                b = wb.at[c, lax.rem(xi + NX - m, NX)]
                pb_s.append(send(b, b, partner))

    def add_into(ref, *others):
        total = ref[...].astype(F32)
        for other in others:
            total = total + other[...].astype(F32)
        ref[...] = total.astype(BF)

    rb_s = []
    for j in range(NY):
        sb[j] = mm(goT[j], mx[o]).astype(BF)
        rb_s.append(send(sb.at[j], rb.at[j], partner))
    for j in range(NY):
        tb[j] = mm(goT[j], mx[c]).astype(BF)
    for j in range(NY):
        rb_s[j].wait_recv()
        add_into(tb.at[j], rb.at[j])

    xb_s = []
    for q in range(2):
        cols = pl.ds(q * W2, W2)
        for m in (1, 3, 2):
            t = lax.rem(xi + m, NX)
            xb_s.append(send(tb.at[t, :, cols], xb.at[m - 1, :, cols], xdev(m)))
    for cp in pb_s:
        cp.wait_recv()
    for h in range(NC):
        part = sum(mm(go[j], wb[h, j]) for j in range(NY)).astype(BF)
        for i in range(3):
            for k in range(2):
                gm[i, (2 * h + k) * 128:(2 * h + k + 1) * 128, :] = (
                    part[i * 128:(i + 1) * 128, k * HD:(k + 1) * HD])

    def norm_back(v, d, cos, sin):
        r = rms(v)
        xn = v * r
        dn = d * cos + pltpu.roll(d * sin, HD // 2, 1)
        return (r * (dn - xn * jnp.mean(dn * xn, axis=-1, keepdims=True))).astype(BF)

    dk = [jnp.zeros((128, HD), F32)] * 3
    dv = [jnp.zeros((128, HD), F32)] * 3
    for i in range(3):
        r0, n = slice(i * 128, (i + 1) * 128), (i + 1) * 128
        do = gm[i]
        p = pb[i, :, :n]
        pf = p.astype(F32)
        dp = mm(do, kv[:n, :], NT)
        delta = jnp.sum(pf * dp, axis=-1, keepdims=True)
        ds = (pf * (dp - delta) * scale).astype(BF)
        tk = mm(ds, qb[i], TN)
        tv = mm(p, do, TN)
        for m in range(i + 1):
            dk[m] = dk[m] + tk[m * 128:(m + 1) * 128]
            dv[m] = dv[m] + tv[m * 128:(m + 1) * 128]
        v = jnp.concatenate(
            [proj[h // 3, r0, (h % 3) * HD:(h % 3 + 1) * HD] for h in range(4)], axis=0)
        grad = norm_back(v, mm(ds, kb[:n, :]), four(cs[r0, :]), four(sn[r0, :]))
        for h in range(4):
            dpr[h // 3, r0, (h % 3) * HD:(h % 3 + 1) * HD] = grad[h * 128:(h + 1) * 128]
    dpr[1, :, HD:2 * HD] = norm_back(
        proj[1, :, HD:2 * HD], jnp.concatenate(dk, axis=0), cs[...], sn[...])
    dpr[1, :, 2 * HD:] = jnp.concatenate(dv, axis=0).astype(BF)

    ra_s = {}

    def partial(k):
        yy = ym(k)
        sa[yy] = mm(scT[yy], dpr[o]).astype(BF)
        ra_s[k] = send(sa.at[yy], ra.at[yy], partner)
        ta[yy] = mm(scT[yy], dpr[c]).astype(BF)

    roffs = [4, 3, -3, 2, -2, 1, -1, 0]

    def tblk(yy, j):
        return ta.at[yy, rows(zm(roffs[j])), pl.ds(0, W1)]

    def thalf(h, k):
        return ta.at[pl.ds(2 * h, 2), rows(zm(k)), pl.ds(W1, W2)]

    s1, s2r, s2l, sz, zc_s = {}, {}, {}, {}, {}
    partial(2)
    partial(1)
    ra_s[2].wait_recv()
    for j in range(8):
        b = rows(zm(roffs[j]))
        add_into(ta.at[ym(2), b, :], ra.at[ym(2), b, :])
        s1[j] = send(tblk(ym(2), j), ya1.at[j], right_y if j % 2 == 0 else left_y)
    partial(3)
    partial(0)
    for k in (1, 3, 0):
        ra_s[k].wait_recv()
        add_into(ta.at[ym(k)], ra.at[ym(k)])

    def zc_send(side, h, s):
        zc_s[side, h, s] = send(
            thalf(h, -s if side else s), zc.at[side, h, s - 1], left_z if side else right_z)

    def zc_add(side, h, s):
        zc_s[side, h, s + 1].wait_recv()
        add_into(thalf(h, -s if side else s), zc.at[side, h, s])

    def zc_round(n):
        for side, h, s in ((0, 0, 4 - n), (1, 1, 4 - n), (0, 1, 3 - n), (1, 0, 3 - n)):
            if s > 0:
                zc_add(side, h, s)
                zc_send(side, h, s)

    def zc_end():
        for h in range(2):
            for side in range(2):
                zc_s[side, h, 1].wait_recv()
            add_into(thalf(h, 0), zc.at[0, h, 0], zc.at[1, h, 0])
        return [
            send(ta.at[ym(k), rows(z), pl.ds(W1, W2)], yc.at[k - 1], dev(ym(k), z))
            for k in (2, 1, 3)]

    zc_send(0, 0, 4)
    zc_send(1, 1, 4)
    zc_send(0, 1, 3)
    zc_send(1, 0, 3)

    def step2(j):
        s1[j].wait_recv()
        add_into(tblk(ym(1) if j % 2 == 0 else ym(3), j), ya1.at[j])
        s2r[j] = send(tblk(ym(1), j), ya2.at[0, j], right_y)
        s2l[j] = send(tblk(ym(3), j), ya2.at[1, j], left_y)

    def step3(j):
        s2r[j].wait_recv()
        s2l[j].wait_recv()
        add_into(tblk(y, j), ya2.at[0, j], ya2.at[1, j])

    def step_z(j):
        if j == 0:
            sz[0] = send(tblk(y, 0), za.at[0], right_z)
        elif j == 7:
            return
        elif j % 2 == 1:
            n = (j + 1) // 2
            sz[n - 1].wait_recv()
            add_into(tblk(y, j), za.at[n - 1])
            sz[n] = send(tblk(y, j), za.at[n], right_z)
        else:
            n = 3 + j // 2
            if n > 4:
                sz[n - 1].wait_recv()
                add_into(tblk(y, j), za.at[n - 1])
            sz[n] = send(tblk(y, j), za.at[n], left_z)

    def out_chunk(j):
        update = sum(mm(mx[h], wb[h, j], NT) for h in range(NC))
        out_ref[:, j * CH:(j + 1) * CH] = (tok[j].astype(F32) + update).astype(BF)

    def row_dots():
        total = sum(
            jnp.sum(dpr[h].astype(F32) * proj[h], axis=-1, keepdims=True) for h in range(NC))
        dots[...] = jnp.broadcast_to(total * (1.0 / D), (T, 128))

    def gt_chunk(j):
        r = rr[...][:, :1]
        g = sum(mm(dpr[h], wa[h, j], NT) for h in range(NC))
        path = (r * (g - tok[j].astype(F32) * (r * dots[...][:, :1]))).astype(BF)
        gt_ref[:, j * CH:(j + 1) * CH] = (
            go[j].astype(F32) + path.astype(F32)).astype(BF)

    zb_s = []

    def sum_x(q):
        cols = pl.ds(q * W2, W2)
        for cp in xb_s[3 * q:3 * q + 3]:
            cp.wait_recv()
        add_into(tb.at[xi, :, cols], *[xb.at[m, :, cols] for m in range(3)])
        for k in (4, 3, 5, 2, 6, 1, 7):
            zb_s.append(send(
                tb.at[xi, rows(zm(k)), cols], zb.at[k - 1, :, cols], dev(y, zm(k))))

    def piece_copy(p):
        t = lax.rem(me8 + p, GROUP)
        return pltpu.make_async_remote_copy(
            src_ref=xsb.at[t], dst_ref=xrb.at[2 * y + c],
            send_sem=fsem.at[p], recv_sem=fsem.at[GROUP + 2 * y + c],
            device_id=((xi * NZ + z) * GROUP + t,), device_id_type=pl.DeviceIdType.MESH,
        )

    def self_copy():
        return pltpu.make_async_copy(
            xsb.at[me8], xrb.at[2 * y + c], fsem.at[GROUP + 2 * y + c])

    def sum_z():
        for cp in zb_s:
            cp.wait_recv()
        finb[:BLK, :] = tb[xi, rows(z), :].astype(F32) + sum(
            zb[k].astype(F32) for k in range(NZ - 1))
        finb[BLK:, :] = jnp.zeros((PAD, WB_), F32)
        for i in range(GROUP):
            xsb[i] = finb[i * ROWS:i * ROWS + PAD, :].astype(BF)
        for p in range(1, GROUP):
            piece_copy(p).start()

        @pl.when(y != xi)
        def _():
            piece_copy(0).start()

        @pl.when(y == xi)
        def _():
            self_copy().start()

    row_dots()
    out_chunk(0)
    out_chunk(1)
    step2(0)
    step2(1)
    zc_round(1)
    sum_x(0)
    out_chunk(2)
    step2(2)
    step2(3)
    out_chunk(3)
    zc_round(2)
    step2(4)
    step2(5)
    gt_chunk(0)
    step2(6)
    step2(7)
    zc_round(3)
    gt_chunk(1)
    step3(0)
    step_z(0)
    gt_chunk(2)
    yc_s = zc_end()
    sum_x(1)
    step3(1)
    step3(2)
    step_z(1)
    step_z(2)
    gt_chunk(3)
    step3(3)
    step3(4)
    step_z(3)
    step_z(4)

    step3(5)
    step3(6)
    step_z(5)
    step_z(6)
    step3(7)
    sum_z()
    for cp in yc_s:
        cp.wait_recv()
    fin[:BLK, W1:] = ta[y, rows(z), W1:].astype(F32) + sum(
        yc[k].astype(F32) for k in range(NY - 1))
    sz[3].wait_recv()
    sz[6].wait_recv()
    fin[:BLK, :W1] = (
        tblk(y, 7)[...].astype(F32) + za[3].astype(F32) + za[6].astype(F32))
    fin[BLK:, :] = jnp.zeros((PAD, WA_), F32)

    for i in range(GROUP):
        xs[i] = fin[i * ROWS:i * ROWS + PAD, :].astype(BF)
    last = []
    for p in range(1, GROUP):
        t = lax.rem(me8 + p, GROUP)
        last.append(send(xs.at[t], xr.at[me8], base + t))
    xr[me8] = xs[me8]
    for i in range(GROUP):
        pltpu.make_async_copy(xsb.at[i], xrb.at[i], fsem.at[GROUP + i]).wait()
    for h in range(NC):
        s_ref[h, :, WA_:] = sum(xrb[2 * i + h].astype(F32) for i in range(NY))
    for cp in copies[:-len(last)]:
        cp.wait_send()
    for p in range(1, GROUP):
        piece_copy(p).wait_send()

    @pl.when(y != xi)
    def _():
        piece_copy(0).wait_send()

    for cp in last:
        cp.wait_recv()
    for h in range(NC):
        s_ref[h, :, :WA_] = sum(xr[2 * i + h].astype(F32) for i in range(NX))
    for cp in last:
        cp.wait_send()


def finish_kernel(out_in, gt_in, s_ref, gain_ref, wq_ref, out_hbm, gt_hbm, gq_ref, gw_ref, gg_ref, sem):
    moves = []
    for i, (src, dst) in enumerate(((out_in, out_hbm), (gt_in, gt_hbm))):
        for j in range(4):
            part = pl.ds(j * (T // 4), T // 4)
            cp = pltpu.make_async_copy(src.at[part, :], dst.at[part, :], sem.at[4 * i + j])
            cp.start()
            moves.append(cp)
    eye = lax.broadcasted_iota(jnp.int32, (ROWS, ROWS), 0) == lax.broadcasted_iota(
        jnp.int32, (ROWS, ROWS), 1)
    gain = jnp.sum(
        jnp.where(eye, jnp.broadcast_to(gain_ref[...].astype(F32), (ROWS, ROWS)), 0.0),
        axis=1, keepdims=True)
    along = jnp.zeros((ROWS, 1), F32)
    for h in range(NC):
        part = s_ref[h][:ROWS, :WA_]
        cols = slice(h * WA_, (h + 1) * WA_)
        gq_ref[:, cols] = part * gain
        along += jnp.sum(part * wq_ref[:, cols].astype(F32), axis=1, keepdims=True)
        gw_ref[:, h * WB_:(h + 1) * WB_] = s_ref[h][:ROWS, WA_:]
    gg_ref[...] = jnp.sum(
        jnp.where(eye, jnp.broadcast_to(along, (ROWS, ROWS)), 0.0), axis=0, keepdims=True)
    for cp in moves:
        cp.wait()


def block_step(tokens, segment_ids, grad_out, norm_gain, w_qkv, w_out):
    any_, vm = pl.BlockSpec(memory_space=pl.ANY), pl.BlockSpec(memory_space=pltpu.VMEM)
    hbm = pl.BlockSpec(memory_space=pltpu.HBM)
    v = pltpu.VMEM
    gain = norm_gain.reshape(1, ROWS)
    out, grad_tokens, sums = pl.pallas_call(
        kernel,
        out_shape=(
            pltpu.VMEM((T, D), BF),
            pltpu.VMEM((T, D), BF),
            pltpu.VMEM((NC, PAD, WX), F32),
        ),
        in_specs=[hbm] * 6,
        out_specs=(vm, vm, vm),
        scratch_shapes=[
            v((1, T), jnp.int32), v((1, ROWS), BF), v((ROWS, NC * WA_), BF), v((ROWS, NC * WB_), BF),
            v((NY, T, CH), BF), v((NY, T, CH), BF), v((NY, T, CH), BF),
            v((NY, CH, T), BF), v((NY, CH, T), BF), v((T, 128), F32),
            v((NC, PAD, WX), BF), v((GROUP, PAD, WX), BF), v((BLK, WX), F32),
            v((NC, NY, CH, WA_), BF), v((NC, NY, CH, WB_), BF),
            v((NC, T, WA_), F32), v((3, 512, HD), BF), v((T, T), F32),
            v((T, HD), F32), v((T, HD), F32),
            v((3, 512, HD), BF), v((T, HD), BF), v((T, HD), BF), v((3, 512, T), BF),
            v((NC, T, WB_), BF), v((NC, T, WA_), BF), v((T, 128), F32),
            v((NY, CH, WA_), BF), v((NY, CH, WA_), BF), v((NY, CH, WA_), BF),
            v((NZ, BLK, W1), BF), v((2, NZ, BLK, W1), BF), v((7, BLK, W1), BF),
            v((2, 2, 4, 2, BLK, W2), BF), v((NY - 1, BLK, W2), BF),
            v((NY, CH, WB_), BF), v((NY, CH, WB_), BF), v((NY, CH, WB_), BF),
            v((3, CH, WB_), BF), v((NZ - 1, BLK, WB_), BF),
            v((BLK + PAD, WA_), F32), v((BLK + PAD, WB_), F32),
            v((GROUP, PAD, WA_), BF), v((GROUP, PAD, WA_), BF),
            v((GROUP, PAD, WB_), BF), v((GROUP, PAD, WB_), BF),
            pltpu.SemaphoreType.DMA((2 * NY + 4,)),
            pltpu.SemaphoreType.DMA((N_COPIES,)), pltpu.SemaphoreType.DMA((N_COPIES,)),
            pltpu.SemaphoreType.DMA((2 * GROUP,)),
        ],
        compiler_params=pltpu.CompilerParams(
            collective_id=0, has_side_effects=True, vmem_limit_bytes=55 * 2 ** 20),
        name="block_step",
    )(tokens, grad_out, segment_ids, gain, w_qkv, w_out.T)
    out, grad_tokens, grad_qkv, grad_wout, grad_gain = pl.pallas_call(
        finish_kernel,
        out_shape=(
            jax.ShapeDtypeStruct((T, D), BF),
            jax.ShapeDtypeStruct((T, D), BF),
            jax.ShapeDtypeStruct((ROWS, NC * WA_), F32),
            jax.ShapeDtypeStruct((ROWS, NC * WB_), F32),
            jax.ShapeDtypeStruct((1, ROWS), F32),
        ),
        in_specs=[vm, vm, vm, vm, vm],
        out_specs=(any_, any_, vm, vm, vm),
        scratch_shapes=[pltpu.SemaphoreType.DMA((8,))],
        compiler_params=pltpu.CompilerParams(vmem_limit_bytes=8 * 2 ** 20),
        name="finish",
    )(out, grad_tokens, sums, gain, w_qkv)
    return out, grad_tokens, grad_qkv, grad_wout.T, grad_gain.reshape(ROWS)


def solution(mesh):
    return jax.shard_map(
        block_step,
        mesh=mesh,
        in_specs=(P("dp", None), P("dp", None), P("dp", None), P("dp"), P("dp", None),
                  P(None, "dp")),
        out_specs=(P("dp", None), P("dp", None), P("dp", None), P(None, "dp"), P("dp")),
        check_vma=False,
    )
```

```python
import math

import jax
import jax.numpy as jnp
from jax import lax
from jax.experimental import pallas as pl
from jax.experimental.pallas import tpu as pltpu
from jax.sharding import PartitionSpec as P

NY, NZ, NX, NC = 4, 8, 4, 2
D, T, HD = 2560, 384, 128
ROWS = 10
GROUP = NX * NC
BLK = GROUP * ROWS
CH = NZ * BLK
WA_, WB_ = 384, 256
WX = WA_ + WB_
W2 = 128
PAD = 16
EPS = 1e-06
LOG_BASE = math.log(1000000.0)
N_COPIES = 256
BF, F32 = jnp.bfloat16, jnp.float32
NT = (((1,), (1,)), ((), ()))
TN = (((0,), (0,)), ((), ()))


def mm(a, b, dims=(((1,), (0,)), ((), ()))):
    return lax.dot_general(a, b, dims, preferred_element_type=F32)


def rms(x):
    return lax.rsqrt(jnp.mean(x * x, axis=-1, keepdims=True) + EPS)


def kernel(
    tok_hbm, go_hbm, seg_hbm, gain_hbm, wq_hbm, wo_hbm,
    out_ref, gt_ref, s_ref,
    seg_ref, gain_ref, wq_ref, wo_ref,
    tok, go, sc, scT, goT, rr, blk, xg, tmp, wa, wb, proj, gm, mask, cs, sn,
    qb, kb, kv, pb, mx, dpr, dots,
    ta, sa, ra, ya1, ya2, za, tb, sb, rb, xb, zb, fin, finb, xs, xr, xsb, xrb,
    lsem, ssem, rsem, fsem,
):
    idx = lax.axis_index("dp")
    me8 = lax.rem(idx, GROUP)
    base = idx - me8
    c = lax.rem(idx, 2)
    o = 1 - c
    xi = lax.div(me8, 2)
    yz = lax.div(idx, GROUP)
    z = lax.rem(yz, NZ)
    y = lax.div(yz, NZ)

    def ym(k):
        return lax.rem(y + (k + NY), NY)

    def zm(k):
        return lax.rem(z + (k + NZ), NZ)

    def dev(yy, zz):
        return (yy * NZ + zz) * GROUP + me8

    def xdev(k):
        return base + lax.rem(me8 + 2 * k, GROUP)

    right_y, left_y = dev(ym(1), z), dev(ym(-1), z)
    right_z, left_z = dev(y, zm(1)), dev(y, zm(-1))
    partner = idx + 1 - 2 * c

    def rows(zz):
        return pl.ds(pl.multiple_of(zz * BLK, 16), BLK)

    copies = []

    def send(src, dst, target):
        n = len(copies)
        copy = pltpu.make_async_remote_copy(
            src_ref=src, dst_ref=dst, send_sem=ssem.at[n], recv_sem=rsem.at[n],
            device_id=(target,), device_id_type=pl.DeviceIdType.MESH,
        )
        copy.start()
        copies.append(copy)
        return copy

    small = []
    for i, (src, dst) in enumerate(
            ((gain_hbm, gain_ref), (wq_hbm, wq_ref), (wo_hbm, wo_ref), (seg_hbm, seg_ref))):
        cp = pltpu.make_async_copy(src, dst, lsem.at[2 * NY + i])
        cp.start()
        small.append(cp)

    barrier = pltpu.get_barrier_semaphore()

    def greet(d):
        pl.semaphore_signal(barrier, inc=1, device_id=(d,), device_id_type=pl.DeviceIdType.MESH)

    greetings = [base + lax.rem(me8 + p, GROUP) for p in range(1, GROUP)]
    greetings += [dev(ym(k), z) for k in range(1, NY)]
    greetings += [dev(y, zm(k)) for k in range(1, NZ)]
    for k in range(NY):
        for core in (c, o):
            if k > 0 or core is o:
                greetings.append((ym(k) * NZ + z) * GROUP + 2 * y + core)
    for d in greetings:
        greet(d)

    @pl.when(y != xi)
    def _():
        greet((y * NZ + z) * GROUP + 2 * y + c)

    loads = []
    for i, (src, dst) in enumerate(((tok_hbm, tok), (go_hbm, go))):
        for j in range(NY):
            cp = pltpu.make_async_copy(
                src.at[:, pl.ds(j * CH, CH)], dst.at[j], lsem.at[i * NY + j])
            cp.start()
            loads.append(cp)

    for cp in small:
        cp.wait()
    diag = lax.broadcasted_iota(jnp.int32, (PAD, ROWS), 0) == lax.broadcasted_iota(
        jnp.int32, (PAD, ROWS), 1)
    gain_diag = jnp.where(diag, jnp.broadcast_to(gain_ref[...].astype(F32), (PAD, ROWS)), 0.0)
    gw = mm(gain_diag.astype(BF), wq_ref[...]).astype(BF)
    wt = mm(diag.astype(F32).astype(BF), wo_ref[...]).astype(BF)
    for h in range(NC):
        blk[h, :, :WA_] = gw[:, h * WA_:(h + 1) * WA_]
        blk[h, :, WA_:] = wt[:, h * WB_:(h + 1) * WB_]

    pl.semaphore_wait(barrier, jnp.where(y == xi, len(greetings), len(greetings) + 1))

    xcop = []
    for p in range(1, GROUP):
        t = lax.rem(me8 + p, GROUP)
        xcop.append(send(blk.at[lax.rem(t, 2)], xg.at[me8], base + t))
    xg[me8] = blk[c]

    for j in range(NY):
        loads[j].wait()

    def scale_rows(i, _):
        r0 = pl.ds(pl.multiple_of(i * 16, 16), 16)
        parts = [tok[j, r0, :].astype(F32) for j in range(NY)]
        total = sum(jnp.sum(p * p, axis=-1, keepdims=True) for p in parts)
        r = lax.rsqrt(total * (1.0 / D) + EPS)
        rr[r0, :] = jnp.broadcast_to(r, (16, 128))
        for j in range(NY):
            sc[j, r0, :] = (parts[j] * r).astype(BF)
        return 0

    lax.fori_loop(0, T // 16, scale_rows, 0, unroll=2)

    for cp in xcop:
        cp.wait_recv()
    for i in range(GROUP):
        tmp[i * ROWS:(i + 1) * ROWS, :] = xg[i].astype(F32)[:ROWS, :]
    wa[c, y, rows(z), :] = tmp[:, :WA_].astype(BF)
    wb[c, y, rows(z), :] = tmp[:, WA_:].astype(BF)

    def ablk(yy, zz):
        return wa.at[c, yy, rows(zz), :]

    def bblk(yy, zz):
        return wb.at[c, yy, rows(zz), :]

    offs = [0, -1, 1, -2, 2, -3, 3, -4]
    za_r, za_l, ya_r, ya_l, ya_f, zb_c, xb_c = {}, {}, {}, {}, {}, {}, []

    def zA(s):
        za_r[s] = send(ablk(y, zm(1 - s)), ablk(y, zm(1 - s)), right_z)
        if s < 4:
            za_l[s] = send(ablk(y, zm(s - 1)), ablk(y, zm(s - 1)), left_z)

    def zA_wait(s):
        za_r[s].wait_recv()
        if s < 4:
            za_l[s].wait_recv()

    def yA(j):
        b = ablk(y, zm(offs[j]))
        ya_r[j] = send(b, b, right_y)
        ya_l[j] = send(b, b, left_y)

    def yA_forward(j):
        ya_r[j].wait_recv()
        ya_l[j].wait_recv()
        if j % 2 == 0:
            b = ablk(ym(-1), zm(offs[j]))
            ya_f[j] = send(b, b, right_y)
        else:
            b = ablk(ym(1), zm(offs[j]))
            ya_f[j] = send(b, b, left_y)

    def zB(k):
        b = bblk(xi, z)
        zb_c[k] = send(b, b, dev(y, zm(k)))

    def xB(k):
        zb_c[k].wait_recv()
        b = bblk(xi, zm(-k))
        for m in (1, 3, 2):
            xb_c.append((m, send(b, b, xdev(m))))

    def transpose(src, dst, j):
        for k in range(CH // 128):
            piece = src[j, :, k * 128:(k + 1) * 128].astype(F32)
            dst[j, k * 128:(k + 1) * 128, :] = piece.T.astype(BF)

    zA(1)
    b = bblk(y, z)
    yb_c = [send(b, b, dev(ym(k), z)) for k in (1, 3, 2)]
    yA(0)

    seg = seg_ref[...].astype(F32)
    row_i = lax.broadcasted_iota(jnp.int32, (T, T), 0)
    col_i = lax.broadcasted_iota(jnp.int32, (T, T), 1)
    seg_s = jnp.broadcast_to(seg, (T, T))
    seg_t = jnp.sum(jnp.where(row_i == col_i, seg_s, 0.0), axis=1, keepdims=True)
    first = jnp.sum(jnp.where(seg_s < seg_t, 1.0, 0.0), axis=1, keepdims=True)
    mask[...] = jnp.where((seg_s == seg_t) & (col_i <= row_i), 1.0, 0.0)
    lane = lax.broadcasted_iota(jnp.int32, (T, HD), 1)
    place = lax.broadcasted_iota(jnp.int32, (T, HD), 0).astype(F32)
    inverse = jnp.exp(lax.rem(lane, HD // 2).astype(F32) * (-2.0 * LOG_BASE / HD))
    angles = (place - first) * inverse
    cs[...] = jnp.cos(angles)
    sn[...] = jnp.where(lane < HD // 2, -1.0, 1.0) * jnp.sin(angles)

    zA_wait(1)
    zA(2)
    yA(1)
    yA(2)
    for cp in yb_c:
        cp.wait_recv()
    zB(1)
    zB(7)
    zB(2)
    zB(6)
    yA_forward(0)
    zA_wait(2)
    zA(3)
    yA(3)
    yA(4)
    zB(3)
    zB(5)
    zB(4)
    xB(1)
    xB(7)
    yA_forward(1)
    yA_forward(2)
    transpose(sc, scT, 0)
    zA_wait(3)
    zA(4)
    yA(5)
    yA(6)
    xB(2)
    xB(6)
    yA_forward(3)
    yA_forward(4)
    transpose(sc, scT, 1)
    zA_wait(4)
    yA(7)
    pa_own = send(wa.at[c, y], wa.at[c, y], partner)
    xB(3)
    xB(5)
    transpose(sc, scT, 2)
    yA_forward(5)
    xB(4)
    yA_forward(6)
    transpose(sc, scT, 3)
    for j in range(NY):
        loads[NY + j].wait()
    transpose(go, goT, 0)
    transpose(go, goT, 1)
    yA_forward(7)
    pa_l = send(wa.at[c, ym(-1)], wa.at[c, ym(-1)], partner)
    pa_r = send(wa.at[c, ym(1)], wa.at[c, ym(1)], partner)
    pb_s = [send(wb.at[c, xi], wb.at[c, xi], partner)]
    transpose(go, goT, 2)
    transpose(go, goT, 3)

    def project(yy, first_one=False):
        left = sc[yy]
        for h in range(NC):
            part = mm(left, wa[h, yy])
            proj[h] = part if first_one else proj[h] + part

    pa_own.wait_recv()
    project(y, True)
    pa_f = []

    def last_chunk(j):
        ya_f[j].wait_recv()
        b = ablk(ym(2), zm(offs[j]))
        pa_f.append(send(b, b, partner))

    for j in range(4):
        last_chunk(j)
    pa_l.wait_recv()
    project(ym(-1))
    last_chunk(4)
    last_chunk(5)
    pa_r.wait_recv()
    project(ym(1))
    last_chunk(6)
    last_chunk(7)
    for cp in pa_f:
        cp.wait_recv()
    project(ym(2))

    def head_cols(h):
        return h // 3, (h % 3) * HD

    def turn(v):
        return v * cs[...] + pltpu.roll(v, HD // 2, 1) * sn[...]

    def four(block):
        return jnp.concatenate([block] * 4, axis=0)

    for h in range(5):
        hf, col = head_cols(h)
        v = proj[hf, :, col:col + HD]
        t = turn(v * rms(v)).astype(BF)
        if h == 4:
            kb[...] = t
        else:
            for i in range(3):
                qb[i, h * 128:(h + 1) * 128, :] = t[i * 128:(i + 1) * 128]
    kv[...] = proj[1, :, 2 * HD:].astype(BF)
    scale = HD ** -0.5
    for i in range(3):
        r0, n = slice(i * 128, (i + 1) * 128), (i + 1) * 128
        w = jnp.exp(mm(qb[i], kb[:n, :], NT) * scale) * four(mask[r0, :n])
        p = (w * (1.0 / jnp.sum(w, axis=-1, keepdims=True))).astype(BF)
        pb[i, :, :n] = p
        mixed = mm(p, kv[:n, :]).astype(BF)
        for h in range(4):
            mx[h // 2, r0, (h % 2) * HD:(h % 2 + 1) * HD] = mixed[h * 128:(h + 1) * 128]
        if i == 1:
            for m in (1, 3, 2):
                for mm_, cp in xb_c:
                    if mm_ == m:
                        cp.wait_recv()
                b = wb.at[c, lax.rem(xi + NX - m, NX)]
                pb_s.append(send(b, b, partner))

    def add_into(ref, *others):
        total = ref[...].astype(F32)
        for other in others:
            total = total + other[...].astype(F32)
        ref[...] = total.astype(BF)

    rb_s = []
    for j in range(NY):
        sb[j] = mm(goT[j], mx[o]).astype(BF)
        rb_s.append(send(sb.at[j], rb.at[j], partner))
    def own_part():
        for j in range(NY):
            own = mm(goT[j], mx[c])
            rb_s[j].wait_recv()
            own = (own + rb[j].astype(F32)).astype(BF)
            for q in range(2):
                tb[q, j] = own[:, q * W2:(q + 1) * W2]

    xb_s = []

    def start_x(q):
        for m in (1, 3, 2):
            t = lax.rem(xi + m, NX)
            xb_s.append(send(tb.at[q, t], xb.at[q, m - 1], xdev(m)))

    for cp in pb_s:
        cp.wait_recv()
    for h in range(NC):
        part = sum(mm(go[j], wb[h, j]) for j in range(NY)).astype(BF)
        for i in range(3):
            for k in range(2):
                gm[i, (2 * h + k) * 128:(2 * h + k + 1) * 128, :] = (
                    part[i * 128:(i + 1) * 128, k * HD:(k + 1) * HD])

    def norm_back(v, d, cos, sin):
        r = rms(v)
        xn = v * r
        dn = d * cos + pltpu.roll(d * sin, HD // 2, 1)
        return (r * (dn - xn * jnp.mean(dn * xn, axis=-1, keepdims=True))).astype(BF)

    dk = [jnp.zeros((128, HD), F32)] * 3
    dv = [jnp.zeros((128, HD), F32)] * 3
    for i in range(3):
        r0, n = slice(i * 128, (i + 1) * 128), (i + 1) * 128
        do = gm[i]
        p = pb[i, :, :n]
        pf = p.astype(F32)
        dp = mm(do, kv[:n, :], NT)
        delta = jnp.sum(pf * dp, axis=-1, keepdims=True)
        ds = (pf * (dp - delta) * scale).astype(BF)
        tk = mm(ds, qb[i], TN)
        tv = mm(p, do, TN)
        for m in range(i + 1):
            dk[m] = dk[m] + tk[m * 128:(m + 1) * 128]
            dv[m] = dv[m] + tv[m * 128:(m + 1) * 128]
        v = jnp.concatenate(
            [proj[h // 3, r0, (h % 3) * HD:(h % 3 + 1) * HD] for h in range(4)], axis=0)
        grad = norm_back(v, mm(ds, kb[:n, :]), four(cs[r0, :]), four(sn[r0, :]))
        for h in range(4):
            dpr[h // 3, r0, (h % 3) * HD:(h % 3 + 1) * HD] = grad[h * 128:(h + 1) * 128]
        if i == 0:
            own_part()
            start_x(0)
    dpr[1, :, HD:2 * HD] = norm_back(
        proj[1, :, HD:2 * HD], jnp.concatenate(dk, axis=0), cs[...], sn[...])
    dpr[1, :, 2 * HD:] = jnp.concatenate(dv, axis=0).astype(BF)

    ra_s = {}

    def partial(k):
        yy = ym(k)
        sa[yy] = mm(scT[yy], dpr[o]).astype(BF)
        ra_s[k] = send(sa.at[yy], ra.at[yy], partner)
        ta[yy] = mm(scT[yy], dpr[c]).astype(BF)

    roffs = [4, 3, -3, 2, -2, 1, -1, 0]

    def tblk(yy, j):
        return ta.at[yy, rows(zm(roffs[j])), :]

    s1, s2r, s2l, sz = {}, {}, {}, {}
    start_x(1)
    partial(2)
    partial(1)
    ra_s[2].wait_recv()
    for j in range(8):
        b = rows(zm(roffs[j]))
        add_into(ta.at[ym(2), b, :], ra.at[ym(2), b, :])
        s1[j] = send(tblk(ym(2), j), ya1.at[j], right_y if j % 2 == 0 else left_y)
    partial(3)
    partial(0)
    for k in (1, 3, 0):
        ra_s[k].wait_recv()
        add_into(ta.at[ym(k)], ra.at[ym(k)])

    def step2(j):
        s1[j].wait_recv()
        add_into(tblk(ym(1) if j % 2 == 0 else ym(3), j), ya1.at[j])
        s2r[j] = send(tblk(ym(1), j), ya2.at[0, j], right_y)
        s2l[j] = send(tblk(ym(3), j), ya2.at[1, j], left_y)

    def step3(j):
        s2r[j].wait_recv()
        s2l[j].wait_recv()
        add_into(tblk(y, j), ya2.at[0, j], ya2.at[1, j])

    def step_z(j):
        if j == 0:
            sz[0] = send(tblk(y, 0), za.at[0], right_z)
        elif j % 2 == 1:
            n = (j + 1) // 2
            sz[n - 1].wait_recv()
            add_into(tblk(y, j), za.at[n - 1])
            sz[n] = send(tblk(y, j), za.at[n], right_z)
        else:
            n = 3 + j // 2
            if n > 4:
                sz[n - 1].wait_recv()
                add_into(tblk(y, j), za.at[n - 1])
            sz[n] = send(tblk(y, j), za.at[n], left_z)

    def out_chunk(j):
        update = sum(mm(mx[h], wb[h, j], NT) for h in range(NC))
        out_ref[:, j * CH:(j + 1) * CH] = (tok[j].astype(F32) + update).astype(BF)

    def row_dots():
        total = sum(
            jnp.sum(dpr[h].astype(F32) * proj[h], axis=-1, keepdims=True) for h in range(NC))
        dots[...] = jnp.broadcast_to(total * (1.0 / D), (T, 128))

    def gt_chunk(j):
        r = rr[...][:, :1]
        g = sum(mm(dpr[h], wa[h, j], NT) for h in range(NC))
        path = (r * (g - tok[j].astype(F32) * (r * dots[...][:, :1]))).astype(BF)
        gt_ref[:, j * CH:(j + 1) * CH] = (
            go[j].astype(F32) + path.astype(F32)).astype(BF)

    zb_s = []

    def sum_x(q):
        for cp in xb_s[3 * q:3 * q + 3]:
            cp.wait_recv()
        add_into(tb.at[q, xi], *[xb.at[q, m] for m in range(3)])
        for k in (4, 3, 5, 2, 6, 1, 7):
            zb_s.append(send(
                tb.at[q, xi, rows(zm(k)), :], zb.at[q, k - 1], dev(y, zm(k))))

    def piece_copy(p):
        t = lax.rem(me8 + p, GROUP)
        return pltpu.make_async_remote_copy(
            src_ref=xsb.at[t], dst_ref=xrb.at[2 * y + c],
            send_sem=fsem.at[p], recv_sem=fsem.at[GROUP + 2 * y + c],
            device_id=((xi * NZ + z) * GROUP + t,), device_id_type=pl.DeviceIdType.MESH,
        )

    def self_copy():
        return pltpu.make_async_copy(
            xsb.at[me8], xrb.at[2 * y + c], fsem.at[GROUP + 2 * y + c])

    def sum_z():
        for cp in zb_s:
            cp.wait_recv()
        for q in range(2):
            finb[:BLK, q * W2:(q + 1) * W2] = tb[q, xi, rows(z), :].astype(F32) + sum(
                zb[q, k].astype(F32) for k in range(NZ - 1))
        finb[BLK:, :] = jnp.zeros((PAD, WB_), F32)
        for i in range(GROUP):
            xsb[i] = finb[i * ROWS:i * ROWS + PAD, :].astype(BF)
        for p in range(1, GROUP):
            piece_copy(p).start()

        @pl.when(y != xi)
        def _():
            piece_copy(0).start()

        @pl.when(y == xi)
        def _():
            self_copy().start()

    row_dots()
    out_chunk(0)
    step2(0)
    step2(1)
    sum_x(0)
    step2(2)
    step2(3)
    step3(0)
    step_z(0)
    step2(4)
    step2(5)
    step3(1)
    step3(2)
    step_z(1)
    step_z(2)
    step2(6)
    step2(7)
    sum_x(1)
    out_chunk(1)
    step3(3)
    step3(4)
    step_z(3)
    step_z(4)
    out_chunk(2)
    out_chunk(3)
    gt_chunk(0)
    step3(5)
    step3(6)
    step_z(5)
    step_z(6)
    gt_chunk(1)
    gt_chunk(2)
    gt_chunk(3)
    sum_z()
    step3(7)
    gt_chunk(3)
    sz[3].wait_recv()
    sz[6].wait_recv()
    fin[:BLK, :] = (
        tblk(y, 7)[...].astype(F32) + za[3].astype(F32) + za[6].astype(F32))
    fin[BLK:, :] = jnp.zeros((PAD, WA_), F32)

    for i in range(GROUP):
        xs[i] = fin[i * ROWS:i * ROWS + PAD, :].astype(BF)
    last = []
    for p in range(1, GROUP):
        t = lax.rem(me8 + p, GROUP)
        last.append(send(xs.at[t], xr.at[me8], base + t))
    xr[me8] = xs[me8]
    for i in range(GROUP):
        pltpu.make_async_copy(xsb.at[i], xrb.at[i], fsem.at[GROUP + i]).wait()
    for h in range(NC):
        s_ref[h, :, WA_:] = sum(xrb[2 * i + h].astype(F32) for i in range(NY))
    for cp in copies[:-len(last)]:
        cp.wait_send()
    for p in range(1, GROUP):
        piece_copy(p).wait_send()

    @pl.when(y != xi)
    def _():
        piece_copy(0).wait_send()

    for cp in last:
        cp.wait_recv()
    for h in range(NC):
        s_ref[h, :, :WA_] = sum(xr[2 * i + h].astype(F32) for i in range(NX))
    for cp in last:
        cp.wait_send()


def finish_kernel(out_in, gt_in, s_ref, gain_ref, wq_ref, out_hbm, gt_hbm, gq_ref, gw_ref, gg_ref, sem):
    moves = []
    for i, (src, dst) in enumerate(((out_in, out_hbm), (gt_in, gt_hbm))):
        for j in range(4):
            part = pl.ds(j * (T // 4), T // 4)
            cp = pltpu.make_async_copy(src.at[part, :], dst.at[part, :], sem.at[4 * i + j])
            cp.start()
            moves.append(cp)
    eye = lax.broadcasted_iota(jnp.int32, (ROWS, ROWS), 0) == lax.broadcasted_iota(
        jnp.int32, (ROWS, ROWS), 1)
    gain = jnp.sum(
        jnp.where(eye, jnp.broadcast_to(gain_ref[...].astype(F32), (ROWS, ROWS)), 0.0),
        axis=1, keepdims=True)
    along = jnp.zeros((ROWS, 1), F32)
    for h in range(NC):
        part = s_ref[h][:ROWS, :WA_]
        cols = slice(h * WA_, (h + 1) * WA_)
        gq_ref[:, cols] = part * gain
        along += jnp.sum(part * wq_ref[:, cols].astype(F32), axis=1, keepdims=True)
        gw_ref[:, h * WB_:(h + 1) * WB_] = s_ref[h][:ROWS, WA_:]
    gg_ref[...] = jnp.sum(
        jnp.where(eye, jnp.broadcast_to(along, (ROWS, ROWS)), 0.0), axis=0, keepdims=True)
    for cp in moves:
        cp.wait()


def block_step(tokens, segment_ids, grad_out, norm_gain, w_qkv, w_out):
    any_, vm = pl.BlockSpec(memory_space=pl.ANY), pl.BlockSpec(memory_space=pltpu.VMEM)
    hbm = pl.BlockSpec(memory_space=pltpu.HBM)
    v = pltpu.VMEM
    gain = norm_gain.reshape(1, ROWS)
    out, grad_tokens, sums = pl.pallas_call(
        kernel,
        out_shape=(
            pltpu.VMEM((T, D), BF),
            pltpu.VMEM((T, D), BF),
            pltpu.VMEM((NC, PAD, WX), F32),
        ),
        in_specs=[hbm] * 6,
        out_specs=(vm, vm, vm),
        scratch_shapes=[
            v((1, T), jnp.int32), v((1, ROWS), BF), v((ROWS, NC * WA_), BF), v((ROWS, NC * WB_), BF),
            v((NY, T, CH), BF), v((NY, T, CH), BF), v((NY, T, CH), BF),
            v((NY, CH, T), BF), v((NY, CH, T), BF), v((T, 128), F32),
            v((NC, PAD, WX), BF), v((GROUP, PAD, WX), BF), v((BLK, WX), F32),
            v((NC, NY, CH, WA_), BF), v((NC, NY, CH, WB_), BF),
            v((NC, T, WA_), F32), v((3, 512, HD), BF), v((T, T), F32),
            v((T, HD), F32), v((T, HD), F32),
            v((3, 512, HD), BF), v((T, HD), BF), v((T, HD), BF), v((3, 512, T), BF),
            v((NC, T, WB_), BF), v((NC, T, WA_), BF), v((T, 128), F32),
            v((NY, CH, WA_), BF), v((NY, CH, WA_), BF), v((NY, CH, WA_), BF),
            v((NZ, BLK, WA_), BF), v((2, NZ, BLK, WA_), BF), v((7, BLK, WA_), BF),
            v((2, NY, CH, W2), BF), v((NY, CH, WB_), BF), v((NY, CH, WB_), BF),
            v((2, 3, CH, W2), BF), v((2, NZ - 1, BLK, W2), BF),
            v((BLK + PAD, WA_), F32), v((BLK + PAD, WB_), F32),
            v((GROUP, PAD, WA_), BF), v((GROUP, PAD, WA_), BF),
            v((GROUP, PAD, WB_), BF), v((GROUP, PAD, WB_), BF),
            pltpu.SemaphoreType.DMA((2 * NY + 4,)),
            pltpu.SemaphoreType.DMA((N_COPIES,)), pltpu.SemaphoreType.DMA((N_COPIES,)),
            pltpu.SemaphoreType.DMA((2 * GROUP,)),
        ],
        compiler_params=pltpu.CompilerParams(
            collective_id=0, has_side_effects=True, vmem_limit_bytes=55 * 2 ** 20),
        name="block_step",
    )(tokens, grad_out, segment_ids, gain, w_qkv, w_out.T)
    out, grad_tokens, grad_qkv, grad_wout, grad_gain = pl.pallas_call(
        finish_kernel,
        out_shape=(
            jax.ShapeDtypeStruct((T, D), BF),
            jax.ShapeDtypeStruct((T, D), BF),
            jax.ShapeDtypeStruct((ROWS, NC * WA_), F32),
            jax.ShapeDtypeStruct((ROWS, NC * WB_), F32),
            jax.ShapeDtypeStruct((1, ROWS), F32),
        ),
        in_specs=[vm, vm, vm, vm, vm],
        out_specs=(any_, any_, vm, vm, vm),
        scratch_shapes=[pltpu.SemaphoreType.DMA((8,))],
        compiler_params=pltpu.CompilerParams(vmem_limit_bytes=8 * 2 ** 20),
        name="finish",
    )(out, grad_tokens, sums, gain, w_qkv)
    return out, grad_tokens, grad_qkv, grad_wout.T, grad_gain.reshape(ROWS)


def solution(mesh):
    return jax.shard_map(
        block_step,
        mesh=mesh,
        in_specs=(P("dp", None), P("dp", None), P("dp", None), P("dp"), P("dp", None),
                  P(None, "dp")),
        out_specs=(P("dp", None), P("dp", None), P("dp", None), P(None, "dp"), P("dp")),
        check_vma=False,
    )
```

```python
import math

import jax
import jax.numpy as jnp
from jax import lax
from jax.experimental import pallas as pl
from jax.experimental.pallas import tpu as pltpu
from jax.sharding import PartitionSpec as P

NY, NZ, NX, NC = 4, 8, 4, 2
D, T, HD = 2560, 384, 128
ROWS = 10
GROUP = NX * NC
BLK = GROUP * ROWS
CH = NZ * BLK
WA_, WB_ = 384, 256
WX = WA_ + WB_
W2 = 128
PAD = 16
EPS = 1e-06
LOG_BASE = math.log(1000000.0)
N_COPIES = 256
BF, F32 = jnp.bfloat16, jnp.float32
NT = (((1,), (1,)), ((), ()))
TN = (((0,), (0,)), ((), ()))


def mm(a, b, dims=(((1,), (0,)), ((), ()))):
    return lax.dot_general(a, b, dims, preferred_element_type=F32)


def rms(x):
    return lax.rsqrt(jnp.mean(x * x, axis=-1, keepdims=True) + EPS)


def kernel(
    tok_hbm, go_hbm, seg_hbm, gain_hbm, wq_hbm, wo_hbm,
    out_ref, gt_ref, s_ref,
    seg_ref, gain_ref, wq_ref, wo_ref,
    tok, go, sc, scT, goT, rr, blk, xg, tmp, wa, wb, proj, gm, mask, cs, sn,
    qb, kb, kv, pb, mx, dpr, dots,
    ta, sa, ra, ya1, ya2, za, tb, sb, rb, xb, zb, fin, finb, xs, xr, xsb, xrb,
    lsem, ssem, rsem, fsem,
):
    idx = lax.axis_index("dp")
    me8 = lax.rem(idx, GROUP)
    base = idx - me8
    c = lax.rem(idx, 2)
    o = 1 - c
    xi = lax.div(me8, 2)
    yz = lax.div(idx, GROUP)
    z = lax.rem(yz, NZ)
    y = lax.div(yz, NZ)

    def ym(k):
        return lax.rem(y + (k + NY), NY)

    def zm(k):
        return lax.rem(z + (k + NZ), NZ)

    def dev(yy, zz):
        return (yy * NZ + zz) * GROUP + me8

    def xdev(k):
        return base + lax.rem(me8 + 2 * k, GROUP)

    right_y, left_y = dev(ym(1), z), dev(ym(-1), z)
    right_z, left_z = dev(y, zm(1)), dev(y, zm(-1))
    partner = idx + 1 - 2 * c

    def rows(zz):
        return pl.ds(pl.multiple_of(zz * BLK, 16), BLK)

    copies = []

    def send(src, dst, target):
        n = len(copies)
        copy = pltpu.make_async_remote_copy(
            src_ref=src, dst_ref=dst, send_sem=ssem.at[n], recv_sem=rsem.at[n],
            device_id=(target,), device_id_type=pl.DeviceIdType.MESH,
        )
        copy.start()
        copies.append(copy)
        return copy

    small = []
    for i, (src, dst) in enumerate(
            ((gain_hbm, gain_ref), (wq_hbm, wq_ref), (wo_hbm, wo_ref), (seg_hbm, seg_ref))):
        cp = pltpu.make_async_copy(src, dst, lsem.at[2 * NY + i])
        cp.start()
        small.append(cp)

    barrier = pltpu.get_barrier_semaphore()

    def greet(d):
        pl.semaphore_signal(barrier, inc=1, device_id=(d,), device_id_type=pl.DeviceIdType.MESH)

    greetings = [base + lax.rem(me8 + p, GROUP) for p in range(1, GROUP)]
    greetings += [dev(ym(k), z) for k in range(1, NY)]
    greetings += [dev(y, zm(k)) for k in range(1, NZ)]
    for k in range(NY):
        for core in (c, o):
            if k > 0 or core is o:
                greetings.append((ym(k) * NZ + z) * GROUP + 2 * y + core)
    for d in greetings:
        greet(d)

    @pl.when(y != xi)
    def _():
        greet((y * NZ + z) * GROUP + 2 * y + c)

    loads = []
    for i, (src, dst) in enumerate(((tok_hbm, tok), (go_hbm, go))):
        for j in range(NY):
            cp = pltpu.make_async_copy(
                src.at[:, pl.ds(j * CH, CH)], dst.at[j], lsem.at[i * NY + j])
            cp.start()
            loads.append(cp)

    for cp in small:
        cp.wait()
    diag = lax.broadcasted_iota(jnp.int32, (PAD, ROWS), 0) == lax.broadcasted_iota(
        jnp.int32, (PAD, ROWS), 1)
    gain_diag = jnp.where(diag, jnp.broadcast_to(gain_ref[...].astype(F32), (PAD, ROWS)), 0.0)
    gw = mm(gain_diag.astype(BF), wq_ref[...]).astype(BF)
    wt = mm(diag.astype(F32).astype(BF), wo_ref[...]).astype(BF)
    for h in range(NC):
        blk[h, :, :WA_] = gw[:, h * WA_:(h + 1) * WA_]
        blk[h, :, WA_:] = wt[:, h * WB_:(h + 1) * WB_]

    pl.semaphore_wait(barrier, jnp.where(y == xi, len(greetings), len(greetings) + 1))

    xcop = []
    for p in range(1, GROUP):
        t = lax.rem(me8 + p, GROUP)
        xcop.append(send(blk.at[lax.rem(t, 2)], xg.at[me8], base + t))
    xg[me8] = blk[c]

    for j in range(NY):
        loads[j].wait()

    def scale_rows(i, _):
        r0 = pl.ds(pl.multiple_of(i * 16, 16), 16)
        parts = [tok[j, r0, :].astype(F32) for j in range(NY)]
        total = sum(jnp.sum(p * p, axis=-1, keepdims=True) for p in parts)
        r = lax.rsqrt(total * (1.0 / D) + EPS)
        rr[r0, :] = jnp.broadcast_to(r, (16, 128))
        for j in range(NY):
            sc[j, r0, :] = (parts[j] * r).astype(BF)
        return 0

    lax.fori_loop(0, T // 16, scale_rows, 0, unroll=2)

    for cp in xcop:
        cp.wait_recv()
    for i in range(GROUP):
        tmp[i * ROWS:(i + 1) * ROWS, :] = xg[i].astype(F32)[:ROWS, :]
    wa[c, y, rows(z), :] = tmp[:, :WA_].astype(BF)
    wb[c, y, rows(z), :] = tmp[:, WA_:].astype(BF)

    def ablk(yy, zz):
        return wa.at[c, yy, rows(zz), :]

    def bblk(yy, zz):
        return wb.at[c, yy, rows(zz), :]

    offs = [0, -1, 1, -2, 2, -3, 3, -4]
    za_r, za_l, ya_r, ya_l, ya_f, zb_c, xb_c = {}, {}, {}, {}, {}, {}, []

    def zA(s):
        za_r[s] = send(ablk(y, zm(1 - s)), ablk(y, zm(1 - s)), right_z)
        if s < 4:
            za_l[s] = send(ablk(y, zm(s - 1)), ablk(y, zm(s - 1)), left_z)

    def zA_wait(s):
        za_r[s].wait_recv()
        if s < 4:
            za_l[s].wait_recv()

    def yA(j):
        b = ablk(y, zm(offs[j]))
        ya_r[j] = send(b, b, right_y)
        ya_l[j] = send(b, b, left_y)

    def yA_forward(j):
        ya_r[j].wait_recv()
        ya_l[j].wait_recv()
        if j % 2 == 0:
            b = ablk(ym(-1), zm(offs[j]))
            ya_f[j] = send(b, b, right_y)
        else:
            b = ablk(ym(1), zm(offs[j]))
            ya_f[j] = send(b, b, left_y)

    def zB(k):
        b = bblk(xi, z)
        zb_c[k] = send(b, b, dev(y, zm(k)))

    def xB(k):
        zb_c[k].wait_recv()
        b = bblk(xi, zm(-k))
        for m in (1, 3, 2):
            xb_c.append((m, send(b, b, xdev(m))))

    def transpose(src, dst, j):
        for k in range(CH // 128):
            piece = src[j, :, k * 128:(k + 1) * 128].astype(F32)
            dst[j, k * 128:(k + 1) * 128, :] = piece.T.astype(BF)

    zA(1)
    b = bblk(y, z)
    yb_c = [send(b, b, dev(ym(k), z)) for k in (1, 3, 2)]
    yA(0)

    seg = seg_ref[...].astype(F32)
    row_i = lax.broadcasted_iota(jnp.int32, (T, T), 0)
    col_i = lax.broadcasted_iota(jnp.int32, (T, T), 1)
    seg_s = jnp.broadcast_to(seg, (T, T))
    seg_t = jnp.sum(jnp.where(row_i == col_i, seg_s, 0.0), axis=1, keepdims=True)
    first = jnp.sum(jnp.where(seg_s < seg_t, 1.0, 0.0), axis=1, keepdims=True)
    mask[...] = jnp.where((seg_s == seg_t) & (col_i <= row_i), 1.0, 0.0)
    lane = lax.broadcasted_iota(jnp.int32, (T, HD), 1)
    place = lax.broadcasted_iota(jnp.int32, (T, HD), 0).astype(F32)
    inverse = jnp.exp(lax.rem(lane, HD // 2).astype(F32) * (-2.0 * LOG_BASE / HD))
    angles = (place - first) * inverse
    cs[...] = jnp.cos(angles)
    sn[...] = jnp.where(lane < HD // 2, -1.0, 1.0) * jnp.sin(angles)

    zA_wait(1)
    zA(2)
    yA(1)
    yA(2)
    for cp in yb_c:
        cp.wait_recv()
    zB(1)
    zB(7)
    zB(2)
    zB(6)
    yA_forward(0)
    zA_wait(2)
    zA(3)
    yA(3)
    yA(4)
    zB(3)
    zB(5)
    zB(4)
    xB(1)
    xB(7)
    yA_forward(1)
    yA_forward(2)
    transpose(sc, scT, 0)
    zA_wait(3)
    zA(4)
    yA(5)
    yA(6)
    xB(2)
    xB(6)
    yA_forward(3)
    yA_forward(4)
    transpose(sc, scT, 1)
    zA_wait(4)
    yA(7)
    pa_own = send(wa.at[c, y], wa.at[c, y], partner)
    xB(3)
    xB(5)
    transpose(sc, scT, 2)
    yA_forward(5)
    xB(4)
    yA_forward(6)
    transpose(sc, scT, 3)
    for j in range(NY):
        loads[NY + j].wait()
    transpose(go, goT, 0)
    transpose(go, goT, 1)
    yA_forward(7)
    pa_l = send(wa.at[c, ym(-1)], wa.at[c, ym(-1)], partner)
    pa_r = send(wa.at[c, ym(1)], wa.at[c, ym(1)], partner)
    pb_s = [send(wb.at[c, xi], wb.at[c, xi], partner)]
    transpose(go, goT, 2)
    transpose(go, goT, 3)

    def project(yy, first_one=False):
        left = sc[yy]
        for h in range(NC):
            part = mm(left, wa[h, yy])
            proj[h] = part if first_one else proj[h] + part

    pa_own.wait_recv()
    project(y, True)
    pa_f = []

    def last_chunk(j):
        ya_f[j].wait_recv()
        b = ablk(ym(2), zm(offs[j]))
        pa_f.append(send(b, b, partner))

    for j in range(4):
        last_chunk(j)
    pa_l.wait_recv()
    project(ym(-1))
    last_chunk(4)
    last_chunk(5)
    pa_r.wait_recv()
    project(ym(1))
    last_chunk(6)
    last_chunk(7)
    for cp in pa_f:
        cp.wait_recv()
    project(ym(2))

    def head_cols(h):
        return h // 3, (h % 3) * HD

    def turn(v):
        return v * cs[...] + pltpu.roll(v, HD // 2, 1) * sn[...]

    def four(block):
        return jnp.concatenate([block] * 4, axis=0)

    for h in range(5):
        hf, col = head_cols(h)
        v = proj[hf, :, col:col + HD]
        t = turn(v * rms(v)).astype(BF)
        if h == 4:
            kb[...] = t
        else:
            for i in range(3):
                qb[i, h * 128:(h + 1) * 128, :] = t[i * 128:(i + 1) * 128]
    kv[...] = proj[1, :, 2 * HD:].astype(BF)
    scale = HD ** -0.5
    for i in range(3):
        r0, n = slice(i * 128, (i + 1) * 128), (i + 1) * 128
        w = jnp.exp(mm(qb[i], kb[:n, :], NT) * scale) * four(mask[r0, :n])
        p = (w * (1.0 / jnp.sum(w, axis=-1, keepdims=True))).astype(BF)
        pb[i, :, :n] = p
        mixed = mm(p, kv[:n, :]).astype(BF)
        for h in range(4):
            mx[h // 2, r0, (h % 2) * HD:(h % 2 + 1) * HD] = mixed[h * 128:(h + 1) * 128]
        if i == 1:
            for m in (1, 3, 2):
                for mm_, cp in xb_c:
                    if mm_ == m:
                        cp.wait_recv()
                b = wb.at[c, lax.rem(xi + NX - m, NX)]
                pb_s.append(send(b, b, partner))

    def add_into(ref, *others):
        total = ref[...].astype(F32)
        for other in others:
            total = total + other[...].astype(F32)
        ref[...] = total.astype(BF)

    rb_s = []
    for j in range(NY):
        sb[j] = mm(goT[j], mx[o]).astype(BF)
        rb_s.append(send(sb.at[j], rb.at[j], partner))
    def own_part():
        for j in range(NY):
            own = mm(goT[j], mx[c])
            rb_s[j].wait_recv()
            own = (own + rb[j].astype(F32)).astype(BF)
            for q in range(2):
                tb[q, j] = own[:, q * W2:(q + 1) * W2]

    xb_s = []

    def start_x(q):
        for m in (1, 3, 2):
            t = lax.rem(xi + m, NX)
            xb_s.append(send(tb.at[q, t], xb.at[q, m - 1], xdev(m)))

    for cp in pb_s:
        cp.wait_recv()
    for h in range(NC):
        part = sum(mm(go[j], wb[h, j]) for j in range(NY)).astype(BF)
        for i in range(3):
            for k in range(2):
                gm[i, (2 * h + k) * 128:(2 * h + k + 1) * 128, :] = (
                    part[i * 128:(i + 1) * 128, k * HD:(k + 1) * HD])

    def norm_back(v, d, cos, sin):
        r = rms(v)
        xn = v * r
        dn = d * cos + pltpu.roll(d * sin, HD // 2, 1)
        return (r * (dn - xn * jnp.mean(dn * xn, axis=-1, keepdims=True))).astype(BF)

    dk = [jnp.zeros((128, HD), F32)] * 3
    dv = [jnp.zeros((128, HD), F32)] * 3
    for i in range(3):
        r0, n = slice(i * 128, (i + 1) * 128), (i + 1) * 128
        do = gm[i]
        p = pb[i, :, :n]
        pf = p.astype(F32)
        dp = mm(do, kv[:n, :], NT)
        delta = jnp.sum(pf * dp, axis=-1, keepdims=True)
        ds = (pf * (dp - delta) * scale).astype(BF)
        tk = mm(ds, qb[i], TN)
        tv = mm(p, do, TN)
        for m in range(i + 1):
            dk[m] = dk[m] + tk[m * 128:(m + 1) * 128]
            dv[m] = dv[m] + tv[m * 128:(m + 1) * 128]
        v = jnp.concatenate(
            [proj[h // 3, r0, (h % 3) * HD:(h % 3 + 1) * HD] for h in range(4)], axis=0)
        grad = norm_back(v, mm(ds, kb[:n, :]), four(cs[r0, :]), four(sn[r0, :]))
        for h in range(4):
            dpr[h // 3, r0, (h % 3) * HD:(h % 3 + 1) * HD] = grad[h * 128:(h + 1) * 128]
        if i == 0:
            own_part()
            start_x(0)
    dpr[1, :, HD:2 * HD] = norm_back(
        proj[1, :, HD:2 * HD], jnp.concatenate(dk, axis=0), cs[...], sn[...])
    dpr[1, :, 2 * HD:] = jnp.concatenate(dv, axis=0).astype(BF)

    ra_s = {}

    def partial(k):
        yy = ym(k)
        sa[yy] = mm(scT[yy], dpr[o]).astype(BF)
        ra_s[k] = send(sa.at[yy], ra.at[yy], partner)
        ta[yy] = mm(scT[yy], dpr[c]).astype(BF)

    roffs = [4, 3, -3, 2, -2, 1, -1, 0]

    def tblk(yy, j):
        return ta.at[yy, rows(zm(roffs[j])), :]

    s1, s2r, s2l, sz = {}, {}, {}, {}
    start_x(1)
    partial(2)
    partial(1)
    ra_s[2].wait_recv()
    for j in range(8):
        b = rows(zm(roffs[j]))
        add_into(ta.at[ym(2), b, :], ra.at[ym(2), b, :])
        s1[j] = send(tblk(ym(2), j), ya1.at[j], right_y if j % 2 == 0 else left_y)
    partial(3)
    partial(0)
    for k in (1, 3, 0):
        ra_s[k].wait_recv()
        add_into(ta.at[ym(k)], ra.at[ym(k)])

    def step2(j):
        s1[j].wait_recv()
        add_into(tblk(ym(1) if j % 2 == 0 else ym(3), j), ya1.at[j])
        s2r[j] = send(tblk(ym(1), j), ya2.at[0, j], right_y)
        s2l[j] = send(tblk(ym(3), j), ya2.at[1, j], left_y)

    def step3(j):
        s2r[j].wait_recv()
        s2l[j].wait_recv()
        add_into(tblk(y, j), ya2.at[0, j], ya2.at[1, j])

    def step_z(j):
        if j == 0:
            sz[0] = send(tblk(y, 0), za.at[0], right_z)
        elif j % 2 == 1:
            n = (j + 1) // 2
            sz[n - 1].wait_recv()
            add_into(tblk(y, j), za.at[n - 1])
            sz[n] = send(tblk(y, j), za.at[n], right_z)
        else:
            n = 3 + j // 2
            if n > 4:
                sz[n - 1].wait_recv()
                add_into(tblk(y, j), za.at[n - 1])
            sz[n] = send(tblk(y, j), za.at[n], left_z)

    def out_chunk(j):
        update = sum(mm(mx[h], wb[h, j], NT) for h in range(NC))
        out_ref[:, j * CH:(j + 1) * CH] = (tok[j].astype(F32) + update).astype(BF)

    def row_dots():
        total = sum(
            jnp.sum(dpr[h].astype(F32) * proj[h], axis=-1, keepdims=True) for h in range(NC))
        dots[...] = jnp.broadcast_to(total * (1.0 / D), (T, 128))

    def gt_chunk(j):
        r = rr[...][:, :1]
        g = sum(mm(dpr[h], wa[h, j], NT) for h in range(NC))
        path = (r * (g - tok[j].astype(F32) * (r * dots[...][:, :1]))).astype(BF)
        gt_ref[:, j * CH:(j + 1) * CH] = (
            go[j].astype(F32) + path.astype(F32)).astype(BF)

    zb_s = []

    def sum_x(q):
        for cp in xb_s[3 * q:3 * q + 3]:
            cp.wait_recv()
        add_into(tb.at[q, xi], *[xb.at[q, m] for m in range(3)])
        for k in (4, 3, 5, 2, 6, 1, 7):
            zb_s.append(send(
                tb.at[q, xi, rows(zm(k)), :], zb.at[q, k - 1], dev(y, zm(k))))

    def piece_copy(p):
        t = lax.rem(me8 + p, GROUP)
        return pltpu.make_async_remote_copy(
            src_ref=xsb.at[t], dst_ref=xrb.at[2 * y + c],
            send_sem=fsem.at[p], recv_sem=fsem.at[GROUP + 2 * y + c],
            device_id=((xi * NZ + z) * GROUP + t,), device_id_type=pl.DeviceIdType.MESH,
        )

    def self_copy():
        return pltpu.make_async_copy(
            xsb.at[me8], xrb.at[2 * y + c], fsem.at[GROUP + 2 * y + c])

    def sum_z():
        for cp in zb_s:
            cp.wait_recv()
        for q in range(2):
            finb[:BLK, q * W2:(q + 1) * W2] = tb[q, xi, rows(z), :].astype(F32) + sum(
                zb[q, k].astype(F32) for k in range(NZ - 1))
        finb[BLK:, :] = jnp.zeros((PAD, WB_), F32)
        for i in range(GROUP):
            xsb[i] = finb[i * ROWS:i * ROWS + PAD, :].astype(BF)
        for p in range(1, GROUP):
            piece_copy(p).start()

        @pl.when(y != xi)
        def _():
            piece_copy(0).start()

        @pl.when(y == xi)
        def _():
            self_copy().start()

    row_dots()
    out_chunk(0)
    step2(0)
    step2(1)
    step2(2)
    step2(3)
    sum_x(0)
    step3(0)
    step_z(0)
    step2(4)
    step2(5)
    step3(1)
    step3(2)
    step_z(1)
    step_z(2)
    step2(6)
    step2(7)
    out_chunk(1)
    step3(3)
    step3(4)
    step_z(3)
    step_z(4)
    sum_x(1)
    out_chunk(2)
    out_chunk(3)
    gt_chunk(0)
    step3(5)
    step3(6)
    step_z(5)
    step_z(6)
    gt_chunk(1)
    gt_chunk(2)
    gt_chunk(3)
    sum_z()
    step3(7)
    gt_chunk(3)
    sz[3].wait_recv()
    sz[6].wait_recv()
    fin[:BLK, :] = (
        tblk(y, 7)[...].astype(F32) + za[3].astype(F32) + za[6].astype(F32))
    fin[BLK:, :] = jnp.zeros((PAD, WA_), F32)

    for i in range(GROUP):
        xs[i] = fin[i * ROWS:i * ROWS + PAD, :].astype(BF)
    last = []
    for p in range(1, GROUP):
        t = lax.rem(me8 + p, GROUP)
        last.append(send(xs.at[t], xr.at[me8], base + t))
    xr[me8] = xs[me8]
    for i in range(GROUP):
        pltpu.make_async_copy(xsb.at[i], xrb.at[i], fsem.at[GROUP + i]).wait()
    for h in range(NC):
        s_ref[h, :, WA_:] = sum(xrb[2 * i + h].astype(F32) for i in range(NY))
    for cp in copies[:-len(last)]:
        cp.wait_send()
    for p in range(1, GROUP):
        piece_copy(p).wait_send()

    @pl.when(y != xi)
    def _():
        piece_copy(0).wait_send()

    for cp in last:
        cp.wait_recv()
    for h in range(NC):
        s_ref[h, :, :WA_] = sum(xr[2 * i + h].astype(F32) for i in range(NX))
    for cp in last:
        cp.wait_send()


def finish_kernel(out_in, gt_in, s_ref, gain_ref, wq_ref, out_hbm, gt_hbm, gq_ref, gw_ref, gg_ref, sem):
    moves = []
    for i, (src, dst) in enumerate(((out_in, out_hbm), (gt_in, gt_hbm))):
        for j in range(4):
            part = pl.ds(j * (T // 4), T // 4)
            cp = pltpu.make_async_copy(src.at[part, :], dst.at[part, :], sem.at[4 * i + j])
            cp.start()
            moves.append(cp)
    eye = lax.broadcasted_iota(jnp.int32, (ROWS, ROWS), 0) == lax.broadcasted_iota(
        jnp.int32, (ROWS, ROWS), 1)
    gain = jnp.sum(
        jnp.where(eye, jnp.broadcast_to(gain_ref[...].astype(F32), (ROWS, ROWS)), 0.0),
        axis=1, keepdims=True)
    along = jnp.zeros((ROWS, 1), F32)
    for h in range(NC):
        part = s_ref[h][:ROWS, :WA_]
        cols = slice(h * WA_, (h + 1) * WA_)
        gq_ref[:, cols] = part * gain
        along += jnp.sum(part * wq_ref[:, cols].astype(F32), axis=1, keepdims=True)
        gw_ref[:, h * WB_:(h + 1) * WB_] = s_ref[h][:ROWS, WA_:]
    gg_ref[...] = jnp.sum(
        jnp.where(eye, jnp.broadcast_to(along, (ROWS, ROWS)), 0.0), axis=0, keepdims=True)
    for cp in moves:
        cp.wait()


def block_step(tokens, segment_ids, grad_out, norm_gain, w_qkv, w_out):
    any_, vm = pl.BlockSpec(memory_space=pl.ANY), pl.BlockSpec(memory_space=pltpu.VMEM)
    hbm = pl.BlockSpec(memory_space=pltpu.HBM)
    v = pltpu.VMEM
    gain = norm_gain.reshape(1, ROWS)
    out, grad_tokens, sums = pl.pallas_call(
        kernel,
        out_shape=(
            pltpu.VMEM((T, D), BF),
            pltpu.VMEM((T, D), BF),
            pltpu.VMEM((NC, PAD, WX), F32),
        ),
        in_specs=[hbm] * 6,
        out_specs=(vm, vm, vm),
        scratch_shapes=[
            v((1, T), jnp.int32), v((1, ROWS), BF), v((ROWS, NC * WA_), BF), v((ROWS, NC * WB_), BF),
            v((NY, T, CH), BF), v((NY, T, CH), BF), v((NY, T, CH), BF),
            v((NY, CH, T), BF), v((NY, CH, T), BF), v((T, 128), F32),
            v((NC, PAD, WX), BF), v((GROUP, PAD, WX), BF), v((BLK, WX), F32),
            v((NC, NY, CH, WA_), BF), v((NC, NY, CH, WB_), BF),
            v((NC, T, WA_), F32), v((3, 512, HD), BF), v((T, T), F32),
            v((T, HD), F32), v((T, HD), F32),
            v((3, 512, HD), BF), v((T, HD), BF), v((T, HD), BF), v((3, 512, T), BF),
            v((NC, T, WB_), BF), v((NC, T, WA_), BF), v((T, 128), F32),
            v((NY, CH, WA_), BF), v((NY, CH, WA_), BF), v((NY, CH, WA_), BF),
            v((NZ, BLK, WA_), BF), v((2, NZ, BLK, WA_), BF), v((7, BLK, WA_), BF),
            v((2, NY, CH, W2), BF), v((NY, CH, WB_), BF), v((NY, CH, WB_), BF),
            v((2, 3, CH, W2), BF), v((2, NZ - 1, BLK, W2), BF),
            v((BLK + PAD, WA_), F32), v((BLK + PAD, WB_), F32),
            v((GROUP, PAD, WA_), BF), v((GROUP, PAD, WA_), BF),
            v((GROUP, PAD, WB_), BF), v((GROUP, PAD, WB_), BF),
            pltpu.SemaphoreType.DMA((2 * NY + 4,)),
            pltpu.SemaphoreType.DMA((N_COPIES,)), pltpu.SemaphoreType.DMA((N_COPIES,)),
            pltpu.SemaphoreType.DMA((2 * GROUP,)),
        ],
        compiler_params=pltpu.CompilerParams(
            collective_id=0, has_side_effects=True, vmem_limit_bytes=55 * 2 ** 20),
        name="block_step",
    )(tokens, grad_out, segment_ids, gain, w_qkv, w_out.T)
    out, grad_tokens, grad_qkv, grad_wout, grad_gain = pl.pallas_call(
        finish_kernel,
        out_shape=(
            jax.ShapeDtypeStruct((T, D), BF),
            jax.ShapeDtypeStruct((T, D), BF),
            jax.ShapeDtypeStruct((ROWS, NC * WA_), F32),
            jax.ShapeDtypeStruct((ROWS, NC * WB_), F32),
            jax.ShapeDtypeStruct((1, ROWS), F32),
        ),
        in_specs=[vm, vm, vm, vm, vm],
        out_specs=(any_, any_, vm, vm, vm),
        scratch_shapes=[pltpu.SemaphoreType.DMA((8,))],
        compiler_params=pltpu.CompilerParams(vmem_limit_bytes=8 * 2 ** 20),
        name="finish",
    )(out, grad_tokens, sums, gain, w_qkv)
    return out, grad_tokens, grad_qkv, grad_wout.T, grad_gain.reshape(ROWS)


def solution(mesh):
    return jax.shard_map(
        block_step,
        mesh=mesh,
        in_specs=(P("dp", None), P("dp", None), P("dp", None), P("dp"), P("dp", None),
                  P(None, "dp")),
        out_specs=(P("dp", None), P("dp", None), P("dp", None), P(None, "dp"), P("dp")),
        check_vma=False,
    )
```
